32 devices in a mesh: gx: 4 (over x, core), gy: 8 (over z, y).
Axes of the slice: x: 2, y: 2, z: 4, core: 2. Of those that a mesh axis runs over, the one named last changes fastest.
Arguments:
- pixels: bfloat16 [8192, 1536], P(('gx', 'gy')), may hold values from -6 to 6
- frame_index: int32 [8192], P(('gx', 'gy')), may hold values from 0 to 2
- patch_cell: int32 [2, 8192], P(None, ('gx', 'gy')), may hold values from 0 to 55
- tile_id: int32 [8192], P(('gx', 'gy')), may hold values from 0 to 16, as said below
- halo_index: int32 [4096], P(('gx', 'gy')), may hold values from 0 to 255
- w_patch: bfloat16 [1536, 768], replicated, may hold values from -0.15625 to 0.15625
- first_gain: float32 [768], replicated, may hold values from 0.1 to 1.9
- first_bias: float32 [768], replicated, may hold values from -2 to 2
- w_project: bfloat16 [768, 2304], replicated, may hold values from -0.21875 to 0.21875
- project_bias: float32 [1536], replicated, may hold values from -3 to 3
- w_output: bfloat16 [768, 768], replicated, may hold values from -3 to 3
- merge_bias: float32 [768], replicated, may hold values from -3 to 3
- second_gain: float32 [768], replicated, may hold values from 0.1 to 1.9
- second_bias: float32 [768], replicated, may hold values from -2 to 2
- w_up: bfloat16 [768, 3072], replicated, may hold values from -0.21875 to 0.21875
- up_bias: float32 [3072], replicated, may hold values from -3 to 3
- w_down: bfloat16 [3072, 768], replicated, may hold values from -0.109375 to 0.109375
- down_bias: float32 [768], replicated, may hold values from -3 to 3
- w_head: bfloat16 [768, 1536], replicated, may hold values from -0.21875 to 0.21875
- cotangent: bfloat16 [8192, 1536], P(('gx', 'gy')), may hold values from -6 to 6
Outputs:
- predicted: bfloat16 [8192, 1536], P(('gx', 'gy'))
- pixel_grad: bfloat16 [8192, 1536], P(('gx', 'gy'))
- patch_grad: float32 [1536, 768], P('gy')
- first_gain_grad: float32 [768], P('gy')
- first_bias_grad: float32 [768], P('gy')
- project_grad: float32 [768, 2304], P('gy')
- project_bias_grad: float32 [1536], P('gy')
- output_grad: float32 [768, 768], P('gy')
- merge_bias_grad: float32 [768], P('gy')
- second_gain_grad: float32 [768], P('gy')
- second_bias_grad: float32 [768], P('gy')
- up_grad: float32 [768, 3072], P('gy')
- up_bias_grad: float32 [3072], P('gy')
- down_grad: float32 [3072, 768], P('gy')
- down_bias_grad: float32 [768], P('gy')
- head_grad: float32 [768, 1536], P('gy')
The draws below stay inside these ranges and needn't reach their ends.
Inputs may be any that keep to these rules, and one draw needn't show every extreme that they name: `tile_id`: on each device's 256 rows, the first rows (at least 64, at most 192) belong to tile 0, shared by all devices of a gx column; the rest belong to tiles 1 + 2 b and 2 + 2 b, used by device gy index b alone; its last row is in tile 2 + 2 b.
All inputs are finite; a program needn't handle non-finite values.
Results may differ from the reference program's by a relative error of at most 0.019.
Values may be sent and summed in bfloat16 or wider, within the bound.
No kernel may reach another device: no remote copies, remote signals or barrier semaphores. Data moves between devices by JAX's collectives and lax.ppermute only.
A program may use at most 256 MiB of HBM per device.

```python
import jax
import jax.numpy as jnp
from jax import lax

HEADS = 12
HEAD_DIM = 64
D = 768
FF = 3072
FRAMES = 3
PIX = 1536
GRID_SIDE = 56
TOK_DEV = 256
HALO = 128
TOKENS = 8192
HALO_ROWS = 4096
N_GX = 4
N_GY = 8


def draw_tile_id(key, part):
    key = jax.random.fold_in(key, 11)
    first_key, second_key = jax.random.split(key)
    devices = TOKENS // TOK_DEV
    cut_first = jax.random.randint(first_key, (devices, 1), TOK_DEV // 4, 3 * TOK_DEV // 4 + 1)
    spread_draw = jax.random.randint(second_key, (devices, 1), 0, TOK_DEV)
    cut_second = cut_first + spread_draw % (TOK_DEV - cut_first)
    places = jnp.arange(TOK_DEV)[None, :]
    gy_index = (jnp.arange(devices) % N_GY)[:, None]
    tiles = jnp.where(places < cut_first, 0, jnp.where(places < cut_second, 1 + 2 * gy_index, 2 + 2 * gy_index))
    return tiles.reshape(-1).astype(jnp.int32)


def set_ends(entries, stream_key, least, top_value):
    place = [jax.random.randint(jax.random.fold_in(stream_key, axis), (), 0, length) for axis, length in enumerate(entries.shape)]
    main_axis = entries.shape.index(max(entries.shape))
    next_to = place[:main_axis] + [(place[main_axis] + 1) % entries.shape[main_axis]] + place[main_axis + 1:]
    return entries.at[tuple(place)].set(least).at[tuple(next_to)].set(top_value)


def shard_levels(rng, extent, shards, least, top_value):
    factor_of = 1.0
    for position, blocks in shards:
        draws = jax.random.uniform(jax.random.fold_in(jax.random.fold_in(rng, 6), position), (blocks,), jnp.float32, least / len(shards), top_value / len(shards))
        factor_of = factor_of * jnp.repeat(jnp.exp(draws), extent[position] // blocks).reshape((-1,) + (1,) * (len(extent) - 1 - position))
    return factor_of


def scatter_about(stream_key, extent, width, reach, cuts=(), held_as=jnp.bfloat16):
    loudness = shard_levels(stream_key, extent, cuts, -0.22, 0.18) if cuts else 1.0
    result = jax.random.normal(stream_key, extent, jnp.float32) * width * loudness
    return jnp.minimum(jnp.maximum(result, -reach), reach).astype(held_as)


def setup_inputs(seed: int = 0) -> dict:
    keys = jax.random.split(jax.random.key(seed), 21)
    return {
        "pixels": scatter_about(keys[0], (TOKENS, PIX), 1.0, 6.0, ((0, 32),)),
        "frame_index": set_ends(jax.random.randint(keys[1], (TOKENS,), 0, FRAMES), jax.random.fold_in(keys[1], 1), 0, FRAMES - 1).astype(jnp.int32),
        "patch_cell": set_ends(jax.random.randint(keys[2], (2, TOKENS), 0, GRID_SIDE), jax.random.fold_in(keys[2], 1), 0, GRID_SIDE - 1).astype(jnp.int32),
        "tile_id": draw_tile_id(jax.random.fold_in(keys[20], 71), 0),
        "halo_index": set_ends(jax.random.randint(keys[4], (HALO_ROWS,), 0, TOK_DEV), jax.random.fold_in(keys[4], 1), 0, TOK_DEV - 1).astype(jnp.int32),
        "w_patch": scatter_about(keys[5], (PIX, D), PIX ** -0.5, 0.15625),
        "first_gain": jnp.clip(1.0 + 0.18 * jax.random.normal(keys[6], (D,), jnp.float32), 0.1, 1.9),
        "first_bias": scatter_about(keys[7], (D,), 0.3, 2.0, (), jnp.float32),
        "w_project": scatter_about(keys[8], (D, 3 * D), D ** -0.5, 0.21875),
        "project_bias": scatter_about(keys[9], (2 * D,), 0.5, 3.0, (), jnp.float32),
        "w_output": scatter_about(keys[10], (D, D), 4 ** -0.5, 3.0),
        "merge_bias": scatter_about(keys[11], (D,), 0.5, 3.0, (), jnp.float32),
        "second_gain": jnp.clip(1.0 + 0.18 * jax.random.normal(keys[12], (D,), jnp.float32), 0.1, 1.9),
        "second_bias": scatter_about(keys[13], (D,), 0.3, 2.0, (), jnp.float32),
        "w_up": scatter_about(keys[14], (D, FF), D ** -0.5, 0.21875),
        "up_bias": scatter_about(keys[15], (FF,), 0.5, 3.0, (), jnp.float32),
        "w_down": scatter_about(keys[16], (FF, D), FF ** -0.5, 0.109375),
        "down_bias": scatter_about(keys[17], (D,), 0.5, 3.0, (), jnp.float32),
        "w_head": scatter_about(keys[18], (D, PIX), D ** -0.5, 0.21875),
        "cotangent": scatter_about(keys[19], (TOKENS, PIX), 1.0, 6.0, ((0, 32),)),
    }


EPS = 1e-06
NEG = -1e+30

@jax.custom_vjp
def low(v):
    return lax.optimization_barrier(v.astype(jnp.bfloat16)).astype(jnp.float32)

@jax.custom_vjp
def low_back(v):
    return v

def low_keep(v):
    return (low(v), None)

def low_pass(kept, grad):
    return (grad,)

def back_keep(v):
    return (v, None)

def back_low(kept, grad):
    return (low(grad),)
low.defvjp(low_keep, low_pass)
low_back.defvjp(back_keep, back_low)

def matmul_high(left, right):
    return jnp.dot(left, right, preferred_element_type=jnp.float32, precision=lax.Precision.HIGHEST)

def sincos_band(coordinate, band_width):
    half_width = band_width // 2
    omegas = 1.0 / 10000.0 ** (jnp.arange(half_width, dtype=jnp.float32) / half_width)
    angles = coordinate.astype(jnp.float32)[:, None] * omegas[None, :]
    return jnp.concatenate([jnp.sin(angles), jnp.cos(angles)], axis=1)

def positions(frame_index, patch_cell, model_width):
    unit_width = model_width // 16
    return jnp.concatenate([sincos_band(frame_index, 4 * unit_width), sincos_band(patch_cell[0], 6 * unit_width), sincos_band(patch_cell[1], 6 * unit_width)], axis=1)

def layer_norm(inputs, scale_gain, shift_bias):
    centered = inputs - lax.optimization_barrier(jnp.mean(inputs, axis=-1, keepdims=True))
    variance = lax.optimization_barrier(jnp.mean(centered * centered, axis=-1, keepdims=True))
    return centered * lax.rsqrt(variance + EPS) * scale_gain + shift_bias

def attend_block(block_items, keys_col, values_col, key_ids, model_width):
    query_block, query_ids = block_items
    scaling = HEAD_DIM ** (-0.5)
    query_heads = query_block.reshape(TOK_DEV, HEADS, HEAD_DIM)
    key_heads = keys_col.reshape(-1, HEADS, HEAD_DIM)
    value_heads = values_col.reshape(-1, HEADS, HEAD_DIM)
    scores = low_back(jnp.einsum('qhd,khd->hqk', query_heads, key_heads, precision=lax.Precision.HIGHEST) * scaling)
    allowed = query_ids[:, None] == key_ids[None, :]
    scores = jnp.where(allowed[None], scores, NEG)
    probs = low(jax.nn.softmax(scores, axis=-1))
    mixed = jnp.einsum('hqk,khd->qhd', probs, value_heads, precision=lax.Precision.HIGHEST)
    return mixed.reshape(TOK_DEV, model_width)

def reference(pixels, frame_index, patch_cell, tile_id, halo_index, w_patch, first_gain, first_bias, w_project, project_bias, w_output, merge_bias, second_gain, second_bias, w_up, up_bias, w_down, down_bias, w_head, cotangent):
    model_width = w_output.shape[0]
    positional = positions(frame_index, patch_cell, model_width)
    tile_grid = tile_id.reshape(N_GX, N_GY, TOK_DEV)
    halo_grid = halo_index.reshape(N_GX, N_GY, HALO)
    column_live = jnp.arange(N_GX)[:, None, None] > 0
    rim_ids = jnp.where(column_live, jnp.zeros((N_GX, N_GY, HALO), jnp.int32), -jnp.ones((N_GX, N_GY, HALO), jnp.int32))
    key_grid = jnp.concatenate([tile_grid, rim_ids], axis=2).reshape(N_GX, -1)

    def attend_column(column_items):
        queries_col, keys_col, values_col, ids_col, key_ids = column_items

        def one_block(block_items):
            return attend_block(block_items, keys_col, values_col, key_ids, model_width)
        return lax.map(jax.checkpoint(one_block), (queries_col, ids_col))

    def forward(pixels_full, patch_weight, gain_one, bias_one, project_weight, project_shift, output_weight, output_shift, gain_two, bias_two, up_weight, up_shift, down_weight, down_shift, head_weight):
        embedded = low_back(matmul_high(pixels_full, patch_weight))
        stream = (embedded + positional).reshape(N_GX, N_GY, TOK_DEV, model_width)
        sent_rows = low(jnp.take_along_axis(stream, halo_grid[..., None], axis=2))
        arrived = jnp.concatenate([jnp.zeros_like(sent_rows[:1]), sent_rows[:-1]], axis=0)
        joined = jnp.concatenate([stream, arrived], axis=2)
        normed = low(layer_norm(joined, gain_one, bias_one))
        queries = low(low_back(matmul_high(normed[:, :, :TOK_DEV], project_weight[:, :model_width]) + project_shift[:model_width]))
        keys_low = low(low_back(matmul_high(normed, project_weight[:, model_width:2 * model_width])))
        values_low = low(low_back(matmul_high(normed, project_weight[:, 2 * model_width:]) + project_shift[model_width:]))
        mixed_full = lax.map(attend_column, (queries, keys_low.reshape(N_GX, -1, model_width), values_low.reshape(N_GX, -1, model_width), tile_grid, key_grid))
        mixed_low = low(low_back(mixed_full))
        after_attn = stream + low_back(matmul_high(mixed_low, output_weight)) + output_shift
        normed_two = low(layer_norm(after_attn, gain_two, bias_two))
        pre_act = low_back(matmul_high(normed_two, up_weight) + up_shift)
        activated = low(jax.nn.gelu(pre_act, approximate=False))
        after_mlp = after_attn + low_back(matmul_high(activated, down_weight)) + down_shift
        return matmul_high(low(after_mlp), head_weight).reshape(-1, PIX)
    predicted, backward = jax.vjp(forward, pixels.astype(jnp.float32), w_patch.astype(jnp.float32), first_gain, first_bias, w_project.astype(jnp.float32), project_bias, w_output.astype(jnp.float32), merge_bias, second_gain, second_bias, w_up.astype(jnp.float32), up_bias, w_down.astype(jnp.float32), down_bias, w_head.astype(jnp.float32))
    gradients = backward(cotangent.astype(jnp.float32))
    return (predicted.astype(jnp.bfloat16), gradients[0].astype(jnp.bfloat16), gradients[1], gradients[2], gradients[3], gradients[4], gradients[5], gradients[6], gradients[7], gradients[8], gradients[9], gradients[10], gradients[11], gradients[12], gradients[13], gradients[14])
```

```python
import functools

import jax
import jax.numpy as jnp
from jax import lax
from jax.experimental import pallas as pl
from jax.experimental.pallas import tpu as pltpu
from jax.sharding import PartitionSpec as P

HEADS = 12
HEAD_DIM = 64
PAIR = 2 * HEAD_DIM
LANES = 384
SHARED = 192
EPS = 1e-06
NEG = -1e30
F32 = jnp.float32
BF16 = jnp.bfloat16
VMEM_LIMIT = 56 * 2**20


def dot(a, b):
    return jnp.dot(a, b, preferred_element_type=F32)


def dot_nt(a, b):
    return lax.dot_general(a, b, (((1,), (1,)), ((), ())), preferred_element_type=F32)


def dot_tn(a, b):
    return lax.dot_general(a, b, (((0,), (0,)), ((), ())), preferred_element_type=F32)


def shifted(x, axis, by):
    length = lax.axis_size(axis)
    pairs = [(i, i + by) for i in range(length) if 0 <= i + by < length]
    return lax.ppermute(x, axis, pairs)


def swap(x, axis, bit):
    length = lax.axis_size(axis)
    return lax.ppermute(x, axis, [(i, i ^ bit) for i in range(length)])


def gather_column(unit):
    n = lax.axis_size("gy")
    if n != 8:
        whole = lax.all_gather(unit, "gy", axis=0, tiled=False)
        me = lax.axis_index("gy")
        return [jnp.roll(whole, -me, axis=0)]
    place = lax.axis_index("gy") // 2
    at_end = (place == 0) | (place == 3)

    def along(x, hops):
        pairs = [(2 * a + y, 2 * b + y) for a, b in hops for y in (0, 1)]
        return lax.ppermute(x, "gy", pairs)

    def across(x):
        return swap(x, "gy", 1)

    outer = [(0, 1), (1, 0), (2, 3), (3, 2)]
    middle = [(1, 2), (2, 1)]
    outward = [(1, 0), (2, 3)]
    near = along(unit, outer)
    mid = along(unit, middle)
    y0 = across(unit)
    y1 = across(near)
    far_end = along(mid, outward)
    far_mid = along(near, middle)
    far = jnp.where(at_end, far_end, far_mid)
    y2 = across(far)
    last_end = along(far_mid, outward)
    last = jnp.where(at_end, last_end, mid)
    y3 = across(last)
    return [part[None] for part in (unit, near, far, last, y0, y1, y2, y3)]


def sincos_band(coordinate, band_width):
    half_width = band_width // 2
    omegas = 1.0 / 10000.0 ** (jnp.arange(half_width, dtype=F32) / half_width)
    angles = coordinate.astype(F32)[:, None] * omegas[None, :]
    return jnp.concatenate([jnp.sin(angles), jnp.cos(angles)], axis=1)


def positions(frame_index, patch_cell, model_width):
    unit_width = model_width // 16
    return jnp.concatenate(
        [
            sincos_band(frame_index, 4 * unit_width),
            sincos_band(patch_cell[0], 6 * unit_width),
            sincos_band(patch_cell[1], 6 * unit_width),
        ],
        axis=1,
    )


def layer_norm(inputs, scale_gain, shift_bias):
    centered = inputs - jnp.mean(inputs, axis=-1, keepdims=True)
    variance = jnp.mean(centered * centered, axis=-1, keepdims=True)
    return centered * lax.rsqrt(variance + EPS) * scale_gain + shift_bias


def exact_gelu(inputs):
    return jax.nn.gelu(inputs, approximate=False)


def half_mask(rows):
    return lax.broadcasted_iota(jnp.int32, (rows, PAIR), 1) < HEAD_DIM


def only_half(x, head):
    low_half = half_mask(x.shape[0])
    zero = jnp.zeros_like(x)
    return jnp.where(low_half, x, zero) if head == 0 else jnp.where(low_half, zero, x)


def merge_halves(first, second):
    return jnp.where(half_mask(first.shape[0]), first, second)


def key_bias(block_refs, key_rows, groups):
    rows = []
    for group in groups:
        width = len(group) * key_rows
        lane = lax.broadcasted_iota(jnp.int32, (1, width), 1).astype(F32)
        bias = jnp.full((1, width), NEG, F32)
        for place, (ref, index) in enumerate(group):
            count = ref[index, key_rows : key_rows + 8, 0:128].astype(F32)[0:1, 0:1]
            live = ref[index, key_rows : key_rows + 8, 128:256].astype(F32)[0:1, 0:1]
            local = lane - float(place * key_rows)
            good = (local >= 0.0) & (local < count)
            rim = (local >= float(SHARED)) & (local < float(key_rows)) & (live > 0.5)
            bias = jnp.where(good | rim, 0.0, bias)
        rows.append(bias)
    return rows


def group_blocks(block_refs):
    flat = [(ref, i) for ref in block_refs for i in range(ref.shape[0])]
    return [flat[i : i + 8] for i in range(0, len(flat), 8)]


def attend_kernel(n_blocks, key_rows, *refs):
    block_refs = refs[:n_blocks]
    own_ref, wq_ref, wk_ref, wv_ref, bq_ref, bv_ref, idc_ref, idr_ref = refs[n_blocks : n_blocks + 8]
    kv_ref, kvown_ref, q_ref, mixed_ref, lse_ref, lrow_ref = refs[n_blocks + 8 :]
    own_rows = idc_ref.shape[0]
    wkv = jnp.concatenate([wk_ref[...], wv_ref[...]], axis=1)
    shift = jnp.concatenate([jnp.zeros_like(bv_ref[...]), bv_ref[...]], axis=1)
    groups = group_blocks(block_refs)
    base = 0
    for group in groups:
        for ref, index in group:
            kv_ref[0, base : base + key_rows, :] = (dot(ref[index, 0:key_rows, :], wkv) + shift).astype(BF16)
            base += key_rows
    kvown_ref[0] = (dot(own_ref[...], wkv) + shift).astype(BF16)
    q = (dot(own_ref[0:own_rows, :], wq_ref[...]) + bq_ref[...]).astype(BF16) * BF16(HEAD_DIM**-0.5)
    q_ref[0] = q
    biases = key_bias(block_refs, key_rows, groups)
    idc, idr = idc_ref[...], idr_ref[...]
    allowed = (idc == idr) & (idc != 0)
    shared_row = idc == 0
    outs, lses = [], []
    for head in range(2):
        qs = only_half(q[0:SHARED], head)
        peak = weight = total = None
        base = 0
        for group, bias in zip(groups, biases):
            width = len(group) * key_rows
            keys = kv_ref[0, base : base + width, 0:PAIR]
            values = kv_ref[0, base : base + width, PAIR:]
            base += width
            scores = dot_nt(qs, keys) + bias
            top = jnp.max(scores, axis=1, keepdims=True)
            if peak is None:
                probs = jnp.exp(scores - top)
                weight = jnp.sum(probs, axis=1, keepdims=True)
                total = dot(probs.astype(BF16), values)
                peak = top
            else:
                new = jnp.maximum(peak, top)
                probs = jnp.exp(scores - new)
                fade = jnp.exp(peak - new)
                weight = weight * fade + jnp.sum(probs, axis=1, keepdims=True)
                total = total * fade + dot(probs.astype(BF16), values)
                peak = new
        shared_out = total / weight
        shared_lse = peak + jnp.log(weight)
        ql = only_half(q, head)
        scores = jnp.where(allowed, dot_nt(ql, kvown_ref[0, 0:own_rows, 0:PAIR]), NEG)
        top = jnp.max(scores, axis=1, keepdims=True)
        probs = jnp.exp(scores - top)
        weight = jnp.sum(probs, axis=1, keepdims=True)
        local_out = dot(probs.astype(BF16), kvown_ref[0, 0:own_rows, PAIR:]) / weight
        local_lse = top + jnp.log(weight)
        outs.append(
            jnp.concatenate(
                [jnp.where(shared_row[0:SHARED], shared_out, local_out[0:SHARED]), local_out[SHARED:]], axis=0
            )
        )
        lses.append(
            jnp.concatenate(
                [jnp.where(shared_row[0:SHARED], shared_lse, local_lse[0:SHARED]), local_lse[SHARED:]], axis=0
            )
        )
    mixed_ref[...] = merge_halves(*outs)
    lse = merge_halves(
        jnp.broadcast_to(lses[0], (own_rows, PAIR)), jnp.broadcast_to(lses[1], (own_rows, PAIR))
    )
    lse_ref[...] = lse
    turned = lse.T
    lrow_ref[0, 0:8, :] = turned[0:8]
    lrow_ref[0, 8:16, :] = turned[HEAD_DIM : HEAD_DIM + 8]


def full(shape):
    zeros = (0,) * len(shape)
    return pl.BlockSpec(tuple(shape), lambda h: zeros, pipeline_mode=pl.Buffered(1))


def params():
    return pltpu.CompilerParams(vmem_limit_bytes=VMEM_LIMIT)


def attend(blocks, first_low, w_project, project_bias, idc, idr, key_rows):
    own_rows = idc.shape[0]
    joined_rows = first_low.shape[0]
    pairs = HEADS // 2
    count = sum(b.shape[0] for b in blocks)
    width = first_low.shape[1]
    keys = count * key_rows
    bias = project_bias.reshape(1, -1)
    col = lambda off: pl.BlockSpec((width, PAIR), lambda h: (0, off + h))
    vec = lambda off: pl.BlockSpec((1, PAIR), lambda h: (0, off + h))
    out_shape = (
        jax.ShapeDtypeStruct((pairs, keys, 2 * PAIR), BF16),
        jax.ShapeDtypeStruct((pairs, joined_rows, 2 * PAIR), BF16),
        jax.ShapeDtypeStruct((pairs, own_rows, PAIR), BF16),
        jax.ShapeDtypeStruct((own_rows, width), F32),
        jax.ShapeDtypeStruct((own_rows, width), F32),
        jax.ShapeDtypeStruct((pairs, 16, own_rows), F32),
    )
    out_specs = (
        pl.BlockSpec((1, keys, 2 * PAIR), lambda h: (h, 0, 0)),
        pl.BlockSpec((1, joined_rows, 2 * PAIR), lambda h: (h, 0, 0)),
        pl.BlockSpec((1, own_rows, PAIR), lambda h: (h, 0, 0)),
        pl.BlockSpec((own_rows, PAIR), lambda h: (0, h)),
        pl.BlockSpec((own_rows, PAIR), lambda h: (0, h)),
        pl.BlockSpec((1, 16, own_rows), lambda h: (h, 0, 0)),
    )
    return pl.pallas_call(
        functools.partial(attend_kernel, len(blocks), key_rows),
        grid=(pairs,),
        in_specs=[full(b.shape) for b in blocks]
        + [full(first_low.shape), col(0), col(pairs), col(2 * pairs), vec(0), vec(pairs), full(idc.shape), full(idr.shape)],
        out_specs=out_specs,
        out_shape=out_shape,
        compiler_params=params(),
        cost_estimate=pl.CostEstimate(
            flops=2 * keys * width * (2 * width + 2 * SHARED), bytes_accessed=20 * 2**20, transcendentals=HEADS * keys * SHARED
        ),
        name="attend",
    )(*blocks, first_low, w_project, w_project, w_project, bias, bias, idc, idr)


def query_kernel(n_blocks, key_rows, *refs):
    block_refs = refs[:n_blocks]
    kv_ref, kvown_ref, q_ref, grad_ref, mixed_ref, lse_ref, wq_ref, bq_ref, idc_ref, idr_ref = refs[
        n_blocks : n_blocks + 10
    ]
    dq_ref, qall_ref = refs[n_blocks + 10 :]
    own_rows = idc_ref.shape[0]
    groups = group_blocks(block_refs)
    base = 0
    for group in groups:
        for ref, index in group:
            qall_ref[0, base : base + SHARED, :] = (dot(ref[index, 0:SHARED, :], wq_ref[...]) + bq_ref[...]).astype(
                BF16
            ) * BF16(HEAD_DIM**-0.5)
            base += SHARED
    biases = key_bias(block_refs, key_rows, groups)
    idc, idr = idc_ref[...], idr_ref[...]
    allowed = (idc == idr) & (idc != 0)
    shared_row = idc == 0
    q = q_ref[0]
    grad = grad_ref[...]
    product = grad.astype(F32) * mixed_ref[...]
    outs = []
    for head in range(2):
        delta = jnp.sum(only_half(product, head), axis=1, keepdims=True)
        lse = lse_ref[:, head * HEAD_DIM : head * HEAD_DIM + 1]
        qm = only_half(q, head)
        gm = only_half(grad, head)
        total = None
        base = 0
        for group, bias in zip(groups, biases):
            width = len(group) * key_rows
            keys = kv_ref[0, base : base + width, 0:PAIR]
            values = kv_ref[0, base : base + width, PAIR:]
            base += width
            probs = jnp.exp(dot_nt(qm[0:SHARED], keys) + bias - lse[0:SHARED])
            dp = dot_nt(gm[0:SHARED], values)
            ds = (probs * (dp - delta[0:SHARED])).astype(BF16)
            part = dot(ds, keys)
            total = part if total is None else total + part
        keys, values = kvown_ref[0, 0:own_rows, 0:PAIR], kvown_ref[0, 0:own_rows, PAIR:]
        probs = jnp.exp(jnp.where(allowed, dot_nt(qm, keys) - lse, NEG))
        ds = (probs * (dot_nt(gm, values) - delta)).astype(BF16)
        local = dot(ds, keys)
        outs.append(
            jnp.concatenate([jnp.where(shared_row[0:SHARED], total, local[0:SHARED]), local[SHARED:]], axis=0)
        )
    dq_ref[...] = (merge_halves(*outs) * HEAD_DIM**-0.5).astype(BF16)


def query_back(blocks, kv, kvown, q, mixed_grad, mixed, lse, w_project, project_bias, idc, idr, key_rows):
    own_rows = idc.shape[0]
    pairs = HEADS // 2
    count = sum(b.shape[0] for b in blocks)
    width = mixed_grad.shape[1]
    keys = count * key_rows
    bias = project_bias.reshape(1, -1)
    lane = lambda: pl.BlockSpec((own_rows, PAIR), lambda h: (0, h))
    lead = lambda x: pl.BlockSpec((1,) + x.shape[1:], lambda h: (h, 0, 0))
    return pl.pallas_call(
        functools.partial(query_kernel, len(blocks), key_rows),
        grid=(pairs,),
        in_specs=[full(b.shape) for b in blocks]
        + [
            lead(kv),
            lead(kvown),
            lead(q),
            lane(),
            lane(),
            lane(),
            pl.BlockSpec((width, PAIR), lambda h: (0, h)),
            pl.BlockSpec((1, PAIR), lambda h: (0, h)),
            full(idc.shape),
            full(idr.shape),
        ],
        out_specs=(
            pl.BlockSpec((own_rows, PAIR), lambda h: (0, h)),
            pl.BlockSpec((1, count * SHARED, PAIR), lambda h: (h, 0, 0)),
        ),
        out_shape=(
            jax.ShapeDtypeStruct((own_rows, width), BF16),
            jax.ShapeDtypeStruct((pairs, count * SHARED, PAIR), BF16),
        ),
        compiler_params=params(),
        cost_estimate=pl.CostEstimate(
            flops=2 * keys * width * 6 * SHARED, bytes_accessed=20 * 2**20, transcendentals=HEADS * keys * SHARED
        ),
        name="query_back",
    )(*blocks, kv, kvown, q, mixed_grad, mixed, lse, w_project, bias, idc, idr)


def key_kernel(n_blocks, *refs):
    grad_refs = refs[:n_blocks]
    kvown_ref, qall_ref, stat_ref, q_ref, grad_ref, lrow_ref, drow_ref, idc_ref, idr_ref, live_ref = refs[
        n_blocks : n_blocks + 10
    ]
    dk_ref, dv_ref, grads_ref = refs[n_blocks + 10 :]
    own_rows = idc_ref.shape[0]
    rim = kvown_ref.shape[1] - own_rows
    base = 0
    for ref in grad_refs:
        for i in range(ref.shape[0]):
            grads_ref[base : base + SHARED, :] = ref[i]
            base += SHARED
    idc, idr = idc_ref[...], idr_ref[...]
    allowed = (idc == idr) & (idc != 0)
    shared_row = idc == 0
    live = live_ref[0:1, 0:1] > 0.5
    kv = kvown_ref[0]
    k_all, v_all = kv[:, 0:PAIR], kv[:, PAIR:]
    k_sh = jnp.concatenate([k_all[0:SHARED], k_all[own_rows:]], axis=0)
    v_sh = jnp.concatenate([v_all[0:SHARED], v_all[own_rows:]], axis=0)
    q, grad = q_ref[0], grad_ref[...]
    dks, dvs = [], []
    chunk = min(base, 1536)
    for head in range(2):
        km, vm = only_half(k_sh, head), only_half(v_sh, head)
        dk = dv = None
        for start in range(0, base, chunk):
            q_all = qall_ref[0, start : start + chunk, :]
            g_all = grads_ref[start : start + chunk, :]
            lse = stat_ref[0, head : head + 1, start : start + chunk]
            delta = stat_ref[0, 2 + head : 3 + head, start : start + chunk]
            probs = jnp.exp(dot_nt(km, q_all) - lse)
            part_v = dot(probs.astype(BF16), g_all)
            ds = (probs * (dot_nt(vm, g_all) - delta)).astype(BF16)
            part_k = dot(ds, q_all)
            dk = part_k if dk is None else dk + part_k
            dv = part_v if dv is None else dv + part_v
        lse = lrow_ref[0, 8 * head : 8 * head + 1, :]
        delta = drow_ref[0, head : head + 1, :]
        probs = jnp.exp(jnp.where(allowed, dot_nt(only_half(k_all[0:own_rows], head), q) - lse, NEG))
        local_v = dot(probs.astype(BF16), grad)
        ds = (probs * (dot_nt(only_half(v_all[0:own_rows], head), grad) - delta)).astype(BF16)
        local_k = dot(ds, q)

        def rows(shared, local):
            return jnp.concatenate(
                [
                    jnp.where(shared_row[0:SHARED], shared[0:SHARED], local[0:SHARED]),
                    local[SHARED:],
                    jnp.where(live, shared[SHARED : SHARED + rim], 0.0),
                ],
                axis=0,
            )

        dks.append(rows(dk, local_k))
        dvs.append(rows(dv, local_v))
    dk_ref[...] = merge_halves(*dks).astype(BF16)
    dv_ref[...] = merge_halves(*dvs).astype(BF16)


def key_back(grads, kvown, qall, stats, q, mixed_grad, lrow, drow, idc, idr, live):
    own_rows = idc.shape[0]
    joined_rows = kvown.shape[1]
    pairs = HEADS // 2
    width = mixed_grad.shape[1]
    lead = lambda x: pl.BlockSpec((1,) + x.shape[1:], lambda h: (h, 0, 0))
    out = lambda: pl.BlockSpec((joined_rows, PAIR), lambda h: (0, h))
    return pl.pallas_call(
        functools.partial(key_kernel, len(grads)),
        grid=(pairs,),
        in_specs=[pl.BlockSpec((g.shape[0], SHARED, PAIR), lambda h: (0, 0, h)) for g in grads]
        + [
            lead(kvown),
            lead(qall),
            lead(stats),
            lead(q),
            pl.BlockSpec((own_rows, PAIR), lambda h: (0, h)),
            lead(lrow),
            lead(drow),
            full(idc.shape),
            full(idr.shape),
            full(live.shape),
        ],
        out_specs=(out(), out()),
        out_shape=(jax.ShapeDtypeStruct((joined_rows, width), BF16),) * 2,
        scratch_shapes=[pltpu.VMEM((qall.shape[1], PAIR), BF16)],
        compiler_params=params(),
        cost_estimate=pl.CostEstimate(
            flops=2 * qall.shape[1] * width * 4 * (SHARED + 128),
            bytes_accessed=10 * 2**20,
            transcendentals=HEADS * qall.shape[1] * (SHARED + 128),
        ),
        name="key_back",
    )(*grads, kvown, qall, stats, q, mixed_grad, lrow, drow, idc, idr, live)


def bit_of(axis, bit):
    return (lax.axis_index(axis) // bit) % 2


def halve(x, axis, bit, dim):
    mine = bit_of(axis, bit)
    send = lax.dynamic_index_in_dim(x, 1 - mine, dim, keepdims=False)
    keep = lax.dynamic_index_in_dim(x, mine, dim, keepdims=False)
    return keep + swap(send, axis, bit)


def core_stage(left, right):
    half = right.shape[1] // 2
    core = bit_of("gx", 1)
    other = lax.dynamic_slice_in_dim(right, (1 - core) * half, half, axis=1)
    mine = lax.dynamic_slice_in_dim(right, core * half, half, axis=1)
    arrived = swap(dot_tn(left, other).astype(BF16), "gx", 1)
    return (dot_tn(left, mine) + arrived.astype(F32)).astype(BF16)


def to_rows(x, n):
    r, blocks = x.shape[0] // n, x.shape[1] // LANES
    return x.reshape(n, r, blocks, LANES).transpose(0, 2, 1, 3).reshape(n, r * blocks, LANES)


def from_rows(x, r):
    blocks = x.shape[0] // r
    return x.reshape(blocks, r, LANES).transpose(1, 0, 2).reshape(r, blocks * LANES)


def scatter_sum(x, x_first):
    n, rows, lanes = x.shape
    x = x.reshape(2, 2, 2, 2, rows // 2, lanes)
    if x_first:
        x = halve(x, "gx", 2, 3)
        x = halve(x, "gy", 1, 2)
    else:
        x = halve(x, "gy", 1, 2)
        x = halve(x, "gx", 2, 2)
    x = halve(x, "gy", 2, 1)
    return halve(x, "gy", 4, 0)


def both_halves(x, axis, bit, dim):
    other = swap(x, axis, bit)
    mine = bit_of(axis, bit)
    first = jnp.where(mine == 0, x, other)
    second = jnp.where(mine == 0, other, x)
    return jnp.concatenate([first, second], axis=dim)


def shards(
    pixels,
    frame_index,
    patch_cell,
    tile_id,
    halo_index,
    w_patch,
    first_gain,
    first_bias,
    w_project,
    project_bias,
    w_output,
    merge_bias,
    second_gain,
    second_bias,
    w_up,
    up_bias,
    w_down,
    down_bias,
    w_head,
    cotangent,
):
    n_gx, n_gy = lax.axis_size("gx"), lax.axis_size("gy")
    own_rows = pixels.shape[0]
    rim_count = halo_index.shape[0]
    width = w_output.shape[0]
    key_rows = SHARED + rim_count
    idc, idr = tile_id.reshape(own_rows, 1), tile_id.reshape(1, own_rows)
    live = jnp.where(lax.axis_index("gx") > 0, 1.0, 0.0).astype(F32)
    count = jnp.sum((tile_id == 0).astype(F32))

    stream = dot(pixels, w_patch) + positions(frame_index, patch_cell, width)
    outgoing = jnp.take(stream, halo_index, axis=0).astype(BF16)
    arrived = shifted(outgoing, "gx", 1).astype(F32)
    normed_own, own_back = jax.vjp(layer_norm, stream, first_gain, first_bias)
    normed_rim, rim_back = jax.vjp(layer_norm, arrived, first_gain, first_bias)
    own_low, rim_low = normed_own.astype(BF16), normed_rim.astype(BF16)
    first_low = jnp.concatenate([own_low, rim_low], axis=0)
    lane = jnp.arange(width)[None, :]
    marks = jnp.where(lane < 128, count, live).astype(BF16)
    unit = jnp.concatenate([own_low[:SHARED], rim_low, jnp.broadcast_to(marks, (16, width))], axis=0)
    blocks = gather_column(unit)
    kv, kvown, q, mixed, lse, lrow = attend(blocks, first_low, w_project, project_bias, idc, idr, key_rows)

    mixed_low = mixed.astype(BF16)
    after_attn = stream + dot(mixed_low, w_output) + merge_bias
    normed_two, second_back = jax.vjp(layer_norm, after_attn, second_gain, second_bias)
    second_low = normed_two.astype(BF16)
    pre_act = dot(second_low, w_up) + up_bias
    activated, gelu_back = jax.vjp(exact_gelu, pre_act)
    act_low = activated.astype(BF16)
    after_mlp = after_attn + dot(act_low, w_down) + down_bias
    final_low = after_mlp.astype(BF16)
    predicted = dot(final_low, w_head).astype(BF16)
    mlp_grad = dot_nt(cotangent, w_head)
    down_bias_grad = jnp.sum(mlp_grad, axis=0)
    mlp_low = mlp_grad.astype(BF16)
    act_grad = dot_nt(mlp_low, w_down)
    pre_grad = gelu_back(act_grad)[0].astype(BF16)
    up_bias_grad = jnp.sum(pre_grad.astype(F32), axis=0)
    normed_two_grad = dot_nt(pre_grad, w_up)
    resid_grad, second_gain_grad, second_bias_grad = second_back(normed_two_grad)
    attn_grad = mlp_grad + resid_grad
    merge_bias_grad = jnp.sum(attn_grad, axis=0)
    attn_low = attn_grad.astype(BF16)
    mixed_grad = dot_nt(attn_low, w_output).astype(BF16)
    delta = jnp.sum((mixed_grad.astype(F32) * mixed).reshape(own_rows, HEADS, HEAD_DIM), axis=2).T

    in_shared = tile_id[:SHARED] == 0
    lse_row = lrow[:, ::8, :].reshape(HEADS, own_rows)
    lse_sent = jnp.where(in_shared[None], lse_row[:, :SHARED], 1e30)
    delta_sent = jnp.where(in_shared[None], delta[:, :SHARED], 0.0)

    def two(x):
        high = x.astype(BF16)
        return high, (x - high.astype(F32)).astype(BF16)

    stats = jnp.concatenate(two(lse_sent) + two(delta_sent), axis=1)
    stats = jnp.pad(stats, ((0, 16 - HEADS), (0, width - 4 * SHARED)))
    grad_sent = jnp.where(in_shared[:, None], mixed_grad[:SHARED], jnp.zeros((), BF16))
    grads = gather_column(jnp.concatenate([grad_sent, stats], axis=0))
    dq, qall = query_back(blocks, kv, kvown, q, mixed_grad, mixed, lse, w_project, project_bias, idc, idr, key_rows)
    packed = jnp.concatenate([g[:, SHARED : SHARED + HEADS, : 4 * SHARED] for g in grads], axis=0).astype(F32)
    packed = packed.reshape(n_gy, HEADS, 4, SHARED)
    packed = jnp.stack([packed[:, :, 0] + packed[:, :, 1], packed[:, :, 2] + packed[:, :, 3]], axis=0)
    packed = packed.reshape(2, n_gy, HEADS // 2, 2, SHARED).transpose(2, 0, 3, 1, 4)
    packed = packed.reshape(HEADS // 2, 4, n_gy * SHARED)
    live_tile = jnp.broadcast_to(live, (8, 128))
    dk, dv = key_back(
        grads, kvown, qall, packed, q, mixed_grad, lrow, delta.reshape(HEADS // 2, 2, own_rows), idc, idr, live_tile
    )

    dq_full = jnp.pad(dq, ((0, rim_count), (0, 0)))
    joint_grad = jnp.concatenate([dq_full, dk, dv], axis=1)
    project_bias_grad = jnp.concatenate([jnp.sum(dq.astype(F32), axis=0), jnp.sum(dv.astype(F32), axis=0)])
    normed_grad = dot_nt(joint_grad, w_project)
    rim_grad, rim_gain, rim_bias = rim_back(normed_grad[own_rows:])
    returned = shifted(rim_grad.astype(BF16), "gx", -1)
    own_grad, own_gain, own_bias = own_back(normed_grad[:own_rows])
    first_gain_grad, first_bias_grad = own_gain + rim_gain, own_bias + rim_bias
    spread = (jnp.arange(own_rows)[:, None] == halo_index[None, :]).astype(BF16)
    stream_grad = own_grad + attn_grad + dot(spread, returned)
    embed_low = stream_grad.astype(BF16)
    pixel_grad = dot_nt(embed_low, w_patch).astype(BF16)

    vectors = [
        first_gain_grad,
        first_bias_grad,
        project_bias_grad,
        merge_bias_grad,
        second_gain_grad,
        second_bias_grad,
        up_bias_grad,
        down_bias_grad,
    ]
    sizes = [v.shape[0] // n_gy for v in vectors]
    joined = [
        (final_low, cotangent),
        (act_low, mlp_low),
        (second_low, pre_grad),
        (mixed_low, attn_low),
        (first_low, joint_grad),
        (pixels, embed_low),
    ]
    if n_gx == 4 and n_gy == 8:
        core = bit_of("gx", 1)
        piles = [to_rows(core_stage(a, b), n_gy) for a, b in joined]
        flat = jnp.concatenate([v.reshape(n_gy, -1) for v in vectors], axis=1).astype(BF16)
        half = sum(sizes) // 2
        flat = flat.reshape(n_gy, 2, half)
        small = halve(flat, "gx", 1, 1)
        small = jnp.pad(small, ((0, 0), (0, 32 * LANES - half))).reshape(n_gy, 32, LANES)
        head_pile, down_pile, up_pile, output_pile, project_pile, patch_pile = piles
        parts = [
            scatter_sum(jnp.concatenate([head_pile, down_pile], axis=1), True),
            scatter_sum(jnp.concatenate([up_pile, output_pile], axis=1), False),
            scatter_sum(project_pile, True),
            scatter_sum(jnp.concatenate([patch_pile, small], axis=1), False),
        ]
        early = [both_halves(p, "gx", 2, 0) for p in parts]
        done = [swap(e, "gx", 1) for e in early]
        lows = [jnp.where(core == 0, e, d).astype(F32) for e, d in zip(early, done)]
        highs = [jnp.where(core == 0, d, e).astype(F32) for e, d in zip(early, done)]

        def cut(group, start, stop, r):
            return jnp.concatenate(
                [from_rows(lows[group][start:stop], r), from_rows(highs[group][start:stop], r)], axis=1
            )

        counts = [p.shape[1] for p in piles]
        rows = [a.shape[1] // n_gy for a, _ in joined]
        head_grad = cut(0, 0, counts[0], rows[0])
        down_grad = cut(0, counts[0], counts[0] + counts[1], rows[1])
        up_grad = cut(1, 0, counts[2], rows[2])
        output_grad = cut(1, counts[2], counts[2] + counts[3], rows[3])
        project_grad = cut(2, 0, counts[4], rows[4])
        patch_grad = cut(3, 0, counts[5], rows[5])
        tail = [part[3][counts[5] :].reshape(-1)[:half] for part in (lows, highs)]
        tail = jnp.concatenate(tail)
    else:

        def total(x):
            part = lax.psum_scatter(x.astype(BF16), "gy", scatter_dimension=0, tiled=True)
            return lax.psum(part, "gx").astype(F32)

        head_grad, down_grad, up_grad, output_grad, project_grad, patch_grad = [
            total(dot_tn(a, b)) for a, b in joined
        ]
        flat = jnp.concatenate([v.reshape(n_gy, -1) for v in vectors], axis=1)
        tail = total(flat).reshape(-1)
    starts = [sum(sizes[:i]) for i in range(len(sizes))]
    small_outs = [tail[s : s + z] for s, z in zip(starts, sizes)]
    return (
        predicted,
        pixel_grad,
        patch_grad,
        small_outs[0],
        small_outs[1],
        project_grad,
        small_outs[2],
        output_grad,
        small_outs[3],
        small_outs[4],
        small_outs[5],
        up_grad,
        small_outs[6],
        down_grad,
        small_outs[7],
        head_grad,
    )


def solution(mesh):
    tokens = P(("gx", "gy"))
    rows = P(("gx", "gy"), None)
    in_specs = (rows, tokens, P(None, ("gx", "gy")), tokens, tokens) + (P(),) * 14 + (rows,)
    matrix, vector = P("gy", None), P("gy")
    out_specs = (
        rows,
        rows,
        matrix,
        vector,
        vector,
        matrix,
        vector,
        matrix,
        vector,
        vector,
        vector,
        matrix,
        vector,
        matrix,
        vector,
        matrix,
    )
    return jax.shard_map(shards, mesh=mesh, in_specs=in_specs, out_specs=out_specs, check_vma=False)
```

```python
import functools

import jax
import jax.numpy as jnp
import numpy as np
from jax import lax
from jax.experimental import pallas as pl
from jax.experimental.pallas import tpu as pltpu
from jax.sharding import PartitionSpec as P

HEADS = 12
HEAD_DIM = 64
PAIR = 2 * HEAD_DIM
PAIRS = HEADS // 2
SCALE = HEAD_DIM**-0.5
LANES = 384
SHARED = 192
MARKS = 16
GRID_SIDE = 56
EPS = 1e-06
NEG = -1e30
F32 = jnp.float32
BF16 = jnp.bfloat16
VMEM_LIMIT = 56 * 2**20


def dot(a, b):
    return jnp.dot(a, b, preferred_element_type=F32)


def dot_nt(a, b, precision=None):
    return lax.dot_general(a, b, (((1,), (1,)), ((), ())), preferred_element_type=F32, precision=precision)


def dot_tn(a, b):
    return lax.dot_general(a, b, (((0,), (0,)), ((), ())), preferred_element_type=F32)


def sds(shape, dtype):
    return jax.ShapeDtypeStruct(tuple(shape), dtype)


def shifted(x, axis, by):
    length = lax.axis_size(axis)
    pairs = [(i, i + by) for i in range(length) if 0 <= i + by < length]
    return lax.ppermute(x, axis, pairs)


def swap(x, axis, bit):
    length = lax.axis_size(axis)
    return lax.ppermute(x, axis, [(i, i ^ bit) for i in range(length)])


def gather_column(unit):
    n = lax.axis_size("gy")
    if n != 8:
        whole = lax.all_gather(unit, "gy", axis=0, tiled=False)
        return [[whole]]
    place = lax.axis_index("gy") // 2
    at_end = (place == 0) | (place == 3)

    def along(x, hops):
        pairs = [(2 * a + y, 2 * b + y) for a, b in hops for y in (0, 1)]
        return lax.ppermute(x, "gy", pairs)

    def across(x):
        return swap(x, "gy", 1)

    outer = [(0, 1), (1, 0), (2, 3), (3, 2)]
    middle = [(1, 2), (2, 1)]
    outward = [(1, 0), (2, 3)]
    y0 = across(unit)
    near = along(unit, outer)
    mid = along(unit, middle)
    y1 = across(near)
    far_end = along(mid, outward)
    far_mid = along(near, middle)
    far = jnp.where(at_end, far_end, far_mid)
    y2 = across(far)
    last_end = along(far_mid, outward)
    last = jnp.where(at_end, last_end, mid)
    y3 = across(last)
    groups = [[unit, near, y0], [y1, far, last], [y2, y3]]
    return [[part[None] for part in group] for group in groups]


def bit_of(axis, bit):
    return (lax.axis_index(axis) // bit) % 2


def call(kernel, ins, outs, name, grid=None, scratch=(), cost=4.0, after=()):
    specs = [spec for _, spec in ins] + [pl.BlockSpec(memory_space=pl.ANY)] * len(after)
    count = len(ins)

    def body(*refs):
        kernel(*refs[:count], *refs[count + len(after) :])

    return pl.pallas_call(
        body,
        grid=grid or (),
        in_specs=specs,
        out_specs=tuple(spec for _, spec in outs),
        out_shape=tuple(shape for shape, _ in outs),
        scratch_shapes=list(scratch),
        compiler_params=pltpu.CompilerParams(vmem_limit_bytes=VMEM_LIMIT),
        cost_estimate=pl.CostEstimate(flops=int(cost * 1e8), bytes_accessed=int(cost * 3e5), transcendentals=0),
        name=name,
    )(*[array for array, _ in ins], *after)


VMEM = pl.BlockSpec(memory_space=pltpu.VMEM)


def plain(*arrays):
    return [(a, VMEM) for a in arrays]


def fixed(array):
    zeros = (0,) * len(array.shape)
    return (array, pl.BlockSpec(tuple(array.shape), lambda h: zeros, pipeline_mode=pl.Buffered(1)))


def lead(array, first=0):
    zeros = (0,) * (len(array.shape) - 1)
    return (array, pl.BlockSpec((1,) + tuple(array.shape[1:]), lambda h: (first + h,) + zeros))


def lanes(array, first=0, width=PAIR):
    return (array, pl.BlockSpec((array.shape[0], width), lambda h: (0, first + h)))


def half_mask(rows):
    return lax.broadcasted_iota(jnp.int32, (rows, PAIR), 1) < HEAD_DIM


def only_half(x, head):
    low_half = half_mask(x.shape[0])
    zero = jnp.zeros_like(x)
    return jnp.where(low_half, x, zero) if head == 0 else jnp.where(low_half, zero, x)


def merge_halves(first, second):
    rows = first.shape[0]
    return jnp.where(half_mask(rows), jnp.broadcast_to(first, (rows, PAIR)), jnp.broadcast_to(second, (rows, PAIR)))


def normalise(x):
    centered = x - jnp.mean(x, axis=1, keepdims=True)
    scale = lax.rsqrt(jnp.mean(centered * centered, axis=1, keepdims=True) + EPS)
    return centered * scale, scale


def norm_back(grad, unit_rows, scale, gain):
    g = grad * gain
    inner = jnp.mean(g * unit_rows, axis=1, keepdims=True)
    rows = scale * (g - jnp.mean(g, axis=1, keepdims=True) - unit_rows * inner)
    return rows, jnp.sum(grad * unit_rows, axis=0, keepdims=True), jnp.sum(grad, axis=0, keepdims=True)


def group_blocks(block_refs):
    flat = [(ref, i) for ref in block_refs for i in range(ref.shape[0])]
    return [flat[i : i + 8] for i in range(0, len(flat), 8)]


def key_bias(groups, key_rows):
    rows = []
    for group in groups:
        width = len(group) * key_rows
        lane = lax.broadcasted_iota(jnp.int32, (1, width), 1).astype(F32)
        bias = jnp.full((1, width), NEG, F32)
        for place, (ref, index) in enumerate(group):
            marks = ref[index, key_rows : key_rows + MARKS, 0:256].astype(F32)
            count, live = marks[0:1, 0:1], marks[0:1, 128:129]
            local = lane - float(place * key_rows)
            good = (local >= 0.0) & (local < count)
            rim = (local >= float(SHARED)) & (local < float(key_rows)) & (live > 0.5)
            bias = jnp.where(good | rim, 0.0, bias)
        rows.append(bias)
    return rows


def position_table(width):
    unit_width = width // 16
    table = np.zeros((128, width), np.float32)
    bands = [(0, 8, 0, 4 * unit_width), (8, GRID_SIDE, 4 * unit_width, 6 * unit_width)]
    bands.append((64, GRID_SIDE, 10 * unit_width, 6 * unit_width))
    for row, count, lane, band in bands:
        half = band // 2
        power = np.arange(half, dtype=np.float32) / np.float32(half)
        omegas = np.float32(1.0) / np.power(np.float32(10000.0), power)
        angles = (np.arange(count, dtype=np.float32)[:, None] * omegas[None]).astype(np.float64)
        table[row : row + count, lane : lane + half] = np.sin(angles)
        table[row : row + count, lane + half : lane + band] = np.cos(angles)
    high = table.astype(jnp.bfloat16)
    low = (table - high.astype(np.float32)).astype(jnp.bfloat16)
    return jnp.asarray(high), jnp.asarray(low)


def embed_kernel(pix, weight, frame, cell, halo, high, low, gain, bias, stream_ref, rim_ref, low_ref):
    rows = pix.shape[0]
    code = lax.broadcasted_iota(jnp.int32, (128, rows), 0)
    first, second = cell[0:1, :], cell[1:2, :]
    hot = (code == frame[...]) | (code == first + 8) | (code == second + 64)
    hot = jnp.where(hot, 1.0, 0.0).astype(BF16)
    stream = dot(pix[...], weight[...]) + (dot_tn(hot, high[...]) + dot_tn(hot, low[...]))
    stream_ref[...] = stream
    place = lax.broadcasted_iota(jnp.int32, (rows, halo.shape[1]), 0)
    pick = jnp.where(place == halo[...], 1.0, 0.0).astype(BF16)
    rim_ref[...] = dot_tn(pick, stream.astype(BF16)).astype(BF16)
    unit_rows, _ = normalise(stream)
    low_ref[...] = (unit_rows * gain[...] + bias[...]).astype(BF16)


def unit_kernel(own, arrived, gain, bias, ids, live, unit_ref, joined_ref):
    rows, width = own.shape
    rim = arrived.shape[0]
    unit_rows, _ = normalise(arrived[...].astype(F32))
    rim_low = (unit_rows * gain[...] + bias[...]).astype(BF16)
    joined_ref[0:rows, :] = own[...]
    joined_ref[rows : rows + rim, :] = rim_low
    unit_ref[0:SHARED, :] = own[0:SHARED, :]
    unit_ref[SHARED : SHARED + rim, :] = rim_low
    count = jnp.sum(jnp.where(ids[...] == 0, 1.0, 0.0), axis=1, keepdims=True)
    lane = lax.broadcasted_iota(jnp.int32, (MARKS, width), 1)
    unit_ref[SHARED + rim :, :] = jnp.where(lane < 128, count, live[0:1, 0:1]).astype(BF16)


def attend_kernel(n_blocks, key_rows, first, last, *refs):
    refs = list(refs)

    def take(n):
        out = refs[:n]
        del refs[:n]
        return out

    block_refs = take(n_blocks)
    wk_ref, wv_ref, bv_ref = take(3)
    if first:
        own_ref, wq_ref, bq_ref, idr_ref = take(4)
    else:
        q_ref, acc_in, peak_in, weight_in = take(4)
        if last:
            out_in, lse_in = take(2)
    idc_ref = take(1)[0]
    kv_ref = take(1)[0]
    if first:
        q_ref, kvown_ref = take(2)
        if not last:
            out_ref, lse_ref = take(2)
    if last:
        mixed_ref, full_lse_ref = take(2)
    else:
        acc_ref, peak_ref, weight_ref = take(3)
    own_rows = idc_ref.shape[0]
    wkv = jnp.concatenate([wk_ref[...], wv_ref[...]], axis=1)
    shift = jnp.concatenate([jnp.zeros_like(bv_ref[...]), bv_ref[...]], axis=1)
    groups = group_blocks(block_refs)
    base = 0
    for group in groups:
        for ref, index in group:
            kv_ref[0, base : base + key_rows, :] = (dot(ref[index, 0:key_rows, :], wkv) + shift).astype(BF16)
            base += key_rows
    if first:
        kvown_ref[0] = (dot(own_ref[...], wkv) + shift).astype(BF16)
        q = (dot(own_ref[0:own_rows, :], wq_ref[...]) + bq_ref[...]).astype(BF16) * BF16(SCALE)
        q_ref[0] = q
    else:
        q = q_ref[0]
    biases = key_bias(groups, key_rows)
    results = []
    for head in range(2):
        qs = only_half(q[0:SHARED], head)
        column = slice(head * HEAD_DIM, head * HEAD_DIM + 1)
        if first:
            peak = weight = total = None
        else:
            peak, weight, total = peak_in[:, column], weight_in[:, column], acc_in[...]
        base = 0
        for group, bias in zip(groups, biases):
            width = len(group) * key_rows
            keys = kv_ref[0, base : base + width, 0:PAIR]
            values = kv_ref[0, base : base + width, PAIR:]
            base += width
            scores = dot_nt(qs, keys) + bias
            top = jnp.max(scores, axis=1, keepdims=True)
            if peak is None:
                probs = jnp.exp(scores - top)
                weight = jnp.sum(probs, axis=1, keepdims=True)
                total = dot(probs.astype(BF16), values)
                peak = top
            else:
                new = jnp.maximum(peak, top)
                probs = jnp.exp(scores - new)
                fade = jnp.exp(peak - new)
                weight = weight * fade + jnp.sum(probs, axis=1, keepdims=True)
                total = total * fade + dot(probs.astype(BF16), values)
                peak = new
        results.append((total, peak, weight))
    (total_a, peak_a, weight_a), (total_b, peak_b, weight_b) = results
    if first:
        idc = idc_ref[...]
        allowed = (idc == idr_ref[...]) & (idc != 0)
        local = []
        for head in range(2):
            scores = jnp.where(allowed, dot_nt(only_half(q, head), kvown_ref[0, 0:own_rows, 0:PAIR]), NEG)
            top = jnp.max(scores, axis=1, keepdims=True)
            probs = jnp.exp(scores - top)
            weight = jnp.sum(probs, axis=1, keepdims=True)
            out = dot(probs.astype(BF16), kvown_ref[0, 0:own_rows, PAIR:]) / weight
            local.append((out, top + jnp.log(weight)))
        local_out = merge_halves(local[0][0], local[1][0])
        local_lse = merge_halves(local[0][1], local[1][1])
        if not last:
            out_ref[...] = local_out
            lse_ref[...] = local_lse
    elif last:
        local_out, local_lse = out_in[...], lse_in[...]
    if last:
        shared_row = idc_ref[0:SHARED, :] == 0
        shared_out = merge_halves(total_a / weight_a, total_b / weight_b)
        shared_lse = merge_halves(peak_a + jnp.log(weight_a), peak_b + jnp.log(weight_b))
        mixed_ref[0:SHARED, :] = jnp.where(shared_row, shared_out, local_out[0:SHARED])
        mixed_ref[SHARED:, :] = local_out[SHARED:]
        full_lse_ref[0:SHARED, :] = jnp.where(shared_row, shared_lse, local_lse[0:SHARED])
        full_lse_ref[SHARED:, :] = local_lse[SHARED:]
    else:
        acc_ref[...] = merge_halves(total_a, total_b)
        peak_ref[...] = merge_halves(peak_a, peak_b)
        weight_ref[...] = merge_halves(weight_a, weight_b)


def attend(groups, first_low, w_project, project_bias, idc, idr, key_rows):
    own_rows, width = idc.shape[0], first_low.shape[1]
    wide = lambda rows: (sds((rows, width), F32), pl.BlockSpec((rows, PAIR), lambda h: (0, h)))
    deep = lambda rows, lane: (sds((PAIRS, rows, lane), BF16), pl.BlockSpec((1, rows, lane), lambda h: (h, 0, 0)))
    kvs, state = [], None
    for place, blocks in enumerate(groups):
        first, last = place == 0, place == len(groups) - 1
        keys = sum(b.shape[0] for b in blocks) * key_rows
        ins = [fixed(b) for b in blocks]
        ins += [lanes(w_project, PAIRS), lanes(w_project, 2 * PAIRS), lanes(project_bias, PAIRS)]
        if first:
            ins += [fixed(first_low), lanes(w_project), lanes(project_bias), fixed(idr)]
        else:
            ins += [lead(q)] + [lanes(s) for s in state]
            if last:
                ins += [lanes(local_out), lanes(local_lse)]
        ins += [fixed(idc)]
        outs = [deep(keys, 2 * PAIR)]
        if first:
            outs += [deep(own_rows, PAIR), deep(first_low.shape[0], 2 * PAIR)]
            if not last:
                outs += [wide(own_rows)] * 2
        outs += [wide(own_rows)] * 2 if last else [wide(SHARED)] * 3
        got = list(
            call(
                functools.partial(attend_kernel, len(blocks), key_rows, first, last),
                ins,
                outs,
                "attend",
                grid=(PAIRS,),
                cost=keys / 320.0 * 2,
            )
        )
        kvs.append(got.pop(0))
        if first:
            q, kvown = got.pop(0), got.pop(0)
            if not last:
                local_out, local_lse = got.pop(0), got.pop(0)
        state = got
    mixed, lse = state
    return kvs, kvown, q, mixed, lse


def erf(x):
    x = jnp.clip(x, -3.832506856900711, 3.832506856900711)
    s = x * x
    top = -2.72614225801306e-10
    for c in (2.77068142495902e-08, -2.10102402082508e-06, -5.69250639462346e-05, -7.34990630326855e-04, -2.95459980854025e-03, -1.60960333262415e-02):
        top = top * s + c
    low = -1.45660718464996e-05
    for c in (-2.13374055278905e-04, -1.68282697438203e-03, -7.37332916720468e-03, -1.42647390514189e-02):
        low = low * s + c
    return x * top / low


def middle_kernel(
    mixed, lse, stream, mlp_grad, act_grad, idc,
    w_output, merge_bias, gain, bias, w_up, up_bias, w_down, down_bias, w_head,
    predicted, act_ref, pre_ref, second_ref, mixed_low_ref, attn_low_ref, final_ref, attn_ref, grad_ref, unit_ref,
    stat_ref, up_sum, gain_sum, bias_sum, merge_sum,
):
    rows, width = mixed.shape
    hidden = w_up.shape[1]
    mixed_low = mixed[...].astype(BF16)
    mixed_low_ref[...] = mixed_low
    after = stream[...] + dot(mixed_low, w_output[...]) + merge_bias[...]
    unit_rows, scale = normalise(after)
    second = (unit_rows * gain[...] + bias[...]).astype(BF16)
    second_ref[...] = second
    out = after + down_bias[...]
    back = jnp.zeros((rows, width), F32)
    step = 768
    for start in range(0, hidden, step):
        part = slice(start, start + step)
        pre = dot(second, w_up[:, part]) + up_bias[:, part]
        cdf = 0.5 + 0.5 * erf(pre * 0.7071067811865476)
        act = (pre * cdf).astype(BF16)
        act_ref[:, part] = act
        slope = cdf + pre * (0.3989422804014327 * jnp.exp(-0.5 * pre * pre))
        grad = (act_grad[:, part] * slope).astype(BF16)
        pre_ref[:, part] = grad
        up_sum[:, part] = jnp.sum(grad.astype(F32), axis=0, keepdims=True)
        out += dot(act, w_down[part, :])
        back += dot_nt(grad, w_up[:, part])
    resid, gain_part, bias_part = norm_back(back, unit_rows, scale, gain[...])
    gain_sum[...] = gain_part
    bias_sum[...] = bias_part
    attn = mlp_grad[...] + resid
    attn_ref[...] = attn
    merge_sum[...] = jnp.sum(attn, axis=0, keepdims=True)
    attn_low = attn.astype(BF16)
    attn_low_ref[...] = attn_low
    grad = dot_nt(attn_low, w_output[...]).astype(BF16)
    grad_ref[...] = grad
    shared_row = idc[0:SHARED, :] == 0
    unit_ref[0:SHARED, :] = jnp.where(shared_row, grad[0:SHARED], jnp.zeros((SHARED, width), BF16))
    lane = lax.broadcasted_iota(jnp.int32, (MARKS, width), 1)
    head = lax.broadcasted_iota(jnp.int32, (MARKS, width), 0)
    ones = jnp.where(lane // HEAD_DIM == head, 1.0, 0.0)
    pick = jnp.where(lane == head * HEAD_DIM, 1.0, 0.0)
    delta = dot_nt(ones, grad.astype(F32) * mixed[...], lax.Precision.HIGHEST)
    turned = dot_nt(pick, lse[...], lax.Precision.HIGHEST)
    stat_ref[0] = turned
    stat_ref[1] = delta
    zeros = jnp.zeros((rows, 128), F32)
    ids = jnp.where(idc[...] == 0, 1.0, 0.0) + zeros
    row_ids = dot_nt(jnp.full((MARKS, 128), 1.0 / 128, F32), ids)
    shared_lane = row_ids[:, 0:SHARED] > 0.5
    sent = []
    for value, other in ((turned, -NEG), (delta, 0.0)):
        value = jnp.where(shared_lane, value[:, 0:SHARED], other)
        high = value.astype(BF16)
        sent += [high, (value - high.astype(F32)).astype(BF16)]
    unit_ref[SHARED:, :] = jnp.concatenate(sent, axis=1)
    final = out.astype(BF16)
    final_ref[...] = final
    predicted[...] = dot(final, w_head[...]).astype(BF16)


def query_kernel(n_blocks, n_kvs, key_rows, *refs):
    block_refs, kv_refs = refs[:n_blocks], refs[n_blocks : n_blocks + n_kvs]
    kvown_ref, q_ref, grad_ref, mixed_ref, lse_ref, wq_ref, bq_ref, idc_ref, idr_ref = refs[
        n_blocks + n_kvs : n_blocks + n_kvs + 9
    ]
    dq_ref, qall_ref = refs[-2:]
    own_rows = idc_ref.shape[0]
    flat = [(ref, i) for ref in block_refs for i in range(ref.shape[0])]
    base = 0
    for ref, index in flat:
        rows = (dot(ref[index, 0:SHARED, :], wq_ref[...]) + bq_ref[...]).astype(BF16)
        qall_ref[0, base : base + SHARED, :] = rows * BF16(SCALE)
        base += SHARED
    idc, idr = idc_ref[...], idr_ref[...]
    allowed = (idc == idr) & (idc != 0)
    shared_row = idc == 0
    q = q_ref[0]
    grad = grad_ref[...]
    product = grad.astype(F32) * mixed_ref[...]
    parts = []
    for kv_ref in kv_refs:
        count = kv_ref.shape[1] // key_rows
        parts += [(kv_ref, i, min(8, count - i)) for i in range(0, count, 8)]
    biases, used = [], 0
    for _, _, size in parts:
        biases += key_bias([flat[used : used + size]], key_rows)
        used += size
    outs = []
    for head in range(2):
        delta = jnp.sum(only_half(product, head), axis=1, keepdims=True)
        lse = lse_ref[:, head * HEAD_DIM : head * HEAD_DIM + 1]
        qm = only_half(q, head)
        gm = only_half(grad, head)
        total = None
        for (kv_ref, start, size), bias in zip(parts, biases):
            span = slice(start * key_rows, (start + size) * key_rows)
            keys = kv_ref[0, span, 0:PAIR]
            values = kv_ref[0, span, PAIR:]
            probs = jnp.exp(dot_nt(qm[0:SHARED], keys) + bias - lse[0:SHARED])
            dp = dot_nt(gm[0:SHARED], values)
            ds = (probs * (dp - delta[0:SHARED])).astype(BF16)
            part = dot(ds, keys)
            total = part if total is None else total + part
        keys, values = kvown_ref[0, 0:own_rows, 0:PAIR], kvown_ref[0, 0:own_rows, PAIR:]
        probs = jnp.exp(jnp.where(allowed, dot_nt(qm, keys) - lse, NEG))
        ds = (probs * (dot_nt(gm, values) - delta)).astype(BF16)
        local = dot(ds, keys)
        outs.append(
            jnp.concatenate([jnp.where(shared_row[0:SHARED], total, local[0:SHARED]), local[SHARED:]], axis=0)
        )
    dq_ref[...] = (merge_halves(*outs) * SCALE).astype(BF16)


def query_back(groups, kvs, kvown, q, mixed_grad, mixed, lse, w_project, project_bias, idc, idr, key_rows, first, pairs, after):
    own_rows = idc.shape[0]
    blocks = [b for group in groups for b in group]
    count = sum(b.shape[0] for b in blocks)
    ins = [fixed(b) for b in blocks] + [lead(kv, first) for kv in kvs] + [lead(kvown, first), lead(q, first)]
    ins += [lanes(x, first) for x in (mixed_grad, mixed, lse, w_project, project_bias)]
    ins += [fixed(idc), fixed(idr)]
    outs = [
        (sds((own_rows, pairs * PAIR), BF16), pl.BlockSpec((own_rows, PAIR), lambda h: (0, h))),
        (sds((pairs, count * SHARED, PAIR), BF16), pl.BlockSpec((1, count * SHARED, PAIR), lambda h: (h, 0, 0))),
    ]
    kernel = functools.partial(query_kernel, len(blocks), len(kvs), key_rows)
    return call(kernel, ins, outs, "query_back", grid=(pairs,), cost=4.0 * pairs, after=after)


def key_kernel(n_blocks, first, *refs):
    grad_refs, stat_refs = refs[:n_blocks], refs[n_blocks : 2 * n_blocks]
    kvown_ref, qall_ref, q_ref, grad_ref, own_stat_ref, idc_ref, idr_ref, live_ref = refs[2 * n_blocks : 2 * n_blocks + 8]
    dk_ref, dv_ref, grads_ref, stats_ref = refs[2 * n_blocks + 8 :]
    own_rows = idc_ref.shape[0]
    rim = kvown_ref.shape[1] - own_rows

    @pl.when(pl.program_id(0) == 0)
    def _():
        base = 0
        rows = [(ref, i) for ref in stat_refs for i in range(ref.shape[0])]
        for begin in range(0, len(rows), 2):
            sums = []
            for ref, i in rows[begin : begin + 2]:
                stat = ref[i].astype(F32)
                sums.append(
                    (
                        stat[:, 0:SHARED] + stat[:, SHARED : 2 * SHARED],
                        stat[:, 2 * SHARED : 3 * SHARED] + stat[:, 3 * SHARED :],
                    )
                )
            for kind in range(2):
                stats_ref[kind, :, base : base + 2 * SHARED] = jnp.concatenate([s[kind] for s in sums], axis=1)
            base += 2 * SHARED

    base = 0
    for ref in grad_refs:
        for i in range(ref.shape[0]):
            grads_ref[base : base + SHARED, :] = ref[i]
            base += SHARED
    idc, idr = idc_ref[...], idr_ref[...]
    allowed = (idc == idr) & (idc != 0)
    shared_row = idc == 0
    live = live_ref[0:1, 0:1] > 0.5
    kv = kvown_ref[0]
    k_all, v_all = kv[:, 0:PAIR], kv[:, PAIR:]
    k_sh = jnp.concatenate([k_all[0:SHARED], k_all[own_rows:]], axis=0)
    v_sh = jnp.concatenate([v_all[0:SHARED], v_all[own_rows:]], axis=0)
    q, grad = q_ref[0], grad_ref[...]
    dks, dvs = [], []
    chunk = min(base, 1536)
    for head in range(2):
        row = pl.ds(2 * (first + pl.program_id(0)) + head, 1)
        km, vm = only_half(k_sh, head), only_half(v_sh, head)
        dk = dv = None
        for start in range(0, base, chunk):
            q_all = qall_ref[0, start : start + chunk, :]
            g_all = grads_ref[start : start + chunk, :]
            lse = stats_ref[0, row, start : start + chunk]
            delta = stats_ref[1, row, start : start + chunk]
            probs = jnp.exp(dot_nt(km, q_all) - lse)
            part_v = dot(probs.astype(BF16), g_all)
            ds = (probs * (dot_nt(vm, g_all) - delta)).astype(BF16)
            part_k = dot(ds, q_all)
            dk = part_k if dk is None else dk + part_k
            dv = part_v if dv is None else dv + part_v
        lse = own_stat_ref[0, row, :]
        delta = own_stat_ref[1, row, :]
        probs = jnp.exp(jnp.where(allowed, dot_nt(only_half(k_all[0:own_rows], head), q) - lse, NEG))
        local_v = dot(probs.astype(BF16), grad)
        ds = (probs * (dot_nt(only_half(v_all[0:own_rows], head), grad) - delta)).astype(BF16)
        local_k = dot(ds, q)

        def rows(shared, local):
            return jnp.concatenate(
                [
                    jnp.where(shared_row[0:SHARED], shared[0:SHARED], local[0:SHARED]),
                    local[SHARED:],
                    jnp.where(live, shared[SHARED : SHARED + rim], 0.0),
                ],
                axis=0,
            )

        dks.append(rows(dk, local_k))
        dvs.append(rows(dv, local_v))
    dk_ref[...] = merge_halves(*dks).astype(BF16)
    dv_ref[...] = merge_halves(*dvs).astype(BF16)


def key_back(groups, kvown, qall, q, mixed_grad, own_stats, idc, idr, live, first, pairs, after):
    joined_rows, width = kvown.shape[1], mixed_grad.shape[1]
    grads = [g for group in groups for g in group]
    ins = [(g, pl.BlockSpec((g.shape[0], SHARED, PAIR), lambda h: (0, 0, first + h))) for g in grads]
    ins += [(g, pl.BlockSpec((g.shape[0], MARKS, width), lambda h: (0, SHARED // MARKS, 0))) for g in grads]
    ins += [lead(kvown, first), lead(qall), lead(q, first), lanes(mixed_grad, first)]
    ins += [fixed(own_stats), fixed(idc), fixed(idr), fixed(live)]
    out = (sds((joined_rows, pairs * PAIR), BF16), pl.BlockSpec((joined_rows, PAIR), lambda h: (0, h)))
    scratch = [pltpu.VMEM((qall.shape[1], PAIR), BF16), pltpu.VMEM((2, MARKS, qall.shape[1]), F32)]
    kernel = functools.partial(key_kernel, len(grads), first)
    return call(kernel, ins, [out, out], "key_back", grid=(pairs,), scratch=scratch, cost=3.0 * pairs, after=after)


def input_kernel(dq, dk, dv, weight, stream, arrived, gain, attn_grad, rim_ref, rows_ref, joint_ref, vec_ref):
    own, width = dq.shape
    dq, dk, dv = dq[...], dk[...], dv[...]
    wq, wk, wv = weight[:, 0:width], weight[:, width : 2 * width], weight[:, 2 * width :]
    rim_grad = dot_nt(dk[own:], wk) + dot_nt(dv[own:], wv)
    rim_rows, rim_scale = normalise(arrived[...].astype(F32))
    rim_back, rim_gain, rim_bias = norm_back(rim_grad, rim_rows, rim_scale, gain[...])
    rim_ref[...] = rim_back.astype(BF16)
    own_grad = dot_nt(dq, wq) + dot_nt(dk[:own], wk) + dot_nt(dv[:own], wv)
    own_rows, own_scale = normalise(stream[...])
    own_back, own_gain, own_bias = norm_back(own_grad, own_rows, own_scale, gain[...])
    rows_ref[...] = own_back + attn_grad[...]
    joint_ref[0:own, 0:width] = dq
    joint_ref[own:, 0:width] = jnp.zeros((dk.shape[0] - own, width), BF16)
    joint_ref[:, width : 2 * width] = dk
    joint_ref[:, 2 * width :] = dv
    vec_ref[0:1, :] = own_gain + rim_gain
    vec_ref[1:2, :] = own_bias + rim_bias
    vec_ref[2:3, :] = jnp.sum(dq.astype(F32), axis=0, keepdims=True)
    vec_ref[3:4, :] = jnp.sum(dv.astype(F32), axis=0, keepdims=True)


def pixel_kernel(rows, returned, halo, weight, low_ref, grad_ref):
    place = lax.broadcasted_iota(jnp.int32, (rows.shape[0], halo.shape[1]), 0)
    spread = jnp.where(place == halo[...], 1.0, 0.0).astype(BF16)
    low = (rows[...] + dot(spread, returned[...])).astype(BF16)
    low_ref[...] = low
    grad_ref[...] = dot_nt(low, weight[...]).astype(BF16)


def product_blocks(left, right, core_half, n):
    half = right.shape[1] // 2
    x = left[...]
    for j in range(half // LANES):
        columns = pl.ds(pl.multiple_of(core_half * half + j * LANES, 128), LANES)
        out = dot_tn(x, right[:, columns])
        yield out.reshape(n, out.shape[0] // n, LANES)


def away_kernel(n, n_pairs, *refs):
    pairs, outs = refs[: 2 * n_pairs], refs[2 * n_pairs :]
    other = 1 - lax.axis_index("gx") % 2
    (out,) = outs
    row = 0
    for p in range(n_pairs):
        for block in product_blocks(pairs[2 * p], pairs[2 * p + 1], other, n):
            out[:, row : row + block.shape[1], :] = block.astype(BF16)
            row += block.shape[1]


def home_kernel(n, n_pairs, x_first, n_small, *refs):
    pairs = refs[: 2 * n_pairs]
    arrived = refs[2 * n_pairs]
    small = refs[2 * n_pairs + 1 : 2 * n_pairs + 1 + n_small]
    send, keep = refs[2 * n_pairs + 1 + n_small :]
    core = lax.axis_index("gx") % 2
    bit = lax.axis_index("gx") // 2 if x_first else lax.axis_index("gy") % 2
    low = bit == 0
    row = half_row = 0

    def put(first, second, start, rows):
        if x_first:
            span = slice(start, start + rows)
            send[:, span, :] = jnp.where(low, second, first)
            keep[:, span, :] = jnp.where(low, first, second)
        else:
            for half, value in ((0, first), (1, second)):
                value = value.reshape(n // 2, 2, rows, LANES)
                send[:, half, start : start + rows, :] = jnp.where(low, value[:, 1], value[:, 0])
                keep[:, half, start : start + rows, :] = jnp.where(low, value[:, 0], value[:, 1])

    for p in range(n_pairs):
        for block in product_blocks(pairs[2 * p], pairs[2 * p + 1], core, n):
            r = block.shape[1]
            block = (block + arrived[:, row : row + r, :].astype(F32)).astype(BF16)
            put(block[:, : r // 2], block[:, r // 2 :], half_row, r // 2)
            row += r
            half_row += r // 2
    for ref in small:
        put(ref[...], jnp.zeros(ref.shape, BF16), half_row, ref.shape[1])
        half_row += ref.shape[1]


def away(pairs, n, name):
    arrays = [x for pair in pairs for x in pair]
    rows = sum(b.shape[1] // 2 // LANES * a.shape[1] // n for a, b in pairs)
    outs = [(sds((n, rows, LANES), BF16), VMEM)]
    return call(functools.partial(away_kernel, n, len(pairs)), plain(*arrays), outs, name, cost=3.0)[0]


def home(pairs, n, arrived, x_first, name, small=(), after=()):
    arrays = [x for pair in pairs for x in pair] + [arrived] + list(small)
    rows = arrived.shape[1] // 2 + sum(s.shape[1] for s in small)
    shape = (n, rows, LANES) if x_first else (n // 2, 2, rows, LANES)
    outs = [(sds(shape, BF16), VMEM)] * 2
    kernel = functools.partial(home_kernel, n, len(pairs), x_first, len(small))
    return call(kernel, plain(*arrays), outs, name, cost=3.0, after=after)


def next_step(keep, arrived, axis, bit, dim):
    mine = bit_of(axis, bit)
    pick = lambda x, i: lax.dynamic_index_in_dim(x, i, dim, keepdims=False)
    return pick(keep, 1 - mine) + pick(arrived, 1 - mine), pick(keep, mine) + pick(arrived, mine)


def steps_of(x_first):
    second = ("gy", 1, 2) if x_first else ("gx", 2, 2)
    return [second, ("gy", 2, 1), ("gy", 4, 0)]


def shards(
    pixels,
    frame_index,
    patch_cell,
    tile_id,
    halo_index,
    w_patch,
    first_gain,
    first_bias,
    w_project,
    project_bias,
    w_output,
    merge_bias,
    second_gain,
    second_bias,
    w_up,
    up_bias,
    w_down,
    down_bias,
    w_head,
    cotangent,
):
    n_gx, n_gy = lax.axis_size("gx"), lax.axis_size("gy")
    own, rim = pixels.shape[0], halo_index.shape[0]
    width, hidden, depth = w_output.shape[0], w_up.shape[1], pixels.shape[1]
    key_rows = SHARED + rim
    idc, idr = tile_id.reshape(own, 1), tile_id.reshape(1, own)
    live = jnp.broadcast_to(jnp.where(lax.axis_index("gx") > 0, 1.0, 0.0).astype(F32), (8, 128))
    halo = halo_index.reshape(1, rim)
    row = lambda v: v.reshape(1, -1)
    mat = lambda rows, columns, dtype: (sds((rows, columns), dtype), VMEM)

    high, low = position_table(width)
    stream, outgoing, own_low = call(
        embed_kernel,
        plain(
            pixels, w_patch, row(frame_index), patch_cell, halo, high, low, row(first_gain), row(first_bias)
        ),
        [mat(own, width, F32), mat(rim, width, BF16), mat(own, width, BF16)],
        "embed",
    )
    arrived = shifted(outgoing, "gx", 1)
    unit, first_low = call(
        unit_kernel,
        plain(own_low, arrived, row(first_gain), row(first_bias), idr, live),
        [mat(key_rows + MARKS, width, BF16), mat(own + rim, width, BF16)],
        "unit",
        cost=1.0,
    )
    groups = gather_column(unit)
    shift = row(project_bias)
    kvs, kvown, q, mixed, lse = attend(groups, first_low, w_project, shift, idc, idr, key_rows)

    mlp_grad = dot_nt(cotangent, w_head)
    down_bias_grad = jnp.sum(mlp_grad, axis=0)
    mlp_low = mlp_grad.astype(BF16)
    act_grad = dot_nt(mlp_low, w_down)
    (
        predicted, act_low, pre_grad, second_low, mixed_low, attn_low, final_low, attn_grad, mixed_grad, grad_unit,
        own_stats, up_sum, second_gain_sum, second_bias_sum, merge_sum,
    ) = call(
        middle_kernel,
        plain(
            mixed, lse, stream, mlp_grad, act_grad, idc, w_output, row(merge_bias), row(second_gain),
            row(second_bias), w_up, row(up_bias), w_down, row(down_bias), w_head,
        ),
        [mat(own, depth, BF16), mat(own, hidden, BF16), mat(own, hidden, BF16)]
        + [mat(own, width, BF16)] * 4
        + [mat(own, width, F32), mat(own, width, BF16), mat(SHARED + MARKS, width, BF16)]
        + [(sds((2, MARKS, own), F32), VMEM), mat(1, hidden, F32)]
        + [mat(1, width, F32)] * 3,
        "middle",
        cost=15.0,
    )
    special = n_gx == 4 and n_gy == 8
    head_pair, down_pair = (final_low, cotangent), (act_low, mlp_low)
    up_pair, output_pair = (second_low, pre_grad), (mixed_low, attn_low)
    grads = gather_column(grad_unit)
    sums, gone = {}, {}
    early = {"a": ([head_pair, down_pair], True), "b": ([up_pair, output_pair], False)}
    after = ()
    if special:
        shares = {k: away(pairs, n_gy, "away") for k, (pairs, _) in early.items()}
        gone = {k: swap(share, "gx", 1) for k, share in shares.items()}
        after = tuple(shares.values())
    q_parts, k_parts = [], []
    for place, first in enumerate((0, 2, 4)):
        q_parts.append(
            query_back(groups, kvs, kvown, q, mixed_grad, mixed, lse, w_project, shift, idc, idr, key_rows, first, 2, after)
        )
        after = (q_parts[-1][0],)
        if special and place == 0:
            for k, (pairs, x_first) in early.items():
                send, keep = home(pairs, n_gy, gone[k], x_first, "home", after=after)
                axis, bit = ("gx", 2) if x_first else ("gy", 1)
                sums[k] = (keep, swap(send, axis, bit))
                after += (send,)
    for place in range(3):
        k_parts.append(
            key_back(grads, kvown, q_parts[place][1], q, mixed_grad, own_stats, idc, idr, live, 2 * place, 2, after)
        )
        after = (k_parts[-1][0],)
    dq = jnp.concatenate([p[0] for p in q_parts], axis=1)
    dk = jnp.concatenate([p[0] for p in k_parts], axis=1)
    dv = jnp.concatenate([p[1] for p in k_parts], axis=1)
    rim_grad, partial, joint_grad, first_sums = call(
        input_kernel,
        plain(dq, dk, dv, w_project, stream, arrived, row(first_gain), attn_grad),
        [mat(rim, width, BF16), mat(own, width, F32), mat(own + rim, 3 * width, BF16), mat(8, width, F32)],
        "input",
        cost=6.0,
    )
    returned = shifted(rim_grad, "gx", -1)
    project_pair = (first_low, joint_grad)
    if special:
        gone["c"] = swap(away([project_pair], n_gy, "away"), "gx", 1)
    embed_low, pixel_grad = call(
        pixel_kernel,
        plain(partial, returned, halo, w_patch),
        [mat(own, width, BF16), mat(own, depth, BF16)],
        "pixel",
        cost=3.0,
    )
    patch_pair = (pixels, embed_low)

    vectors = [
        first_sums[0],
        first_sums[1],
        first_sums[2:4].reshape(-1),
        merge_sum[0],
        second_gain_sum[0],
        second_bias_sum[0],
        up_sum[0],
        down_bias_grad,
    ]
    sizes = [v.shape[0] // n_gy for v in vectors]
    flat = jnp.concatenate([v.reshape(n_gy, -1) for v in vectors], axis=1).astype(BF16)
    if special:
        core, x_bit = bit_of("gx", 1), bit_of("gx", 2)
        half = sum(sizes) // 2
        flat = flat.reshape(n_gy, 2, half)
        mine = lax.dynamic_index_in_dim(flat, core, 1, keepdims=False)
        other = lax.dynamic_index_in_dim(flat, 1 - core, 1, keepdims=False)
        small = mine + swap(other, "gx", 1)
        small = jnp.pad(small, ((0, 0), (0, MARKS * LANES - half))).reshape(n_gy, MARKS, LANES)
        gone["d"] = swap(away([patch_pair], n_gy, "away"), "gx", 1)
        send, keep = home([project_pair], n_gy, gone["c"], True, "home")
        sums["c"] = (keep, swap(send, "gx", 2))
        send, keep = home([patch_pair], n_gy, gone["d"], False, "home", small=[small])
        sums["d"] = (keep, swap(send, "gy", 1))
        orders = {"a": True, "b": False, "c": True, "d": False}
        for k, x_first in orders.items():
            keep, got = sums[k]
            lead_shape = (2, 2, 2) if x_first else (2, 2)
            tail_shape = keep.shape[1:] if x_first else keep.shape[1:]
            keep, got = keep.reshape(lead_shape + tail_shape), got.reshape(lead_shape + tail_shape)
            for axis, bit, dim in steps_of(x_first):
                send, keep = next_step(keep, got, axis, bit, dim)
                got = swap(send, axis, bit)
            part = keep + got
            over = swap(part, "gx", 2)
            both = jnp.stack([jnp.where(x_bit == 0, part, over), jnp.where(x_bit == 0, over, part)])
            across = swap(both, "gx", 1)
            sums[k] = [jnp.where(core == 0, both, across), jnp.where(core == 0, across, both)]

        def cut(key, pairs):
            outs, start = [], 0
            for a, b in pairs:
                r, blocks = a.shape[1] // n_gy, b.shape[1] // 2 // LANES
                halves = []
                for side in sums[key]:
                    piece = side[:, start : start + blocks * r // 2].reshape(2, blocks, r // 2, LANES)
                    halves.append(piece.transpose(0, 2, 1, 3).reshape(r, blocks * LANES))
                start += blocks * r // 2
                outs.append(jnp.concatenate(halves, axis=1).astype(F32))
            return outs, start

        (head_grad, down_grad), _ = cut("a", early["a"][0])
        (up_grad, output_grad), _ = cut("b", early["b"][0])
        (project_grad,), _ = cut("c", [project_pair])
        (patch_grad,), start = cut("d", [patch_pair])
        tail = [side[0, start:].reshape(-1)[:half] for side in sums["d"]]
        tail = jnp.concatenate(tail).astype(F32)
    else:

        def total(x):
            part = lax.psum_scatter(x.astype(BF16), "gy", scatter_dimension=0, tiled=True)
            return lax.psum(part, "gx").astype(F32)

        pairs = [head_pair, down_pair, up_pair, output_pair, project_pair, patch_pair]
        head_grad, down_grad, up_grad, output_grad, project_grad, patch_grad = [total(dot_tn(a, b)) for a, b in pairs]
        tail = total(flat).reshape(-1)
    starts = [sum(sizes[:i]) for i in range(len(sizes))]
    small_outs = [tail[s : s + z] for s, z in zip(starts, sizes)]
    return (
        predicted,
        pixel_grad,
        patch_grad,
        small_outs[0],
        small_outs[1],
        project_grad,
        small_outs[2],
        output_grad,
        small_outs[3],
        small_outs[4],
        small_outs[5],
        up_grad,
        small_outs[6],
        down_grad,
        small_outs[7],
        head_grad,
    )


def solution(mesh):
    tokens = P(("gx", "gy"))
    rows = P(("gx", "gy"), None)
    in_specs = (rows, tokens, P(None, ("gx", "gy")), tokens, tokens) + (P(),) * 14 + (rows,)
    matrix, vector = P("gy", None), P("gy")
    out_specs = (
        rows,
        rows,
        matrix,
        vector,
        vector,
        matrix,
        vector,
        matrix,
        vector,
        vector,
        vector,
        matrix,
        vector,
        matrix,
        vector,
        matrix,
    )
    return jax.shard_map(shards, mesh=mesh, in_specs=in_specs, out_specs=out_specs, check_vma=False)
```

```python
import functools

import jax
import jax.numpy as jnp
import numpy as np
from jax import lax
from jax.experimental import pallas as pl
from jax.experimental.pallas import tpu as pltpu
from jax.sharding import PartitionSpec as P

HEADS = 12
HEAD_DIM = 64
PAIR = 2 * HEAD_DIM
PAIRS = HEADS // 2
SCALE = HEAD_DIM**-0.5
LANES = 384
SHARED = 192
MARKS = 16
GRID_SIDE = 56
EPS = 1e-06
NEG = -1e30
F32 = jnp.float32
BF16 = jnp.bfloat16
VMEM_LIMIT = 56
CFG = dict(qp=(3, 3), kp=(3, 3), home=1, gate=0, b="yx", c="x", d="z", ab2=None, ab3=None, merged=False, direct=False, sc=False, limit=56, limits={}, chain=False, away_first=True, early=False, join=False)
PACE = 1.0


def dot(a, b):
    return jnp.dot(a, b, preferred_element_type=F32)


def dot_nt(a, b, precision=None):
    return lax.dot_general(a, b, (((1,), (1,)), ((), ())), preferred_element_type=F32, precision=precision)


def dot_tn(a, b):
    return lax.dot_general(a, b, (((0,), (0,)), ((), ())), preferred_element_type=F32)


def sds(shape, dtype):
    return jax.ShapeDtypeStruct(tuple(shape), dtype)


def shifted(x, axis, by):
    length = lax.axis_size(axis)
    pairs = [(i, i + by) for i in range(length) if 0 <= i + by < length]
    return lax.ppermute(x, axis, pairs)


def swap(x, axis, bit):
    length = lax.axis_size(axis)
    return lax.ppermute(x, axis, [(i, i ^ bit) for i in range(length)])


def swap_chip(x, dx, dz, dy):
    n_gx, n_gy = lax.axis_size("gx"), lax.axis_size("gy")
    flip = 2 * dx * n_gy + 2 * dz + dy
    return lax.ppermute(x, ("gx", "gy"), [(i, i ^ flip) for i in range(n_gx * n_gy)])


class ColumnGather:
    def __init__(self, unit):
        self.unit = unit
        self.direct = lax.axis_size("gy") == 8
        if not self.direct:
            self.groups = [[lax.all_gather(unit, "gy", axis=0, tiled=False)]]
            return
        self.y0 = self.across(unit)
        self.near = self.along(unit, [(0, 1), (1, 0), (2, 3), (3, 2)])
        self.mid = self.along(unit, [(1, 2), (2, 1)])

    def along(self, x, hops):
        return lax.ppermute(x, "gy", [(2 * a + y, 2 * b + y) for a, b in hops for y in (0, 1)])

    def across(self, x):
        return swap(x, "gy", 1)

    def second(self):
        self.y1 = self.across(self.near)
        self.far_end = self.along(self.mid, [(1, 0), (2, 3)])
        self.far_mid = self.along(self.near, [(1, 2), (2, 1)])

    def third(self, after):
        self.last_end = self.along(self.far_mid, [(1, 0), (2, 3)])
        self.far = choose(self.far_end, self.far_mid, after)
        self.y2 = self.across(self.far)

    def fourth(self, after):
        self.last = choose(self.last_end, self.mid, after)
        self.y3 = self.across(self.last)
        self.group()

    def group(self):
        groups = [[self.unit, self.near, self.y0], [self.y1, self.far], [self.last, self.y2, self.y3]]
        if CFG["early"]:
            groups = [[self.unit, self.near], [self.y0, self.y1, self.far], [self.last, self.y2, self.y3]]
        self.groups = [[part[None] for part in group] for group in groups]


class FreeGather(ColumnGather):
    def __init__(self, unit):
        super().__init__(unit)
        if not self.direct:
            return
        self.second()
        place = lax.axis_index("gy") // 2
        at_end = (place == 0) | (place == 3)
        self.far = jnp.where(at_end, self.far_end, self.far_mid)
        self.y2 = self.across(self.far)
        self.last_end = self.along(self.far_mid, [(1, 0), (2, 3)])
        self.last = jnp.where(at_end, self.last_end, self.mid)
        self.y3 = self.across(self.last)
        self.group()


class DirectGather:
    def __init__(self, unit):
        self.unit = unit
        if lax.axis_size("gy") != 8:
            self.groups = [[lax.all_gather(unit, "gy", axis=0, tiled=False)]]
            return
        self.near, self.y0 = swap_chip(unit, 0, 1, 0), swap_chip(unit, 0, 0, 1)
        self.mid = self.far_end = self.far_mid = self.last_end = self.near
        self.far, self.last = swap_chip(unit, 0, 2, 0), swap_chip(unit, 0, 3, 0)

        self.second()

    def second(self):
        y1, y2, y3 = (swap_chip(x, 0, 0, 1) for x in (self.near, self.far, self.last))
        self.y1, self.y2, self.y3 = y1, y2, y3
        groups = [[self.unit, self.near, self.y0], [y1, self.far], [self.last, y2, y3]]
        self.groups = [[part[None] for part in group] for group in groups]


def choose(at_end, inside, after):
    def kernel(a, b, out):
        place = lax.axis_index("gy") // 2
        out[...] = jnp.where((place == 0) | (place == 3), a[...], b[...])

    return call(kernel, plain(at_end, inside), [(sds(inside.shape, inside.dtype), VMEM)], "choose", cost=2.3, after=after)[0]


def bit_of(axis, bit):
    return (lax.axis_index(axis) // bit) % 2


def call(kernel, ins, outs, name, grid=None, scratch=(), cost=4.0, after=()):
    limit = CFG["limits"].get(name, CFG["limit"]) if lax.axis_size("gy") == 8 else VMEM_LIMIT
    specs = [spec for _, spec in ins] + [pl.BlockSpec(memory_space=pl.ANY)] * len(after)
    count = len(ins)

    def body(*refs):
        kernel(*refs[:count], *refs[count + len(after) :])

    return pl.pallas_call(
        body,
        grid=grid or (),
        in_specs=specs,
        out_specs=tuple(spec for _, spec in outs),
        out_shape=tuple(shape for shape, _ in outs),
        scratch_shapes=list(scratch),
        compiler_params=pltpu.CompilerParams(vmem_limit_bytes=limit * 2**20),
        cost_estimate=pl.CostEstimate(flops=int(cost * 1e8), bytes_accessed=int(cost * 3e5), transcendentals=0),
        name=name,
    )(*[array for array, _ in ins], *after)


VMEM = pl.BlockSpec(memory_space=pltpu.VMEM)


def plain(*arrays):
    return [(a, VMEM) for a in arrays]


def fixed(array):
    zeros = (0,) * len(array.shape)
    return (array, pl.BlockSpec(tuple(array.shape), lambda h: zeros, pipeline_mode=pl.Buffered(1)))


def lead(array, first=0):
    zeros = (0,) * (len(array.shape) - 1)
    return (array, pl.BlockSpec((1,) + tuple(array.shape[1:]), lambda h: (first + h,) + zeros))


def lanes(array, first=0, width=PAIR):
    return (array, pl.BlockSpec((array.shape[0], width), lambda h: (0, first + h)))


def half_mask(rows):
    return lax.broadcasted_iota(jnp.int32, (rows, PAIR), 1) < HEAD_DIM


def only_half(x, head):
    low_half = half_mask(x.shape[0])
    zero = jnp.zeros_like(x)
    return jnp.where(low_half, x, zero) if head == 0 else jnp.where(low_half, zero, x)


def merge_halves(first, second):
    rows = first.shape[0]
    return jnp.where(half_mask(rows), jnp.broadcast_to(first, (rows, PAIR)), jnp.broadcast_to(second, (rows, PAIR)))


def normalise(x):
    centered = x - jnp.mean(x, axis=1, keepdims=True)
    scale = lax.rsqrt(jnp.mean(centered * centered, axis=1, keepdims=True) + EPS)
    return centered * scale, scale


def norm_back(grad, unit_rows, scale, gain):
    g = grad * gain
    inner = jnp.mean(g * unit_rows, axis=1, keepdims=True)
    rows = scale * (g - jnp.mean(g, axis=1, keepdims=True) - unit_rows * inner)
    return rows, jnp.sum(grad * unit_rows, axis=0, keepdims=True), jnp.sum(grad, axis=0, keepdims=True)


def stack_heads(x):
    low_half = half_mask(x.shape[0])
    zero = jnp.zeros_like(x)
    return jnp.concatenate([jnp.where(low_half, x, zero), jnp.where(low_half, zero, x)], axis=0)


def unstack_heads(x):
    rows = x.shape[0] // 2
    return merge_halves(x[:rows], x[rows:])


def twice(x):
    return jnp.concatenate([x, x], axis=0)


def pair_lanes(ref, pair):
    return ref[:, pl.ds(pl.multiple_of(pair * PAIR, PAIR), PAIR)]


def group_blocks(block_refs):
    flat = [(ref, i) for ref in block_refs for i in range(ref.shape[0])]
    return [flat[i : i + 8] for i in range(0, len(flat), 8)]


def key_marks(ref, index, key_rows):
    marks = ref[index, key_rows : key_rows + MARKS, 0:256].astype(F32)
    return marks[0:1, 0:1], marks[0:1, 128:129]


def key_bias(group, key_rows):
    width = len(group) * key_rows
    lane = lax.broadcasted_iota(jnp.int32, (1, width), 1).astype(F32)
    bias = jnp.full((1, width), NEG, F32)
    for place, (ref, index) in enumerate(group):
        count, live = key_marks(ref, index, key_rows)
        local = lane - float(place * key_rows)
        good = (local >= 0.0) & (local < count)
        rim = (local >= float(SHARED)) & (local < float(key_rows)) & (live > 0.5)
        bias = jnp.where(good | rim, 0.0, bias)
    return bias


def key_bias_column(group, key_rows):
    parts = []
    for ref, index in group:
        count, live = key_marks(ref, index, key_rows)
        place = lax.broadcasted_iota(jnp.int32, (key_rows, 1), 0).astype(F32)
        good = (place < count) | ((place >= float(SHARED)) & (live > 0.5))
        parts.append(jnp.where(good, 0.0, NEG))
    return jnp.concatenate(parts, axis=0)


def position_table(width):
    unit_width = width // 16
    table = np.zeros((128, width), np.float32)
    bands = [(0, 8, 0, 4 * unit_width), (8, GRID_SIDE, 4 * unit_width, 6 * unit_width)]
    bands.append((64, GRID_SIDE, 10 * unit_width, 6 * unit_width))
    for row, count, lane, band in bands:
        half = band // 2
        power = np.arange(half, dtype=np.float32) / np.float32(half)
        omegas = np.float32(1.0) / np.power(np.float32(10000.0), power)
        angles = (np.arange(count, dtype=np.float32)[:, None] * omegas[None]).astype(np.float64)
        table[row : row + count, lane : lane + half] = np.sin(angles)
        table[row : row + count, lane + half : lane + band] = np.cos(angles)
    high = table.astype(jnp.bfloat16)
    low = (table - high.astype(np.float32)).astype(jnp.bfloat16)
    return jnp.asarray(high), jnp.asarray(low)


def embed_kernel(pix, weight, frame, cell, halo, high, low, gain, bias, stream_ref, rim_ref, low_ref):
    rows = pix.shape[0]
    code = lax.broadcasted_iota(jnp.int32, (128, rows), 0)
    first, second = cell[0:1, :], cell[1:2, :]
    hot = (code == frame[...]) | (code == first + 8) | (code == second + 64)
    hot = jnp.where(hot, 1.0, 0.0).astype(BF16)
    stream = dot(pix[...], weight[...]) + (dot_tn(hot, high[...]) + dot_tn(hot, low[...]))
    stream_ref[...] = stream
    place = lax.broadcasted_iota(jnp.int32, (rows, halo.shape[1]), 0)
    pick = jnp.where(place == halo[...], 1.0, 0.0).astype(BF16)
    rim_ref[...] = dot_tn(pick, stream.astype(BF16)).astype(BF16)
    unit_rows, _ = normalise(stream)
    low_ref[...] = (unit_rows * gain[...] + bias[...]).astype(BF16)


def unit_kernel(own, arrived, gain, bias, ids, live, unit_ref, joined_ref):
    rows, width = own.shape
    rim = arrived.shape[0]
    unit_rows, _ = normalise(arrived[...].astype(F32))
    rim_low = (unit_rows * gain[...] + bias[...]).astype(BF16)
    joined_ref[0:rows, :] = own[...]
    joined_ref[rows : rows + rim, :] = rim_low
    unit_ref[0:SHARED, :] = own[0:SHARED, :]
    unit_ref[SHARED : SHARED + rim, :] = rim_low
    count = jnp.sum(jnp.where(ids[...] == 0, 1.0, 0.0), axis=1, keepdims=True)
    lane = lax.broadcasted_iota(jnp.int32, (MARKS, width), 1)
    unit_ref[SHARED + rim :, :] = jnp.where(lane < 128, count, live[0:1, 0:1]).astype(BF16)


def attend_kernel(n_blocks, key_rows, first, last, *refs):
    refs = list(refs)

    def take(n):
        out = refs[:n]
        del refs[:n]
        return out

    block_refs = take(n_blocks)
    wk_ref, wv_ref, bias_ref = take(3)
    if first:
        own_ref, wq_ref, idr_ref = take(3)
    else:
        q_ref, acc_in, stat_in = take(3)
        if last:
            out_in, lse_in = take(2)
    idc_ref = take(1)[0]
    kv_ref = take(1)[0]
    if first:
        q_ref, kvown_ref = take(2)
        if not last:
            out_ref, lse_ref = take(2)
    if last:
        mixed_ref, full_lse_ref = take(2)
    else:
        acc_ref, stat_ref = take(2)
    pair = pl.program_id(0)
    own_rows = idc_ref.shape[0]
    groups = group_blocks(block_refs)
    biases = [key_bias_column(group, key_rows) for group in groups]
    here = pl.ds(pl.multiple_of(pair * PAIR, PAIR), PAIR)
    wkv = jnp.concatenate([wk_ref[...], wv_ref[...]], axis=1)
    shift = pair_lanes(bias_ref, PAIRS + pair)
    shift = jnp.concatenate([jnp.zeros_like(shift), shift], axis=1)
    base = 0
    for group in groups:
        for ref, index in group:
            kv_ref[0, base : base + key_rows, :] = (dot(ref[index, 0:key_rows, :], wkv) + shift).astype(BF16)
            base += key_rows
    if first:
        kvown_ref[0] = (dot(own_ref[...], wkv) + shift).astype(BF16)
        q = (dot(own_ref[0:own_rows, :], wq_ref[...]) + pair_lanes(bias_ref, pair)).astype(BF16) * BF16(SCALE)
        q_ref[0] = q
    else:
        q = q_ref[0]
    qs = stack_heads(q[0:SHARED])
    if first:
        peak = weight = total = None
    else:
        total = acc_in[0]
        peak, weight = stat_in[0, 0:1, :], stat_in[0, 8:9, :]
    base = 0
    for group, bias in zip(groups, biases):
        width = len(group) * key_rows
        span = slice(base, base + width)
        keys, values = kv_ref[0, span, 0:PAIR], kv_ref[0, span, PAIR:]
        base += width
        scores = dot_nt(keys, qs) + bias
        new = jnp.max(scores, axis=0, keepdims=True)
        if peak is not None:
            new = jnp.maximum(peak, new)
        probs = jnp.exp(scores - new)
        sums = jnp.sum(probs, axis=0, keepdims=True)
        part = dot_tn(values, probs.astype(BF16))
        if peak is None:
            weight, total = sums, part
        else:
            fade = jnp.exp(peak - new)
            weight = weight * fade + sums
            total = total * fade + part
        peak = new
    if first:
        idc = idc_ref[...]
        allowed = twice((idc == idr_ref[...]) & (idc != 0))
        scores = jnp.where(allowed, dot_nt(stack_heads(q), kvown_ref[0, 0:own_rows, 0:PAIR]), NEG)
        top = jnp.max(scores, axis=1, keepdims=True)
        probs = jnp.exp(scores - top)
        local_weight = jnp.sum(probs, axis=1, keepdims=True)
        local_out = unstack_heads(dot(probs.astype(BF16), kvown_ref[0, 0:own_rows, PAIR:]) / local_weight)
        local_lse = unstack_heads(top + jnp.log(local_weight))
        if not last:
            out_ref[:, here] = local_out
            lse_ref[:, here] = local_lse
    elif last:
        local_out, local_lse = out_in[:, here], lse_in[:, here]
    if last:
        shared_row = idc_ref[0:SHARED, :] == 0
        shared_out = unstack_heads((total / weight).T)
        shared_lse = unstack_heads(jnp.broadcast_to(peak + jnp.log(weight), (8, 2 * SHARED)).T[:, 0:1])
        mixed_ref[0:SHARED, here] = jnp.where(shared_row, shared_out, local_out[0:SHARED])
        mixed_ref[SHARED:, here] = local_out[SHARED:]
        full_lse_ref[0:SHARED, here] = jnp.where(shared_row, shared_lse, local_lse[0:SHARED])
        full_lse_ref[SHARED:, here] = local_lse[SHARED:]
    else:
        acc_ref[0] = total
        stat_ref[0, 0:8, :] = jnp.broadcast_to(peak, (8, 2 * SHARED))
        stat_ref[0, 8:16, :] = jnp.broadcast_to(weight, (8, 2 * SHARED))


class Attention:
    def __init__(self, first_low, weights, project_bias, idc, idr, key_rows):
        self.fixed = first_low, weights, project_bias, idc, idr
        self.key_rows = key_rows
        self.kvs = []

    def piece(self, blocks, last):
        first_low, weights, project_bias, idc, idr = self.fixed
        key_rows = self.key_rows
        own_rows, width = idc.shape[0], first_low.shape[1]
        wide = lambda rows: (sds((rows, width), F32), pl.BlockSpec((rows, width), lambda h: (0, 0)))
        deep = lambda rows, lane, dtype: (
            sds((PAIRS, rows, lane), dtype),
            pl.BlockSpec((1, rows, lane), lambda h: (h, 0, 0)),
        )
        first = not self.kvs
        keys = sum(b.shape[0] for b in blocks) * key_rows
        ins = [fixed(b) for b in blocks] + [lanes(weights, PAIRS), lanes(weights, 2 * PAIRS), fixed(project_bias)]
        if first:
            ins += [fixed(first_low), lanes(weights), fixed(idr)]
        else:
            ins += [lead(self.q)] + [lead(s) for s in self.state]
            if last:
                ins += [fixed(x) for x in self.local]
        ins += [fixed(idc)]
        outs = [deep(keys, 2 * PAIR, BF16)]
        if first:
            outs += [deep(own_rows, PAIR, BF16), deep(first_low.shape[0], 2 * PAIR, BF16)]
            if not last:
                outs += [wide(own_rows)] * 2
        outs += [wide(own_rows)] * 2 if last else [deep(PAIR, 2 * SHARED, F32), deep(16, 2 * SHARED, F32)]
        kernel = functools.partial(attend_kernel, len(blocks), key_rows, first, last)
        got = list(call(kernel, ins, outs, "attend", grid=(PAIRS,), cost=3.0 + keys / 90.0))
        self.kvs.append(got.pop(0))
        if first:
            self.q, self.kvown = got.pop(0), got.pop(0)
            if not last:
                self.local = [got.pop(0), got.pop(0)]
        self.state = got
        return (got[0],)


def erf(x):
    x = jnp.clip(x, -3.832506856900711, 3.832506856900711)
    s = x * x
    top = -2.72614225801306e-10
    for c in (2.77068142495902e-08, -2.10102402082508e-06, -5.69250639462346e-05, -7.34990630326855e-04, -2.95459980854025e-03, -1.60960333262415e-02):
        top = top * s + c
    low = -1.45660718464996e-05
    for c in (-2.13374055278905e-04, -1.68282697438203e-03, -7.37332916720468e-03, -1.42647390514189e-02):
        low = low * s + c
    return x * top / low


def middle_kernel(
    mixed, lse, stream, mlp_grad, act_grad, idc,
    w_output, merge_bias, gain, bias, w_up, up_bias, w_down, down_bias, w_head,
    predicted, act_ref, pre_ref, second_ref, mixed_low_ref, attn_low_ref, final_ref, attn_ref, grad_ref, unit_ref,
    stat_ref, up_sum, gain_sum, bias_sum, merge_sum,
):
    rows, width = mixed.shape
    hidden = w_up.shape[1]
    mixed_low = mixed[...].astype(BF16)
    mixed_low_ref[...] = mixed_low
    after = stream[...] + dot(mixed_low, w_output[...]) + merge_bias[...]
    unit_rows, scale = normalise(after)
    second = (unit_rows * gain[...] + bias[...]).astype(BF16)
    second_ref[...] = second
    out = after + down_bias[...]
    back = jnp.zeros((rows, width), F32)
    step = 768
    for start in range(0, hidden, step):
        part = slice(start, start + step)
        pre = dot(second, w_up[:, part]) + up_bias[:, part]
        cdf = 0.5 + 0.5 * erf(pre * 0.7071067811865476)
        act = (pre * cdf).astype(BF16)
        act_ref[:, part] = act
        slope = cdf + pre * (0.3989422804014327 * jnp.exp(-0.5 * pre * pre))
        grad = (act_grad[:, part] * slope).astype(BF16)
        pre_ref[:, part] = grad
        up_sum[:, part] = jnp.sum(grad.astype(F32), axis=0, keepdims=True)
        out += dot(act, w_down[part, :])
        back += dot_nt(grad, w_up[:, part])
    resid, gain_part, bias_part = norm_back(back, unit_rows, scale, gain[...])
    gain_sum[...] = gain_part
    bias_sum[...] = bias_part
    attn = mlp_grad[...] + resid
    attn_ref[...] = attn
    merge_sum[...] = jnp.sum(attn, axis=0, keepdims=True)
    attn_low = attn.astype(BF16)
    attn_low_ref[...] = attn_low
    grad = dot_nt(attn_low, w_output[...]).astype(BF16)
    grad_ref[...] = grad
    shared_row = idc[0:SHARED, :] == 0
    unit_ref[0:SHARED, :] = jnp.where(shared_row, grad[0:SHARED], jnp.zeros((SHARED, width), BF16))
    lane = lax.broadcasted_iota(jnp.int32, (MARKS, width), 1)
    head = lax.broadcasted_iota(jnp.int32, (MARKS, width), 0)
    ones = jnp.where(lane // HEAD_DIM == head, 1.0, 0.0)
    pick = jnp.where(lane == head * HEAD_DIM, 1.0, 0.0)
    delta = dot_nt(ones, grad.astype(F32) * mixed[...], lax.Precision.HIGHEST)
    turned = dot_nt(pick, lse[...], lax.Precision.HIGHEST)
    stat_ref[0] = turned
    stat_ref[1] = delta
    zeros = jnp.zeros((rows, 128), F32)
    ids = jnp.where(idc[...] == 0, 1.0, 0.0) + zeros
    row_ids = dot_nt(jnp.full((MARKS, 128), 1.0 / 128, F32), ids)
    shared_lane = row_ids[:, 0:SHARED] > 0.5
    sent = []
    for value, other in ((turned, -NEG), (delta, 0.0)):
        value = jnp.where(shared_lane, value[:, 0:SHARED], other)
        high = value.astype(BF16)
        sent += [high, (value - high.astype(F32)).astype(BF16)]
    unit_ref[SHARED:, :] = jnp.concatenate(sent, axis=1)
    final = out.astype(BF16)
    final_ref[...] = final
    predicted[...] = dot(final, w_head[...]).astype(BF16)


def query_kernel(n_blocks, n_kvs, key_rows, first, *refs):
    block_refs, kv_refs = refs[:n_blocks], refs[n_blocks : n_blocks + n_kvs]
    kvown_ref, q_ref, wq_ref, grad_ref, mixed_ref, lse_ref, bias_ref, idc_ref, idr_ref = refs[
        n_blocks + n_kvs : n_blocks + n_kvs + 9
    ]
    dq_ref, qall_ref = refs[-2:]
    pair = first + pl.program_id(0)
    own_rows = idc_ref.shape[0]
    flat = [(ref, i) for ref in block_refs for i in range(ref.shape[0])]
    base = 0
    wq, shift = wq_ref[...], pair_lanes(bias_ref, pair)
    for ref, index in flat:
        rows = (dot(ref[index, 0:SHARED, :], wq) + shift).astype(BF16)
        qall_ref[0, base : base + SHARED, :] = rows * BF16(SCALE)
        base += SHARED
    idc = idc_ref[...]
    allowed = twice((idc == idr_ref[...]) & (idc != 0))
    shared_row = idc == 0
    q = q_ref[0]
    grad = pair_lanes(grad_ref, pair)
    product = stack_heads(grad.astype(F32) * pair_lanes(mixed_ref, pair))
    delta = jnp.sum(product, axis=1, keepdims=True)
    lse = pair_lanes(lse_ref, pair)
    lse = jnp.concatenate([lse[:, 0:1], lse[:, HEAD_DIM : HEAD_DIM + 1]], axis=0)
    qm, gm = stack_heads(q), stack_heads(grad)
    part_rows = lambda x: jnp.concatenate([x[0:SHARED], x[own_rows : own_rows + SHARED]], axis=0)
    qs, gs, delta_s, lse_s = part_rows(qm), part_rows(gm), part_rows(delta), part_rows(lse)
    total, used = None, 0
    for kv_ref in kv_refs:
        count = kv_ref.shape[1] // key_rows
        for start in range(0, count, 8):
            size = min(8, count - start)
            bias = key_bias(flat[used : used + size], key_rows)
            used += size
            span = slice(start * key_rows, (start + size) * key_rows)
            keys = kv_ref[0, span, 0:PAIR]
            values = kv_ref[0, span, PAIR:]
            probs = jnp.exp(dot_nt(qs, keys) + bias - lse_s)
            ds = (probs * (dot_nt(gs, values) - delta_s)).astype(BF16)
            part = dot(ds, keys)
            total = part if total is None else total + part
    keys, values = kvown_ref[0, 0:own_rows, 0:PAIR], kvown_ref[0, 0:own_rows, PAIR:]
    probs = jnp.exp(jnp.where(allowed, dot_nt(qm, keys) - lse, NEG))
    ds = (probs * (dot_nt(gm, values) - delta)).astype(BF16)
    local = unstack_heads(dot(ds, keys)) * SCALE
    shared = jnp.where(shared_row[0:SHARED], unstack_heads(total) * SCALE, local[0:SHARED])
    here = pl.ds(pl.multiple_of(pl.program_id(0) * PAIR, PAIR), PAIR)
    dq_ref[0:SHARED, here] = shared.astype(BF16)
    dq_ref[SHARED:, here] = local[SHARED:].astype(BF16)


def query_back(groups, kvs, kvown, q, mixed_grad, mixed, lse, wq, project_bias, idc, idr, key_rows, first, pairs, after):
    own_rows = idc.shape[0]
    blocks = [b for group in groups for b in group]
    count = sum(b.shape[0] for b in blocks)
    ins = [fixed(b) for b in blocks] + [lead(kv, first) for kv in kvs] + [lead(x, first) for x in (kvown, q)] + [lanes(wq, first)]
    ins += [fixed(x) for x in (mixed_grad, mixed, lse, project_bias, idc, idr)]
    outs = [
        (sds((own_rows, pairs * PAIR), BF16), pl.BlockSpec((own_rows, pairs * PAIR), lambda h: (0, 0))),
        (sds((pairs, count * SHARED, PAIR), BF16), pl.BlockSpec((1, count * SHARED, PAIR), lambda h: (h, 0, 0))),
    ]
    kernel = functools.partial(query_kernel, len(blocks), len(kvs), key_rows, first)
    return call(kernel, ins, outs, "query_back", grid=(pairs,), cost=4.2 * pairs, after=after)


def key_kernel(n_blocks, first, *refs):
    grad_refs = refs[:n_blocks]
    kvown_ref, qall_ref, q_ref, grad_ref, own_stat_ref, idc_ref, idr_ref, live_ref = refs[n_blocks : n_blocks + 8]
    dk_ref, dv_ref, grads_ref, stats_ref = refs[n_blocks + 8 :]
    pair = first + pl.program_id(0)
    own_rows = idc_ref.shape[0]
    rim = kvown_ref.shape[1] - own_rows
    flat = [(ref, i) for ref in grad_refs for i in range(ref.shape[0])]

    @pl.when(pl.program_id(0) == 0)
    def _():
        base = 0
        for begin in range(0, len(flat), 2):
            sums = []
            for ref, i in flat[begin : begin + 2]:
                stat = ref[i, SHARED:, :].astype(F32)
                sums.append(
                    (
                        stat[:, 0:SHARED] + stat[:, SHARED : 2 * SHARED],
                        stat[:, 2 * SHARED : 3 * SHARED] + stat[:, 3 * SHARED :],
                    )
                )
            for kind in range(2):
                stats_ref[kind, :, base : base + 2 * SHARED] = jnp.concatenate([s[kind] for s in sums], axis=1)
            base += 2 * SHARED

    base = 0
    there = pl.ds(pl.multiple_of(pair * PAIR, PAIR), PAIR)
    for ref, i in flat:
        grads_ref[base : base + SHARED, :] = ref[i, 0:SHARED, there]
        base += SHARED
    idc = idc_ref[...]
    allowed = twice((idc == idr_ref[...]) & (idc != 0))
    shared_row = idc == 0
    live = live_ref[0:1, 0:1] > 0.5
    kv = kvown_ref[0]
    k_all, v_all = kv[:, 0:PAIR], kv[:, PAIR:]
    in_shared = lambda x: jnp.concatenate([x[0:SHARED], x[own_rows:]], axis=0)
    q, grad = q_ref[0], pair_lanes(grad_ref, pair)
    n_shared = SHARED + rim
    k_sh, v_sh = stack_heads(in_shared(k_all)), stack_heads(in_shared(v_all))

    def both_rows(ref, kind, rows, columns):
        picked = [ref[kind, pl.ds(2 * pair + head, 1), columns] for head in range(2)]
        return jnp.concatenate([jnp.broadcast_to(p, (rows, p.shape[1])) for p in picked], axis=0)

    dk = dv = None
    chunk = min(base, 1536)
    for start in range(0, base, chunk):
        span = slice(start, start + chunk)
        q_all, g_all = qall_ref[0, span, :], grads_ref[span, :]
        probs = jnp.exp(dot_nt(k_sh, q_all) - both_rows(stats_ref, 0, n_shared, span))
        part_v = dot(probs.astype(BF16), g_all)
        ds = (probs * (dot_nt(v_sh, g_all) - both_rows(stats_ref, 1, n_shared, span))).astype(BF16)
        part_k = dot(ds, q_all)
        dk = part_k if dk is None else dk + part_k
        dv = part_v if dv is None else dv + part_v
    every = slice(None)
    scores = dot_nt(stack_heads(k_all[0:own_rows]), q) - both_rows(own_stat_ref, 0, own_rows, every)
    probs = jnp.exp(jnp.where(allowed, scores, NEG))
    local_v = dot(probs.astype(BF16), grad)
    ds = dot_nt(stack_heads(v_all[0:own_rows]), grad) - both_rows(own_stat_ref, 1, own_rows, every)
    local_k = dot((probs * ds).astype(BF16), q)
    here = pl.ds(pl.multiple_of(pl.program_id(0) * PAIR, PAIR), PAIR)
    for out, shared, local in ((dk_ref, dk, local_k), (dv_ref, dv, local_v)):
        shared, local = unstack_heads(shared), unstack_heads(local)
        out[0:SHARED, here] = jnp.where(shared_row[0:SHARED], shared[0:SHARED], local[0:SHARED]).astype(BF16)
        out[SHARED:own_rows, here] = local[SHARED:].astype(BF16)
        out[own_rows:, here] = jnp.where(live, shared[SHARED:], 0.0).astype(BF16)


def key_back(groups, kvown, qall, q, mixed_grad, own_stats, idc, idr, live, first, pairs, after):
    joined_rows = kvown.shape[1]
    grads = [g for group in groups for g in group]
    ins = [fixed(g) for g in grads] + [lead(kvown, first), lead(qall), lead(q, first)]
    ins += [fixed(x) for x in (mixed_grad, own_stats, idc, idr, live)]
    out = (sds((joined_rows, pairs * PAIR), BF16), pl.BlockSpec((joined_rows, pairs * PAIR), lambda h: (0, 0)))
    scratch = [pltpu.VMEM((qall.shape[1], PAIR), BF16), pltpu.VMEM((2, MARKS, qall.shape[1]), F32)]
    kernel = functools.partial(key_kernel, len(grads), first)
    return call(kernel, ins, [out, out], "key_back", grid=(pairs,), scratch=scratch, cost=3.7 * pairs, after=after)


def input_kernel(dq, dk, dv, weight, stream, arrived, gain, attn_grad, rim_ref, rows_ref, joint_ref, vec_ref):
    own, width = dq.shape
    dq, dk, dv = dq[...], dk[...], dv[...]
    wq, wk, wv = weight[:, 0:width], weight[:, width : 2 * width], weight[:, 2 * width :]
    rim_grad = dot_nt(dk[own:], wk) + dot_nt(dv[own:], wv)
    rim_rows, rim_scale = normalise(arrived[...].astype(F32))
    rim_back, rim_gain, rim_bias = norm_back(rim_grad, rim_rows, rim_scale, gain[...])
    rim_ref[...] = rim_back.astype(BF16)
    own_grad = dot_nt(dq, wq) + dot_nt(dk[:own], wk) + dot_nt(dv[:own], wv)
    own_rows, own_scale = normalise(stream[...])
    own_back, own_gain, own_bias = norm_back(own_grad, own_rows, own_scale, gain[...])
    rows_ref[...] = own_back + attn_grad[...]
    joint_ref[0:own, 0:width] = dq
    joint_ref[own:, 0:width] = jnp.zeros((dk.shape[0] - own, width), BF16)
    joint_ref[:, width : 2 * width] = dk
    joint_ref[:, 2 * width :] = dv
    vec_ref[0:1, :] = own_gain + rim_gain
    vec_ref[1:2, :] = own_bias + rim_bias
    vec_ref[2:3, :] = jnp.sum(dq.astype(F32), axis=0, keepdims=True)
    vec_ref[3:4, :] = jnp.sum(dv.astype(F32), axis=0, keepdims=True)


def pixel_kernel(rows, returned, halo, weight, low_ref, grad_ref):
    place = lax.broadcasted_iota(jnp.int32, (rows.shape[0], halo.shape[1]), 0)
    spread = jnp.where(place == halo[...], 1.0, 0.0).astype(BF16)
    low = (rows[...] + dot(spread, returned[...])).astype(BF16)
    low_ref[...] = low
    grad_ref[...] = dot_nt(low, weight[...]).astype(BF16)


ORDERS = {
    "x": [("gx", 2, None), ("gy", 1, 2), ("gy", 2, 1), ("gy", 4, 0)],
    "y": [("gy", 1, None), ("gy", 2, 1), ("gy", 4, 0)],
    "z": [("gy", 2, None), ("gy", 4, 0), ("gy", 1, 0)],
    "s": [("gy", 1, None)],
    "yx": [("gy", 1, None), ("gx", 2, 2), ("gy", 2, 1), ("gy", 4, 0)],
}


def product_blocks(left, right, core_half, n):
    half = right.shape[1] // 2
    x = left[...]
    for j in range(half // LANES):
        columns = pl.ds(pl.multiple_of(core_half * half + j * LANES, 128), LANES)
        out = dot_tn(x, right[:, columns])
        yield out.reshape(n, out.shape[0] // n, LANES)


def away_kernel(n, n_pairs, *refs):
    pairs, outs = refs[: 2 * n_pairs], refs[2 * n_pairs :]
    other = 1 - lax.axis_index("gx") % 2
    (out,) = outs
    row = 0
    for p in range(n_pairs):
        for block in product_blocks(pairs[2 * p], pairs[2 * p + 1], other, n):
            out[:, row : row + block.shape[1], :] = block.astype(BF16)
            row += block.shape[1]


def home_kernel(n, n_pairs, order, n_small, row, *refs):
    pairs = refs[: 2 * n_pairs]
    arrived = refs[2 * n_pairs]
    small = refs[2 * n_pairs + 1 : 2 * n_pairs + 1 + n_small]
    send, keep = refs[2 * n_pairs + 1 + n_small :][-2:] if order != "s" else (None, refs[-1])
    core = lax.axis_index("gx") % 2
    axis, bit = ORDERS[order][0][:2]
    low = lax.axis_index(axis) // bit % 2 == 0
    half_row = 0

    def put(first, second, start, rows):
        if order == "s":
            for half, value in ((0, first), (1, second)):
                keep[:, half, start : start + rows, :] = value
            return
        if order == "x":
            span = slice(start, start + rows)
            send[:, span, :] = jnp.where(low, second, first)
            keep[:, span, :] = jnp.where(low, first, second)
            return
        for half, value in ((0, first), (1, second)):
            span = slice(start, start + rows)
            value = value.reshape(n // 2 // bit, 2, bit, rows, LANES)
            for out, one, other in ((send, value[:, 1], value[:, 0]), (keep, value[:, 0], value[:, 1])):
                out[:, half, span, :] = jnp.where(low, one, other).reshape(n // 2, rows, LANES)

    for p in range(n_pairs):
        for block in product_blocks(pairs[2 * p], pairs[2 * p + 1], core, n):
            r = block.shape[1]
            block = (block + arrived[:, row : row + r, :].astype(F32)).astype(BF16)
            put(block[:, : r // 2], block[:, r // 2 :], half_row, r // 2)
            row += r
            half_row += r // 2
    if n_small:
        value = small[0][...] + small[1][...]
        put(value, jnp.zeros(value.shape, BF16), half_row, value.shape[1])


def away(pairs, n, name, after=()):
    arrays = [x for pair in pairs for x in pair]
    rows = sum(b.shape[1] // 2 // LANES * a.shape[1] // n for a, b in pairs)
    outs = [(sds((n, rows, LANES), BF16), VMEM)]
    return call(functools.partial(away_kernel, n, len(pairs)), plain(*arrays), outs, name, cost=rows / 135.0, after=after)[0]


def home(pairs, n, arrived, order, name, small=(), first_row=0, after=()):
    arrays = [x for pair in pairs for x in pair] + [arrived] + list(small)
    rows = sum(b.shape[1] // 2 // LANES * a.shape[1] // n // 2 for a, b in pairs)
    rows += small[0].shape[1] if small else 0
    shape = (n, rows, LANES) if order == "x" else (n // 2, 2, rows, LANES)
    kernel = functools.partial(home_kernel, n, len(pairs), order, len(small), first_row)
    if order == "s":
        outs = [(sds((n, 2, rows, LANES), BF16), VMEM)]
        whole = call(kernel, plain(*arrays), outs, name, after=after)[0]
        return whole, lax.psum_scatter(whole, "gy", scatter_dimension=0, tiled=False)
    outs = [(sds(shape, BF16), VMEM)] * 2
    send, keep = call(kernel, plain(*arrays), outs, name, after=after)
    got = swap(send, *ORDERS[order][0][:2])
    shape = ((2, 2, 2) if order == "x" else (2, 2)) + keep.shape[1:]
    return send, (keep.reshape(shape), got.reshape(shape))


def next_step(group, axis, bit, dim):
    keep, got = group
    mine = bit_of(axis, bit)
    pick = lambda x, i: lax.dynamic_index_in_dim(x, i, dim, keepdims=False)
    send = pick(keep, 1 - mine) + pick(got, 1 - mine)
    return send, (pick(keep, mine) + pick(got, mine), swap(send, axis, bit))


def held_step(group, axis, bit, dim, after):
    keep, got = group
    shape = keep.shape[:dim] + keep.shape[dim + 1 :]

    def kernel(keep, got, send, left):
        mine = lax.axis_index(axis) // bit % 2
        for out, side in ((send, 1 - mine), (left, mine)):
            index = (slice(None),) * dim + (side,)
            out[...] = keep[index] + got[index]

    send, left = call(kernel, plain(keep, got), [(sds(shape, BF16), VMEM)] * 2, "step", after=after)
    return send, (left, swap(send, axis, bit))


def all_of(group):
    part = group[0] + group[1] if isinstance(group, tuple) else group
    x_low, core_low = bit_of("gx", 2) == 0, bit_of("gx", 1) == 0
    over = swap(part, "gx", 2)
    if part.ndim == 3:
        both = part + over
    else:
        both = jnp.stack([jnp.where(x_low, part, over), jnp.where(x_low, over, part)])
    across = swap(both, "gx", 1)
    return [jnp.where(core_low, both, across), jnp.where(core_low, across, both)]


def cut(sides, pairs, n):
    outs, start = [], 0
    for a, b in pairs:
        r, blocks = a.shape[1] // n, b.shape[1] // 2 // LANES
        halves = []
        for side in sides:
            piece = side[:, start : start + blocks * r // 2].reshape(2, blocks, r // 2, LANES)
            halves.append(piece.transpose(0, 2, 1, 3).reshape(r, blocks * LANES))
        start += blocks * r // 2
        outs.append(jnp.concatenate(halves, axis=1).astype(F32))
    return outs, [side[0, start:].astype(F32) for side in sides]


def shards(
    pixels,
    frame_index,
    patch_cell,
    tile_id,
    halo_index,
    w_patch,
    first_gain,
    first_bias,
    w_project,
    project_bias,
    w_output,
    merge_bias,
    second_gain,
    second_bias,
    w_up,
    up_bias,
    w_down,
    down_bias,
    w_head,
    cotangent,
):
    n_gx, n_gy = lax.axis_size("gx"), lax.axis_size("gy")
    own, rim = pixels.shape[0], halo_index.shape[0]
    width, hidden, depth = w_output.shape[0], w_up.shape[1], pixels.shape[1]
    key_rows = SHARED + rim
    idc, idr = tile_id.reshape(own, 1), tile_id.reshape(1, own)
    live = jnp.broadcast_to(jnp.where(lax.axis_index("gx") > 0, 1.0, 0.0).astype(F32), (8, 128))
    halo = halo_index.reshape(1, rim)
    row = lambda v: v.reshape(1, -1)
    mat = lambda rows, columns, dtype: (sds((rows, columns), dtype), VMEM)

    high, low = position_table(width)
    stream, outgoing, own_low = call(
        embed_kernel,
        plain(
            pixels, w_patch, row(frame_index), patch_cell, halo, high, low, row(first_gain), row(first_bias)
        ),
        [mat(own, width, F32), mat(rim, width, BF16), mat(own, width, BF16)],
        "embed",
    )
    arrived = shifted(outgoing, "gx", 1)
    unit, first_low = call(
        unit_kernel,
        plain(own_low, arrived, row(first_gain), row(first_bias), idr, live),
        [mat(key_rows + MARKS, width, BF16), mat(own + rim, width, BF16)],
        "unit",
        cost=2.4,
    )
    column = ColumnGather(unit)
    shift = row(project_bias)
    attention = Attention(first_low, w_project, shift, idc, idr, key_rows)
    if column.direct:
        column.second()
        if CFG["early"]:
            after = attention.piece([unit[None], column.near[None]], False)
            column.third(after)
            column.fourth((column.far,))
            attention.piece(column.groups[1], False)
            attention.piece(column.groups[2], True)
        else:
            after = attention.piece([unit[None], column.near[None], column.y0[None]], False)
            column.third(after)
            after = attention.piece([column.y1[None], column.far[None]], False)
            column.fourth(after)
            attention.piece([column.last[None], column.y2[None], column.y3[None]], True)
    else:
        attention.piece(column.groups[0], True)
    groups, kvs, kvown, q = column.groups, attention.kvs, attention.kvown, attention.q
    mixed, lse = attention.state

    mlp_grad = dot_nt(cotangent, w_head)
    down_bias_grad = jnp.sum(mlp_grad, axis=0)
    mlp_low = mlp_grad.astype(BF16)
    act_grad = dot_nt(mlp_low, w_down)
    (
        predicted, act_low, pre_grad, second_low, mixed_low, attn_low, final_low, attn_grad, mixed_grad, grad_unit,
        own_stats, up_sum, second_gain_sum, second_bias_sum, merge_sum,
    ) = call(
        middle_kernel,
        plain(
            mixed, lse, stream, mlp_grad, act_grad, idc, w_output, row(merge_bias), row(second_gain),
            row(second_bias), w_up, row(up_bias), w_down, row(down_bias), w_head,
        ),
        [mat(own, depth, BF16), mat(own, hidden, BF16), mat(own, hidden, BF16)]
        + [mat(own, width, BF16)] * 4
        + [mat(own, width, F32), mat(own, width, BF16), mat(SHARED + MARKS, width, BF16)]
        + [(sds((2, MARKS, own), F32), VMEM), mat(1, hidden, F32)]
        + [mat(1, width, F32)] * 3,
        "middle",
        cost=18.0,
    )
    special = n_gx == 4 and n_gy == 8
    head_pair, down_pair = (final_low, cotangent), (act_low, mlp_low)
    up_pair, output_pair = (second_low, pre_grad), (mixed_low, attn_low)
    gather = (DirectGather if CFG["direct"] else FreeGather)(grad_unit)
    early_a, early_b = [head_pair, down_pair], [up_pair, output_pair]
    q_parts, k_parts = [], []

    def query_piece(first, pairs, after):
        part = query_back(
            groups, kvs, kvown, q, mixed_grad, mixed, lse, w_project, shift, idc, idr, key_rows, first, pairs, after
        )
        q_parts.append(part)
        return (part[0],)

    def key_piece(place, first, pairs, after):
        qall = jnp.concatenate([p[1] for p in q_parts], axis=0) if CFG["qp"] != CFG["kp"] else q_parts[place][1]
        part = key_back(gather.groups, kvown, qall, q, mixed_grad, own_stats, idc, idr, live, first, pairs, after)
        k_parts.append(part)
        return (part[0],)

    after = ()
    if special:
        if CFG["merged"]:
            share_a = share_b = away(early_a + early_b, n_gy, "away")
            gone_a = gone_b = swap(share_a, "gx", 1)
        else:
            share_a, share_b = away(early_a, n_gy, "away"), away(early_b, n_gy, "away")
            gone_a, gone_b = swap(share_a, "gx", 1), swap(share_b, "gx", 1)
        after = (share_a, share_b) if CFG["away_first"] else ()

    def homes(after):
        gate = CFG["gate"]
        if gate >= 1:
            after += (gather.near, gather.mid, gather.y0)
        if gate >= 3:
            after += (gather.far_end, gather.far_mid, gather.y1)
        if CFG["sc"]:
            send, group = home(early_a + early_b, n_gy, gone_a, "s", "home", after=after)
            return (send,), group, None
        send_a, group_a = home(early_a, n_gy, gone_a, "x", "home", after=after)
        after += (send_a,)
        if gate >= 2:
            after += (gather.far_end, gather.far_mid, gather.y1)
        if gate >= 3:
            after += (gather.last_end, gather.y2)
        first_row = 2 * group_a[0].shape[-2] if CFG["merged"] else 0
        send_b, group_b = home(early_b, n_gy, gone_b, CFG["b"], "home", first_row=first_row, after=after)
        return (send_a, send_b), group_a, group_b

    def second_steps(group_a, group_b, after):
        send_a, group_a = held_step(group_a, *ORDERS["x"][1], after)
        send_b, group_b = held_step(group_b, *ORDERS[CFG["b"]][1], after + (send_a,))
        return (send_a, send_b), group_a, group_b

    done_a = done_b = 1
    first = 0
    for i, size in enumerate(CFG["qp"]):
        after = query_piece(first, size, after)
        first += size
        if special and CFG["home"] == i:
            more, group_a, group_b = homes(after)
            after += more
    first = 0
    for i, size in enumerate(CFG["kp"]):
        part = key_piece(i, first, size, after)
        after = part
        first += size
        if special and CFG["ab2"] == i:
            more, group_a, group_b = second_steps(group_a, group_b, after)
            after += more
            done_a = done_b = 2
    dq = jnp.concatenate([p[0] for p in q_parts], axis=1)
    dk = jnp.concatenate([p[0] for p in k_parts], axis=1)
    dv = jnp.concatenate([p[1] for p in k_parts], axis=1)
    rim_grad, partial, joint_grad, first_sums = call(
        input_kernel,
        plain(dq, dk, dv, w_project, stream, arrived, row(first_gain), attn_grad),
        [mat(rim, width, BF16), mat(own, width, F32), mat(own + rim, 3 * width, BF16), mat(8, width, F32)],
        "input",
        cost=6.0,
        after=after,
    )
    returned = shifted(rim_grad, "gx", -1)
    project_pair = (first_low, joint_grad)
    after = ()
    if special:
        share_c = away([project_pair], n_gy, "away")
        gone_c = swap(share_c, "gx", 1)
        after = ()
        if CFG["ab2"] == "c":
            after, group_a, group_b = second_steps(group_a, group_b, (share_c,))
            done_a = done_b = 2
    embed_low, pixel_grad = call(
        pixel_kernel,
        plain(partial, returned, halo, w_patch),
        [mat(own, width, BF16), mat(own, depth, BF16)],
        "pixel",
        cost=3.0,
        after=after if special else (),
    )
    patch_pair = (pixels, embed_low)

    vectors = [
        first_sums[0],
        first_sums[1],
        first_sums[2:4].reshape(-1),
        merge_sum[0],
        second_gain_sum[0],
        second_bias_sum[0],
        up_sum[0],
        down_bias_grad,
    ]
    sizes = [v.shape[0] // n_gy for v in vectors]
    if special:
        core = bit_of("gx", 1)
        small = jnp.stack([jnp.pad(v.reshape(n_gy, z), ((0, 0), (0, LANES - z))) for v, z in zip(vectors, sizes)], axis=1)
        small = jnp.pad(small.astype(BF16).reshape(n_gy, 2, 4, LANES), ((0, 0), (0, 0), (0, MARKS - 4), (0, 0)))
        small_mine = lax.dynamic_index_in_dim(small, core, 1, keepdims=False)
        small_gone = swap(lax.dynamic_index_in_dim(small, 1 - core, 1, keepdims=False), "gx", 1)
        share_d = away([patch_pair], n_gy, "away")
        gone_d = swap(share_d, "gx", 1)
        send_c, group_c = home([project_pair], n_gy, gone_c, CFG["c"], "home", after=(share_d,) if CFG["chain"] else ())
        send_d, group_d = home(
            [patch_pair], n_gy, gone_d, CFG["d"], "home", small=[small_mine, small_gone], after=(send_c,) if CFG["chain"] else ()
        )
        if CFG["ab3"] and done_a == 2:
            send_a, group_a = held_step(group_a, *ORDERS["x"][2], (send_d,))
            send_b, group_b = held_step(group_b, *ORDERS[CFG["b"]][2], (send_d,))
            done_a = done_b = 3
        if CFG["join"]:

            def joined(groups, orders):
                groups = [next_step(group, *ORDERS[order][1])[1] for group, order in zip(groups, orders)]
                for axis, bit, dim in ORDERS["x"][2:]:
                    mine = bit_of(axis, bit)
                    pick = lambda x, i: lax.dynamic_index_in_dim(x, i, dim, keepdims=False)
                    put = lambda i: jnp.concatenate([pick(k, i) + pick(g, i) for k, g in groups], axis=-2)
                    groups = [(put(mine), swap(put(1 - mine), axis, bit))]
                return all_of(groups[0])

            sides = joined([group_a, group_b], ["x", CFG["b"]])
            (head_grad, down_grad, up_grad, output_grad), _ = cut(sides, early_a + early_b, n_gy)
            sides = joined([group_c, group_d], [CFG["c"], CFG["d"]])
            (project_grad, patch_grad), marks = cut(sides, [project_pair, patch_pair], n_gy)
            groups = None
        else:
            groups = []
            for group, hops in (
                *(((group_a, ()),) if CFG["sc"] else ((group_a, ORDERS["x"][done_a:]), (group_b, ORDERS[CFG["b"]][done_b:]))),
                (group_c, ORDERS[CFG["c"]][1:]),
                (group_d, ORDERS[CFG["d"]][1:]),
            ):
                for hop in hops:
                    _, group = next_step(group, *hop)
                groups.append(all_of(group))
        if groups is None:
            pass
        elif CFG["sc"]:
            groups.insert(0, None)
            (head_grad, down_grad, up_grad, output_grad), _ = cut(groups[1], early_a + early_b, n_gy)
        else:
            (head_grad, down_grad), _ = cut(groups[0], early_a, n_gy)
            (up_grad, output_grad), _ = cut(groups[1], early_b, n_gy)
        if groups is not None:
            (project_grad,), _ = cut(groups[2], [project_pair], n_gy)
            (patch_grad,), marks = cut(groups[3], [patch_pair], n_gy)
        small_outs = [marks[i // 4][i % 4, :size] for i, size in enumerate(sizes)]
    else:

        def total(x):
            part = lax.psum_scatter(x.astype(BF16), "gy", scatter_dimension=0, tiled=True)
            return lax.psum(part, "gx").astype(F32)

        pairs = [head_pair, down_pair, up_pair, output_pair, project_pair, patch_pair]
        head_grad, down_grad, up_grad, output_grad, project_grad, patch_grad = [total(dot_tn(a, b)) for a, b in pairs]
        tail = total(jnp.concatenate([v.reshape(n_gy, -1) for v in vectors], axis=1)).reshape(-1)
        starts = [sum(sizes[:i]) for i in range(len(sizes))]
        small_outs = [tail[s : s + z] for s, z in zip(starts, sizes)]
    return (
        predicted,
        pixel_grad,
        patch_grad,
        small_outs[0],
        small_outs[1],
        project_grad,
        small_outs[2],
        output_grad,
        small_outs[3],
        small_outs[4],
        small_outs[5],
        up_grad,
        small_outs[6],
        down_grad,
        small_outs[7],
        head_grad,
    )


def solution(mesh):
    tokens = P(("gx", "gy"))
    rows = P(("gx", "gy"), None)
    in_specs = (rows, tokens, P(None, ("gx", "gy")), tokens, tokens) + (P(),) * 14 + (rows,)
    matrix, vector = P("gy", None), P("gy")
    out_specs = (
        rows,
        rows,
        matrix,
        vector,
        vector,
        matrix,
        vector,
        matrix,
        vector,
        vector,
        vector,
        matrix,
        vector,
        matrix,
        vector,
        matrix,
    )
    return jax.shard_map(shards, mesh=mesh, in_specs=in_specs, out_specs=out_specs, check_vma=False)
```

```python
import functools

import jax
import jax.numpy as jnp
import numpy as np
from jax import lax
from jax.experimental import pallas as pl
from jax.experimental.pallas import tpu as pltpu
from jax.sharding import PartitionSpec as P

HEADS = 12
HEAD_DIM = 64
PAIR = 2 * HEAD_DIM
PAIRS = HEADS // 2
SCALE = HEAD_DIM**-0.5
LANES = 384
SHARED = 192
MARKS = 16
GRID_SIDE = 56
EPS = 1e-06
NEG = -1e30
F32 = jnp.float32
BF16 = jnp.bfloat16
VMEM_LIMIT = 56
CFG = dict(qp=(3, 3), kp=(3, 3), home=1, gate=0, b="yx", c="x", d="z", ab2=None, ab3=None, merged=False, direct=False, sc=False, limit=56, limits={}, chain="s", away_first=True, early=False, join=False)
PACE = 1.0


def dot(a, b):
    return jnp.dot(a, b, preferred_element_type=F32)


def dot_nt(a, b, precision=None):
    return lax.dot_general(a, b, (((1,), (1,)), ((), ())), preferred_element_type=F32, precision=precision)


def dot_tn(a, b):
    return lax.dot_general(a, b, (((0,), (0,)), ((), ())), preferred_element_type=F32)


def sds(shape, dtype):
    return jax.ShapeDtypeStruct(tuple(shape), dtype)


def shifted(x, axis, by):
    length = lax.axis_size(axis)
    pairs = [(i, i + by) for i in range(length) if 0 <= i + by < length]
    return lax.ppermute(x, axis, pairs)


def swap(x, axis, bit):
    length = lax.axis_size(axis)
    return lax.ppermute(x, axis, [(i, i ^ bit) for i in range(length)])


def swap_chip(x, dx, dz, dy):
    n_gx, n_gy = lax.axis_size("gx"), lax.axis_size("gy")
    flip = 2 * dx * n_gy + 2 * dz + dy
    return lax.ppermute(x, ("gx", "gy"), [(i, i ^ flip) for i in range(n_gx * n_gy)])


class ColumnGather:
    def __init__(self, unit):
        self.unit = unit
        self.direct = lax.axis_size("gy") == 8
        if not self.direct:
            self.groups = [[lax.all_gather(unit, "gy", axis=0, tiled=False)]]
            return
        self.y0 = self.across(unit)
        self.near = self.along(unit, [(0, 1), (1, 0), (2, 3), (3, 2)])
        self.mid = self.along(unit, [(1, 2), (2, 1)])

    def along(self, x, hops):
        return lax.ppermute(x, "gy", [(2 * a + y, 2 * b + y) for a, b in hops for y in (0, 1)])

    def across(self, x):
        return swap(x, "gy", 1)

    def second(self):
        self.y1 = self.across(self.near)
        self.far_end = self.along(self.mid, [(1, 0), (2, 3)])
        self.far_mid = self.along(self.near, [(1, 2), (2, 1)])

    def third(self, after):
        self.last_end = self.along(self.far_mid, [(1, 0), (2, 3)])
        self.far = choose(self.far_end, self.far_mid, after)
        self.y2 = self.across(self.far)

    def fourth(self, after):
        self.last = choose(self.last_end, self.mid, after)
        self.y3 = self.across(self.last)
        self.group()

    def group(self):
        groups = [[self.unit, self.near, self.y0], [self.y1, self.far], [self.last, self.y2, self.y3]]
        if CFG["early"]:
            groups = [[self.unit, self.near], [self.y0, self.y1, self.far], [self.last, self.y2, self.y3]]
        self.groups = [[part[None] for part in group] for group in groups]


class FreeGather(ColumnGather):
    def __init__(self, unit):
        super().__init__(unit)
        if not self.direct:
            return
        self.second()
        place = lax.axis_index("gy") // 2
        at_end = (place == 0) | (place == 3)
        self.far = jnp.where(at_end, self.far_end, self.far_mid)
        self.y2 = self.across(self.far)
        self.last_end = self.along(self.far_mid, [(1, 0), (2, 3)])
        self.last = jnp.where(at_end, self.last_end, self.mid)
        self.y3 = self.across(self.last)
        self.group()


class DirectGather:
    def __init__(self, unit):
        self.unit = unit
        if lax.axis_size("gy") != 8:
            self.groups = [[lax.all_gather(unit, "gy", axis=0, tiled=False)]]
            return
        self.near, self.y0 = swap_chip(unit, 0, 1, 0), swap_chip(unit, 0, 0, 1)
        self.mid = self.far_end = self.far_mid = self.last_end = self.near
        self.far, self.last = swap_chip(unit, 0, 2, 0), swap_chip(unit, 0, 3, 0)

        self.second()

    def second(self):
        y1, y2, y3 = (swap_chip(x, 0, 0, 1) for x in (self.near, self.far, self.last))
        self.y1, self.y2, self.y3 = y1, y2, y3
        groups = [[self.unit, self.near, self.y0], [y1, self.far], [self.last, y2, y3]]
        self.groups = [[part[None] for part in group] for group in groups]


def choose(at_end, inside, after):
    def kernel(a, b, out):
        place = lax.axis_index("gy") // 2
        out[...] = jnp.where((place == 0) | (place == 3), a[...], b[...])

    return call(kernel, plain(at_end, inside), [(sds(inside.shape, inside.dtype), VMEM)], "choose", cost=2.3, after=after)[0]


def bit_of(axis, bit):
    return (lax.axis_index(axis) // bit) % 2


def call(kernel, ins, outs, name, grid=None, scratch=(), cost=4.0, after=()):
    limit = CFG["limits"].get(name, CFG["limit"]) if lax.axis_size("gy") == 8 else VMEM_LIMIT
    specs = [spec for _, spec in ins] + [pl.BlockSpec(memory_space=pl.ANY)] * len(after)
    count = len(ins)

    def body(*refs):
        kernel(*refs[:count], *refs[count + len(after) :])

    return pl.pallas_call(
        body,
        grid=grid or (),
        in_specs=specs,
        out_specs=tuple(spec for _, spec in outs),
        out_shape=tuple(shape for shape, _ in outs),
        scratch_shapes=list(scratch),
        compiler_params=pltpu.CompilerParams(vmem_limit_bytes=limit * 2**20),
        cost_estimate=pl.CostEstimate(flops=int(cost * 1e8), bytes_accessed=int(cost * 3e5), transcendentals=0),
        name=name,
    )(*[array for array, _ in ins], *after)


VMEM = pl.BlockSpec(memory_space=pltpu.VMEM)


def plain(*arrays):
    return [(a, VMEM) for a in arrays]


def fixed(array):
    zeros = (0,) * len(array.shape)
    return (array, pl.BlockSpec(tuple(array.shape), lambda h: zeros, pipeline_mode=pl.Buffered(1)))


def lead(array, first=0):
    zeros = (0,) * (len(array.shape) - 1)
    return (array, pl.BlockSpec((1,) + tuple(array.shape[1:]), lambda h: (first + h,) + zeros))


def lanes(array, first=0, width=PAIR):
    return (array, pl.BlockSpec((array.shape[0], width), lambda h: (0, first + h)))


def half_mask(rows):
    return lax.broadcasted_iota(jnp.int32, (rows, PAIR), 1) < HEAD_DIM


def only_half(x, head):
    low_half = half_mask(x.shape[0])
    zero = jnp.zeros_like(x)
    return jnp.where(low_half, x, zero) if head == 0 else jnp.where(low_half, zero, x)


def merge_halves(first, second):
    rows = first.shape[0]
    return jnp.where(half_mask(rows), jnp.broadcast_to(first, (rows, PAIR)), jnp.broadcast_to(second, (rows, PAIR)))


def normalise(x):
    centered = x - jnp.mean(x, axis=1, keepdims=True)
    scale = lax.rsqrt(jnp.mean(centered * centered, axis=1, keepdims=True) + EPS)
    return centered * scale, scale


def norm_back(grad, unit_rows, scale, gain):
    g = grad * gain
    inner = jnp.mean(g * unit_rows, axis=1, keepdims=True)
    rows = scale * (g - jnp.mean(g, axis=1, keepdims=True) - unit_rows * inner)
    return rows, jnp.sum(grad * unit_rows, axis=0, keepdims=True), jnp.sum(grad, axis=0, keepdims=True)


def stack_heads(x):
    low_half = half_mask(x.shape[0])
    zero = jnp.zeros_like(x)
    return jnp.concatenate([jnp.where(low_half, x, zero), jnp.where(low_half, zero, x)], axis=0)


def unstack_heads(x):
    rows = x.shape[0] // 2
    return merge_halves(x[:rows], x[rows:])


def twice(x):
    return jnp.concatenate([x, x], axis=0)


def pair_lanes(ref, pair):
    return ref[:, pl.ds(pl.multiple_of(pair * PAIR, PAIR), PAIR)]


def group_blocks(block_refs):
    flat = [(ref, i) for ref in block_refs for i in range(ref.shape[0])]
    return [flat[i : i + 8] for i in range(0, len(flat), 8)]


def key_marks(ref, index, key_rows):
    marks = ref[index, key_rows : key_rows + MARKS, 0:256].astype(F32)
    return marks[0:1, 0:1], marks[0:1, 128:129]


def key_bias(group, key_rows):
    width = len(group) * key_rows
    lane = lax.broadcasted_iota(jnp.int32, (1, width), 1).astype(F32)
    bias = jnp.full((1, width), NEG, F32)
    for place, (ref, index) in enumerate(group):
        count, live = key_marks(ref, index, key_rows)
        local = lane - float(place * key_rows)
        good = (local >= 0.0) & (local < count)
        rim = (local >= float(SHARED)) & (local < float(key_rows)) & (live > 0.5)
        bias = jnp.where(good | rim, 0.0, bias)
    return bias


def key_bias_column(group, key_rows):
    parts = []
    for ref, index in group:
        count, live = key_marks(ref, index, key_rows)
        place = lax.broadcasted_iota(jnp.int32, (key_rows, 1), 0).astype(F32)
        good = (place < count) | ((place >= float(SHARED)) & (live > 0.5))
        parts.append(jnp.where(good, 0.0, NEG))
    return jnp.concatenate(parts, axis=0)


def position_table(width):
    unit_width = width // 16
    table = np.zeros((128, width), np.float32)
    bands = [(0, 8, 0, 4 * unit_width), (8, GRID_SIDE, 4 * unit_width, 6 * unit_width)]
    bands.append((64, GRID_SIDE, 10 * unit_width, 6 * unit_width))
    for row, count, lane, band in bands:
        half = band // 2
        power = np.arange(half, dtype=np.float32) / np.float32(half)
        omegas = np.float32(1.0) / np.power(np.float32(10000.0), power)
        angles = (np.arange(count, dtype=np.float32)[:, None] * omegas[None]).astype(np.float64)
        table[row : row + count, lane : lane + half] = np.sin(angles)
        table[row : row + count, lane + half : lane + band] = np.cos(angles)
    high = table.astype(jnp.bfloat16)
    low = (table - high.astype(np.float32)).astype(jnp.bfloat16)
    return jnp.asarray(high), jnp.asarray(low)


def embed_kernel(pix, weight, frame, cell, halo, high, low, gain, bias, stream_ref, rim_ref, low_ref):
    rows = pix.shape[0]
    code = lax.broadcasted_iota(jnp.int32, (128, rows), 0)
    first, second = cell[0:1, :], cell[1:2, :]
    hot = (code == frame[...]) | (code == first + 8) | (code == second + 64)
    hot = jnp.where(hot, 1.0, 0.0).astype(BF16)
    stream = dot(pix[...], weight[...]) + (dot_tn(hot, high[...]) + dot_tn(hot, low[...]))
    stream_ref[...] = stream
    place = lax.broadcasted_iota(jnp.int32, (rows, halo.shape[1]), 0)
    pick = jnp.where(place == halo[...], 1.0, 0.0).astype(BF16)
    rim_ref[...] = dot_tn(pick, stream.astype(BF16)).astype(BF16)
    unit_rows, _ = normalise(stream)
    low_ref[...] = (unit_rows * gain[...] + bias[...]).astype(BF16)


def unit_kernel(own, arrived, gain, bias, ids, live, unit_ref, joined_ref):
    rows, width = own.shape
    rim = arrived.shape[0]
    unit_rows, _ = normalise(arrived[...].astype(F32))
    rim_low = (unit_rows * gain[...] + bias[...]).astype(BF16)
    joined_ref[0:rows, :] = own[...]
    joined_ref[rows : rows + rim, :] = rim_low
    unit_ref[0:SHARED, :] = own[0:SHARED, :]
    unit_ref[SHARED : SHARED + rim, :] = rim_low
    count = jnp.sum(jnp.where(ids[...] == 0, 1.0, 0.0), axis=1, keepdims=True)
    lane = lax.broadcasted_iota(jnp.int32, (MARKS, width), 1)
    unit_ref[SHARED + rim :, :] = jnp.where(lane < 128, count, live[0:1, 0:1]).astype(BF16)


def attend_kernel(n_blocks, key_rows, first, last, *refs):
    refs = list(refs)

    def take(n):
        out = refs[:n]
        del refs[:n]
        return out

    block_refs = take(n_blocks)
    wk_ref, wv_ref, bias_ref = take(3)
    if first:
        own_ref, wq_ref, idr_ref = take(3)
    else:
        q_ref, acc_in, stat_in = take(3)
        if last:
            out_in, lse_in = take(2)
    idc_ref = take(1)[0]
    kv_ref = take(1)[0]
    if first:
        q_ref, kvown_ref = take(2)
        if not last:
            out_ref, lse_ref = take(2)
    if last:
        mixed_ref, full_lse_ref = take(2)
    else:
        acc_ref, stat_ref = take(2)
    pair = pl.program_id(0)
    own_rows = idc_ref.shape[0]
    groups = group_blocks(block_refs)
    biases = [key_bias_column(group, key_rows) for group in groups]
    here = pl.ds(pl.multiple_of(pair * PAIR, PAIR), PAIR)
    wkv = jnp.concatenate([wk_ref[...], wv_ref[...]], axis=1)
    shift = pair_lanes(bias_ref, PAIRS + pair)
    shift = jnp.concatenate([jnp.zeros_like(shift), shift], axis=1)
    base = 0
    for group in groups:
        for ref, index in group:
            kv_ref[0, base : base + key_rows, :] = (dot(ref[index, 0:key_rows, :], wkv) + shift).astype(BF16)
            base += key_rows
    if first:
        kvown_ref[0] = (dot(own_ref[...], wkv) + shift).astype(BF16)
        q = (dot(own_ref[0:own_rows, :], wq_ref[...]) + pair_lanes(bias_ref, pair)).astype(BF16) * BF16(SCALE)
        q_ref[0] = q
    else:
        q = q_ref[0]
    qs = stack_heads(q[0:SHARED])
    if first:
        peak = weight = total = None
    else:
        total = acc_in[0]
        peak, weight = stat_in[0, 0:1, :], stat_in[0, 8:9, :]
    base = 0
    for group, bias in zip(groups, biases):
        width = len(group) * key_rows
        span = slice(base, base + width)
        keys, values = kv_ref[0, span, 0:PAIR], kv_ref[0, span, PAIR:]
        base += width
        scores = dot_nt(keys, qs) + bias
        new = jnp.max(scores, axis=0, keepdims=True)
        if peak is not None:
            new = jnp.maximum(peak, new)
        probs = jnp.exp(scores - new)
        sums = jnp.sum(probs, axis=0, keepdims=True)
        part = dot_tn(values, probs.astype(BF16))
        if peak is None:
            weight, total = sums, part
        else:
            fade = jnp.exp(peak - new)
            weight = weight * fade + sums
            total = total * fade + part
        peak = new
    if first:
        idc = idc_ref[...]
        allowed = twice((idc == idr_ref[...]) & (idc != 0))
        scores = jnp.where(allowed, dot_nt(stack_heads(q), kvown_ref[0, 0:own_rows, 0:PAIR]), NEG)
        top = jnp.max(scores, axis=1, keepdims=True)
        probs = jnp.exp(scores - top)
        local_weight = jnp.sum(probs, axis=1, keepdims=True)
        local_out = unstack_heads(dot(probs.astype(BF16), kvown_ref[0, 0:own_rows, PAIR:]) / local_weight)
        local_lse = unstack_heads(top + jnp.log(local_weight))
        if not last:
            out_ref[:, here] = local_out
            lse_ref[:, here] = local_lse
    elif last:
        local_out, local_lse = out_in[:, here], lse_in[:, here]
    if last:
        shared_row = idc_ref[0:SHARED, :] == 0
        shared_out = unstack_heads((total / weight).T)
        shared_lse = unstack_heads(jnp.broadcast_to(peak + jnp.log(weight), (8, 2 * SHARED)).T[:, 0:1])
        mixed_ref[0:SHARED, here] = jnp.where(shared_row, shared_out, local_out[0:SHARED])
        mixed_ref[SHARED:, here] = local_out[SHARED:]
        full_lse_ref[0:SHARED, here] = jnp.where(shared_row, shared_lse, local_lse[0:SHARED])
        full_lse_ref[SHARED:, here] = local_lse[SHARED:]
    else:
        acc_ref[0] = total
        stat_ref[0, 0:8, :] = jnp.broadcast_to(peak, (8, 2 * SHARED))
        stat_ref[0, 8:16, :] = jnp.broadcast_to(weight, (8, 2 * SHARED))


class Attention:
    def __init__(self, first_low, weights, project_bias, idc, idr, key_rows):
        self.fixed = first_low, weights, project_bias, idc, idr
        self.key_rows = key_rows
        self.kvs = []

    def piece(self, blocks, last):
        first_low, weights, project_bias, idc, idr = self.fixed
        key_rows = self.key_rows
        own_rows, width = idc.shape[0], first_low.shape[1]
        wide = lambda rows: (sds((rows, width), F32), pl.BlockSpec((rows, width), lambda h: (0, 0)))
        deep = lambda rows, lane, dtype: (
            sds((PAIRS, rows, lane), dtype),
            pl.BlockSpec((1, rows, lane), lambda h: (h, 0, 0)),
        )
        first = not self.kvs
        keys = sum(b.shape[0] for b in blocks) * key_rows
        ins = [fixed(b) for b in blocks] + [lanes(weights, PAIRS), lanes(weights, 2 * PAIRS), fixed(project_bias)]
        if first:
            ins += [fixed(first_low), lanes(weights), fixed(idr)]
        else:
            ins += [lead(self.q)] + [lead(s) for s in self.state]
            if last:
                ins += [fixed(x) for x in self.local]
        ins += [fixed(idc)]
        outs = [deep(keys, 2 * PAIR, BF16)]
        if first:
            outs += [deep(own_rows, PAIR, BF16), deep(first_low.shape[0], 2 * PAIR, BF16)]
            if not last:
                outs += [wide(own_rows)] * 2
        outs += [wide(own_rows)] * 2 if last else [deep(PAIR, 2 * SHARED, F32), deep(16, 2 * SHARED, F32)]
        kernel = functools.partial(attend_kernel, len(blocks), key_rows, first, last)
        got = list(call(kernel, ins, outs, "attend", grid=(PAIRS,), cost=3.0 + keys / 90.0))
        self.kvs.append(got.pop(0))
        if first:
            self.q, self.kvown = got.pop(0), got.pop(0)
            if not last:
                self.local = [got.pop(0), got.pop(0)]
        self.state = got
        return (got[0],)


def erf(x):
    x = jnp.clip(x, -3.832506856900711, 3.832506856900711)
    s = x * x
    top = -2.72614225801306e-10
    for c in (2.77068142495902e-08, -2.10102402082508e-06, -5.69250639462346e-05, -7.34990630326855e-04, -2.95459980854025e-03, -1.60960333262415e-02):
        top = top * s + c
    low = -1.45660718464996e-05
    for c in (-2.13374055278905e-04, -1.68282697438203e-03, -7.37332916720468e-03, -1.42647390514189e-02):
        low = low * s + c
    return x * top / low


def middle_kernel(
    mixed, lse, stream, mlp_grad, act_grad, idc,
    w_output, merge_bias, gain, bias, w_up, up_bias, w_down, down_bias, w_head,
    predicted, act_ref, pre_ref, second_ref, mixed_low_ref, attn_low_ref, final_ref, attn_ref, grad_ref, unit_ref,
    stat_ref, up_sum, gain_sum, bias_sum, merge_sum,
):
    rows, width = mixed.shape
    hidden = w_up.shape[1]
    mixed_low = mixed[...].astype(BF16)
    mixed_low_ref[...] = mixed_low
    after = stream[...] + dot(mixed_low, w_output[...]) + merge_bias[...]
    unit_rows, scale = normalise(after)
    second = (unit_rows * gain[...] + bias[...]).astype(BF16)
    second_ref[...] = second
    out = after + down_bias[...]
    back = jnp.zeros((rows, width), F32)
    step = 768
    for start in range(0, hidden, step):
        part = slice(start, start + step)
        pre = dot(second, w_up[:, part]) + up_bias[:, part]
        cdf = 0.5 + 0.5 * erf(pre * 0.7071067811865476)
        act = (pre * cdf).astype(BF16)
        act_ref[:, part] = act
        slope = cdf + pre * (0.3989422804014327 * jnp.exp(-0.5 * pre * pre))
        grad = (act_grad[:, part] * slope).astype(BF16)
        pre_ref[:, part] = grad
        up_sum[:, part] = jnp.sum(grad.astype(F32), axis=0, keepdims=True)
        out += dot(act, w_down[part, :])
        back += dot_nt(grad, w_up[:, part])
    resid, gain_part, bias_part = norm_back(back, unit_rows, scale, gain[...])
    gain_sum[...] = gain_part
    bias_sum[...] = bias_part
    attn = mlp_grad[...] + resid
    attn_ref[...] = attn
    merge_sum[...] = jnp.sum(attn, axis=0, keepdims=True)
    attn_low = attn.astype(BF16)
    attn_low_ref[...] = attn_low
    grad = dot_nt(attn_low, w_output[...]).astype(BF16)
    grad_ref[...] = grad
    shared_row = idc[0:SHARED, :] == 0
    unit_ref[0:SHARED, :] = jnp.where(shared_row, grad[0:SHARED], jnp.zeros((SHARED, width), BF16))
    lane = lax.broadcasted_iota(jnp.int32, (MARKS, width), 1)
    head = lax.broadcasted_iota(jnp.int32, (MARKS, width), 0)
    ones = jnp.where(lane // HEAD_DIM == head, 1.0, 0.0)
    pick = jnp.where(lane == head * HEAD_DIM, 1.0, 0.0)

    def by_head(chooser, value):
        chooser, high = chooser.astype(BF16), value.astype(BF16)
        return dot_nt(chooser, high) + dot_nt(chooser, (value - high.astype(F32)).astype(BF16))

    delta = by_head(ones, grad.astype(F32) * mixed[...])
    turned = by_head(pick, lse[...])
    stat_ref[0] = turned
    stat_ref[1] = delta
    zeros = jnp.zeros((rows, 128), F32)
    ids = jnp.where(idc[...] == 0, 1.0, 0.0) + zeros
    row_ids = dot_nt(jnp.full((MARKS, 128), 1.0 / 128, F32), ids)
    shared_lane = row_ids[:, 0:SHARED] > 0.5
    sent = []
    for value, other in ((turned, -NEG), (delta, 0.0)):
        value = jnp.where(shared_lane, value[:, 0:SHARED], other)
        high = value.astype(BF16)
        sent += [high, (value - high.astype(F32)).astype(BF16)]
    unit_ref[SHARED:, :] = jnp.concatenate(sent, axis=1)
    final = out.astype(BF16)
    final_ref[...] = final
    predicted[...] = dot(final, w_head[...]).astype(BF16)


def query_kernel(n_blocks, n_kvs, key_rows, first, *refs):
    block_refs, kv_refs = refs[:n_blocks], refs[n_blocks : n_blocks + n_kvs]
    kvown_ref, q_ref, wq_ref, grad_ref, mixed_ref, lse_ref, bias_ref, idc_ref, idr_ref = refs[
        n_blocks + n_kvs : n_blocks + n_kvs + 9
    ]
    dq_ref, qall_ref = refs[-2:]
    pair = first + pl.program_id(0)
    own_rows = idc_ref.shape[0]
    flat = [(ref, i) for ref in block_refs for i in range(ref.shape[0])]
    base = 0
    wq, shift = wq_ref[...], pair_lanes(bias_ref, pair)
    for ref, index in flat:
        rows = (dot(ref[index, 0:SHARED, :], wq) + shift).astype(BF16)
        qall_ref[0, base : base + SHARED, :] = rows * BF16(SCALE)
        base += SHARED
    idc = idc_ref[...]
    allowed = twice((idc == idr_ref[...]) & (idc != 0))
    shared_row = idc == 0
    q = q_ref[0]
    grad = pair_lanes(grad_ref, pair)
    product = stack_heads(grad.astype(F32) * pair_lanes(mixed_ref, pair))
    delta = jnp.sum(product, axis=1, keepdims=True)
    lse = pair_lanes(lse_ref, pair)
    lse = jnp.concatenate([lse[:, 0:1], lse[:, HEAD_DIM : HEAD_DIM + 1]], axis=0)
    qm, gm = stack_heads(q), stack_heads(grad)
    part_rows = lambda x: jnp.concatenate([x[0:SHARED], x[own_rows : own_rows + SHARED]], axis=0)
    qs, gs, delta_s, lse_s = part_rows(qm), part_rows(gm), part_rows(delta), part_rows(lse)
    total, used = None, 0
    for kv_ref in kv_refs:
        count = kv_ref.shape[1] // key_rows
        for start in range(0, count, 8):
            size = min(8, count - start)
            bias = key_bias(flat[used : used + size], key_rows)
            used += size
            span = slice(start * key_rows, (start + size) * key_rows)
            keys = kv_ref[0, span, 0:PAIR]
            values = kv_ref[0, span, PAIR:]
            probs = jnp.exp(dot_nt(qs, keys) + bias - lse_s)
            ds = (probs * (dot_nt(gs, values) - delta_s)).astype(BF16)
            part = dot(ds, keys)
            total = part if total is None else total + part
    keys, values = kvown_ref[0, 0:own_rows, 0:PAIR], kvown_ref[0, 0:own_rows, PAIR:]
    probs = jnp.exp(jnp.where(allowed, dot_nt(qm, keys) - lse, NEG))
    ds = (probs * (dot_nt(gm, values) - delta)).astype(BF16)
    local = unstack_heads(dot(ds, keys)) * SCALE
    shared = jnp.where(shared_row[0:SHARED], unstack_heads(total) * SCALE, local[0:SHARED])
    here = pl.ds(pl.multiple_of(pl.program_id(0) * PAIR, PAIR), PAIR)
    dq_ref[0:SHARED, here] = shared.astype(BF16)
    dq_ref[SHARED:, here] = local[SHARED:].astype(BF16)


def query_back(groups, kvs, kvown, q, mixed_grad, mixed, lse, wq, project_bias, idc, idr, key_rows, first, pairs, after):
    own_rows = idc.shape[0]
    blocks = [b for group in groups for b in group]
    count = sum(b.shape[0] for b in blocks)
    ins = [fixed(b) for b in blocks] + [lead(kv, first) for kv in kvs] + [lead(x, first) for x in (kvown, q)] + [lanes(wq, first)]
    ins += [fixed(x) for x in (mixed_grad, mixed, lse, project_bias, idc, idr)]
    outs = [
        (sds((own_rows, pairs * PAIR), BF16), pl.BlockSpec((own_rows, pairs * PAIR), lambda h: (0, 0))),
        (sds((pairs, count * SHARED, PAIR), BF16), pl.BlockSpec((1, count * SHARED, PAIR), lambda h: (h, 0, 0))),
    ]
    kernel = functools.partial(query_kernel, len(blocks), len(kvs), key_rows, first)
    return call(kernel, ins, outs, "query_back", grid=(pairs,), cost=4.2 * pairs, after=after)


def key_kernel(n_blocks, first, *refs):
    grad_refs = refs[:n_blocks]
    kvown_ref, qall_ref, q_ref, grad_ref, own_stat_ref, idc_ref, idr_ref, live_ref = refs[n_blocks : n_blocks + 8]
    dk_ref, dv_ref, grads_ref, stats_ref = refs[n_blocks + 8 :]
    pair = first + pl.program_id(0)
    own_rows = idc_ref.shape[0]
    rim = kvown_ref.shape[1] - own_rows
    flat = [(ref, i) for ref in grad_refs for i in range(ref.shape[0])]

    @pl.when(pl.program_id(0) == 0)
    def _():
        base = 0
        for begin in range(0, len(flat), 2):
            sums = []
            for ref, i in flat[begin : begin + 2]:
                stat = ref[i, SHARED:, :].astype(F32)
                sums.append(
                    (
                        stat[:, 0:SHARED] + stat[:, SHARED : 2 * SHARED],
                        stat[:, 2 * SHARED : 3 * SHARED] + stat[:, 3 * SHARED :],
                    )
                )
            for kind in range(2):
                stats_ref[kind, :, base : base + 2 * SHARED] = jnp.concatenate([s[kind] for s in sums], axis=1)
            base += 2 * SHARED

    base = 0
    there = pl.ds(pl.multiple_of(pair * PAIR, PAIR), PAIR)
    for ref, i in flat:
        grads_ref[base : base + SHARED, :] = ref[i, 0:SHARED, there]
        base += SHARED
    idc = idc_ref[...]
    allowed = twice((idc == idr_ref[...]) & (idc != 0))
    shared_row = idc == 0
    live = live_ref[0:1, 0:1] > 0.5
    kv = kvown_ref[0]
    k_all, v_all = kv[:, 0:PAIR], kv[:, PAIR:]
    in_shared = lambda x: jnp.concatenate([x[0:SHARED], x[own_rows:]], axis=0)
    q, grad = q_ref[0], pair_lanes(grad_ref, pair)
    n_shared = SHARED + rim
    k_sh, v_sh = stack_heads(in_shared(k_all)), stack_heads(in_shared(v_all))

    def both_rows(ref, kind, rows, columns):
        picked = [ref[kind, pl.ds(2 * pair + head, 1), columns] for head in range(2)]
        return jnp.concatenate([jnp.broadcast_to(p, (rows, p.shape[1])) for p in picked], axis=0)

    dk = dv = None
    chunk = min(base, 1536)
    for start in range(0, base, chunk):
        span = slice(start, start + chunk)
        q_all, g_all = qall_ref[0, span, :], grads_ref[span, :]
        probs = jnp.exp(dot_nt(k_sh, q_all) - both_rows(stats_ref, 0, n_shared, span))
        part_v = dot(probs.astype(BF16), g_all)
        ds = (probs * (dot_nt(v_sh, g_all) - both_rows(stats_ref, 1, n_shared, span))).astype(BF16)
        part_k = dot(ds, q_all)
        dk = part_k if dk is None else dk + part_k
        dv = part_v if dv is None else dv + part_v
    every = slice(None)
    scores = dot_nt(stack_heads(k_all[0:own_rows]), q) - both_rows(own_stat_ref, 0, own_rows, every)
    probs = jnp.exp(jnp.where(allowed, scores, NEG))
    local_v = dot(probs.astype(BF16), grad)
    ds = dot_nt(stack_heads(v_all[0:own_rows]), grad) - both_rows(own_stat_ref, 1, own_rows, every)
    local_k = dot((probs * ds).astype(BF16), q)
    here = pl.ds(pl.multiple_of(pl.program_id(0) * PAIR, PAIR), PAIR)
    for out, shared, local in ((dk_ref, dk, local_k), (dv_ref, dv, local_v)):
        shared, local = unstack_heads(shared), unstack_heads(local)
        out[0:SHARED, here] = jnp.where(shared_row[0:SHARED], shared[0:SHARED], local[0:SHARED]).astype(BF16)
        out[SHARED:own_rows, here] = local[SHARED:].astype(BF16)
        out[own_rows:, here] = jnp.where(live, shared[SHARED:], 0.0).astype(BF16)


def key_back(groups, kvown, qall, q, mixed_grad, own_stats, idc, idr, live, first, pairs, after):
    joined_rows = kvown.shape[1]
    grads = [g for group in groups for g in group]
    ins = [fixed(g) for g in grads] + [lead(kvown, first), lead(qall), lead(q, first)]
    ins += [fixed(x) for x in (mixed_grad, own_stats, idc, idr, live)]
    out = (sds((joined_rows, pairs * PAIR), BF16), pl.BlockSpec((joined_rows, pairs * PAIR), lambda h: (0, 0)))
    scratch = [pltpu.VMEM((qall.shape[1], PAIR), BF16), pltpu.VMEM((2, MARKS, qall.shape[1]), F32)]
    kernel = functools.partial(key_kernel, len(grads), first)
    return call(kernel, ins, [out, out], "key_back", grid=(pairs,), scratch=scratch, cost=3.7 * pairs, after=after)


def input_kernel(dq, dk, dv, weight, stream, arrived, gain, attn_grad, rim_ref, rows_ref, joint_ref, vec_ref):
    own, width = dq.shape
    dq, dk, dv = dq[...], dk[...], dv[...]
    wq, wk, wv = weight[:, 0:width], weight[:, width : 2 * width], weight[:, 2 * width :]
    rim_grad = dot_nt(dk[own:], wk) + dot_nt(dv[own:], wv)
    rim_rows, rim_scale = normalise(arrived[...].astype(F32))
    rim_back, rim_gain, rim_bias = norm_back(rim_grad, rim_rows, rim_scale, gain[...])
    rim_ref[...] = rim_back.astype(BF16)
    own_grad = dot_nt(dq, wq) + dot_nt(dk[:own], wk) + dot_nt(dv[:own], wv)
    own_rows, own_scale = normalise(stream[...])
    own_back, own_gain, own_bias = norm_back(own_grad, own_rows, own_scale, gain[...])
    rows_ref[...] = own_back + attn_grad[...]
    joint_ref[0:own, 0:width] = dq
    joint_ref[own:, 0:width] = jnp.zeros((dk.shape[0] - own, width), BF16)
    joint_ref[:, width : 2 * width] = dk
    joint_ref[:, 2 * width :] = dv
    vec_ref[0:1, :] = own_gain + rim_gain
    vec_ref[1:2, :] = own_bias + rim_bias
    vec_ref[2:3, :] = jnp.sum(dq.astype(F32), axis=0, keepdims=True)
    vec_ref[3:4, :] = jnp.sum(dv.astype(F32), axis=0, keepdims=True)


def pixel_kernel(rows, returned, halo, weight, low_ref, grad_ref):
    place = lax.broadcasted_iota(jnp.int32, (rows.shape[0], halo.shape[1]), 0)
    spread = jnp.where(place == halo[...], 1.0, 0.0).astype(BF16)
    low = (rows[...] + dot(spread, returned[...])).astype(BF16)
    low_ref[...] = low
    grad_ref[...] = dot_nt(low, weight[...]).astype(BF16)


ORDERS = {
    "x": [("gx", 2, None), ("gy", 1, 2), ("gy", 2, 1), ("gy", 4, 0)],
    "y": [("gy", 1, None), ("gy", 2, 1), ("gy", 4, 0)],
    "z": [("gy", 2, None), ("gy", 4, 0), ("gy", 1, 0)],
    "s": [("gy", 1, None)],
    "yx": [("gy", 1, None), ("gx", 2, 2), ("gy", 2, 1), ("gy", 4, 0)],
}


def product_blocks(left, right, core_half, n):
    half = right.shape[1] // 2
    x = left[...]
    for j in range(half // LANES):
        columns = pl.ds(pl.multiple_of(core_half * half + j * LANES, 128), LANES)
        out = dot_tn(x, right[:, columns])
        yield out.reshape(n, out.shape[0] // n, LANES)


def away_kernel(n, n_pairs, *refs):
    pairs, outs = refs[: 2 * n_pairs], refs[2 * n_pairs :]
    other = 1 - lax.axis_index("gx") % 2
    (out,) = outs
    row = 0
    for p in range(n_pairs):
        for block in product_blocks(pairs[2 * p], pairs[2 * p + 1], other, n):
            out[:, row : row + block.shape[1], :] = block.astype(BF16)
            row += block.shape[1]


def home_kernel(n, n_pairs, order, n_small, row, *refs):
    pairs = refs[: 2 * n_pairs]
    arrived = refs[2 * n_pairs]
    small = refs[2 * n_pairs + 1 : 2 * n_pairs + 1 + n_small]
    send, keep = refs[2 * n_pairs + 1 + n_small :][-2:] if order != "s" else (None, refs[-1])
    core = lax.axis_index("gx") % 2
    axis, bit = ORDERS[order][0][:2]
    low = lax.axis_index(axis) // bit % 2 == 0
    half_row = 0

    def put(first, second, start, rows):
        if order == "s":
            for half, value in ((0, first), (1, second)):
                keep[:, half, start : start + rows, :] = value
            return
        if order == "x":
            span = slice(start, start + rows)
            send[:, span, :] = jnp.where(low, second, first)
            keep[:, span, :] = jnp.where(low, first, second)
            return
        for half, value in ((0, first), (1, second)):
            span = slice(start, start + rows)
            value = value.reshape(n // 2 // bit, 2, bit, rows, LANES)
            for out, one, other in ((send, value[:, 1], value[:, 0]), (keep, value[:, 0], value[:, 1])):
                out[:, half, span, :] = jnp.where(low, one, other).reshape(n // 2, rows, LANES)

    for p in range(n_pairs):
        for block in product_blocks(pairs[2 * p], pairs[2 * p + 1], core, n):
            r = block.shape[1]
            block = (block + arrived[:, row : row + r, :].astype(F32)).astype(BF16)
            put(block[:, : r // 2], block[:, r // 2 :], half_row, r // 2)
            row += r
            half_row += r // 2
    if n_small:
        value = small[0][...] + small[1][...]
        put(value, jnp.zeros(value.shape, BF16), half_row, value.shape[1])


def away(pairs, n, name, after=()):
    arrays = [x for pair in pairs for x in pair]
    rows = sum(b.shape[1] // 2 // LANES * a.shape[1] // n for a, b in pairs)
    outs = [(sds((n, rows, LANES), BF16), VMEM)]
    return call(functools.partial(away_kernel, n, len(pairs)), plain(*arrays), outs, name, cost=rows / 135.0, after=after)[0]


def home(pairs, n, arrived, order, name, small=(), first_row=0, after=()):
    arrays = [x for pair in pairs for x in pair] + [arrived] + list(small)
    rows = sum(b.shape[1] // 2 // LANES * a.shape[1] // n // 2 for a, b in pairs)
    rows += small[0].shape[1] if small else 0
    shape = (n, rows, LANES) if order == "x" else (n // 2, 2, rows, LANES)
    kernel = functools.partial(home_kernel, n, len(pairs), order, len(small), first_row)
    if order == "s":
        outs = [(sds((n, 2, rows, LANES), BF16), VMEM)]
        whole = call(kernel, plain(*arrays), outs, name, after=after)[0]
        return whole, lax.psum_scatter(whole, "gy", scatter_dimension=0, tiled=False)
    outs = [(sds(shape, BF16), VMEM)] * 2
    send, keep = call(kernel, plain(*arrays), outs, name, after=after)
    got = swap(send, *ORDERS[order][0][:2])
    shape = ((2, 2, 2) if order == "x" else (2, 2)) + keep.shape[1:]
    return send, (keep.reshape(shape), got.reshape(shape))


def next_step(group, axis, bit, dim):
    keep, got = group
    mine = bit_of(axis, bit)
    pick = lambda x, i: lax.dynamic_index_in_dim(x, i, dim, keepdims=False)
    send = pick(keep, 1 - mine) + pick(got, 1 - mine)
    return send, (pick(keep, mine) + pick(got, mine), swap(send, axis, bit))


def held_step(group, axis, bit, dim, after):
    keep, got = group
    shape = keep.shape[:dim] + keep.shape[dim + 1 :]

    def kernel(keep, got, send, left):
        mine = lax.axis_index(axis) // bit % 2
        for out, side in ((send, 1 - mine), (left, mine)):
            index = (slice(None),) * dim + (side,)
            out[...] = keep[index] + got[index]

    send, left = call(kernel, plain(keep, got), [(sds(shape, BF16), VMEM)] * 2, "step", after=after)
    return send, (left, swap(send, axis, bit))


def all_of(group):
    part = group[0] + group[1] if isinstance(group, tuple) else group
    x_low, core_low = bit_of("gx", 2) == 0, bit_of("gx", 1) == 0
    over = swap(part, "gx", 2)
    if part.ndim == 3:
        both = part + over
    else:
        both = jnp.stack([jnp.where(x_low, part, over), jnp.where(x_low, over, part)])
    across = swap(both, "gx", 1)
    return [jnp.where(core_low, both, across), jnp.where(core_low, across, both)]


def cut(sides, pairs, n):
    outs, start = [], 0
    for a, b in pairs:
        r, blocks = a.shape[1] // n, b.shape[1] // 2 // LANES
        halves = []
        for side in sides:
            piece = side[:, start : start + blocks * r // 2].reshape(2, blocks, r // 2, LANES)
            halves.append(piece.transpose(0, 2, 1, 3).reshape(r, blocks * LANES))
        start += blocks * r // 2
        outs.append(jnp.concatenate(halves, axis=1).astype(F32))
    return outs, [side[0, start:].astype(F32) for side in sides]


def shards(
    pixels,
    frame_index,
    patch_cell,
    tile_id,
    halo_index,
    w_patch,
    first_gain,
    first_bias,
    w_project,
    project_bias,
    w_output,
    merge_bias,
    second_gain,
    second_bias,
    w_up,
    up_bias,
    w_down,
    down_bias,
    w_head,
    cotangent,
):
    n_gx, n_gy = lax.axis_size("gx"), lax.axis_size("gy")
    own, rim = pixels.shape[0], halo_index.shape[0]
    width, hidden, depth = w_output.shape[0], w_up.shape[1], pixels.shape[1]
    key_rows = SHARED + rim
    idc, idr = tile_id.reshape(own, 1), tile_id.reshape(1, own)
    live = jnp.broadcast_to(jnp.where(lax.axis_index("gx") > 0, 1.0, 0.0).astype(F32), (8, 128))
    halo = halo_index.reshape(1, rim)
    row = lambda v: v.reshape(1, -1)
    mat = lambda rows, columns, dtype: (sds((rows, columns), dtype), VMEM)

    high, low = position_table(width)
    stream, outgoing, own_low = call(
        embed_kernel,
        plain(
            pixels, w_patch, row(frame_index), patch_cell, halo, high, low, row(first_gain), row(first_bias)
        ),
        [mat(own, width, F32), mat(rim, width, BF16), mat(own, width, BF16)],
        "embed",
    )
    arrived = shifted(outgoing, "gx", 1)
    unit, first_low = call(
        unit_kernel,
        plain(own_low, arrived, row(first_gain), row(first_bias), idr, live),
        [mat(key_rows + MARKS, width, BF16), mat(own + rim, width, BF16)],
        "unit",
        cost=2.4,
    )
    column = ColumnGather(unit)
    shift = row(project_bias)
    attention = Attention(first_low, w_project, shift, idc, idr, key_rows)
    if column.direct:
        column.second()
        if CFG["early"]:
            after = attention.piece([unit[None], column.near[None]], False)
            column.third(after)
            column.fourth((column.far,))
            attention.piece(column.groups[1], False)
            attention.piece(column.groups[2], True)
        else:
            after = attention.piece([unit[None], column.near[None], column.y0[None]], False)
            column.third(after)
            after = attention.piece([column.y1[None], column.far[None]], False)
            column.fourth(after)
            attention.piece([column.last[None], column.y2[None], column.y3[None]], True)
    else:
        attention.piece(column.groups[0], True)
    groups, kvs, kvown, q = column.groups, attention.kvs, attention.kvown, attention.q
    mixed, lse = attention.state

    mlp_grad = dot_nt(cotangent, w_head)
    down_bias_grad = jnp.sum(mlp_grad, axis=0)
    mlp_low = mlp_grad.astype(BF16)
    act_grad = dot_nt(mlp_low, w_down)
    (
        predicted, act_low, pre_grad, second_low, mixed_low, attn_low, final_low, attn_grad, mixed_grad, grad_unit,
        own_stats, up_sum, second_gain_sum, second_bias_sum, merge_sum,
    ) = call(
        middle_kernel,
        plain(
            mixed, lse, stream, mlp_grad, act_grad, idc, w_output, row(merge_bias), row(second_gain),
            row(second_bias), w_up, row(up_bias), w_down, row(down_bias), w_head,
        ),
        [mat(own, depth, BF16), mat(own, hidden, BF16), mat(own, hidden, BF16)]
        + [mat(own, width, BF16)] * 4
        + [mat(own, width, F32), mat(own, width, BF16), mat(SHARED + MARKS, width, BF16)]
        + [(sds((2, MARKS, own), F32), VMEM), mat(1, hidden, F32)]
        + [mat(1, width, F32)] * 3,
        "middle",
        cost=18.0,
    )
    special = n_gx == 4 and n_gy == 8
    head_pair, down_pair = (final_low, cotangent), (act_low, mlp_low)
    up_pair, output_pair = (second_low, pre_grad), (mixed_low, attn_low)
    gather = (DirectGather if CFG["direct"] else FreeGather)(grad_unit)
    early_a, early_b = [head_pair, down_pair], [up_pair, output_pair]
    q_parts, k_parts = [], []

    def query_piece(first, pairs, after):
        part = query_back(
            groups, kvs, kvown, q, mixed_grad, mixed, lse, w_project, shift, idc, idr, key_rows, first, pairs, after
        )
        q_parts.append(part)
        return (part[0],)

    def key_piece(place, first, pairs, after):
        qall = jnp.concatenate([p[1] for p in q_parts], axis=0) if CFG["qp"] != CFG["kp"] else q_parts[place][1]
        part = key_back(gather.groups, kvown, qall, q, mixed_grad, own_stats, idc, idr, live, first, pairs, after)
        k_parts.append(part)
        return (part[0],)

    after = ()
    if special:
        if CFG["merged"]:
            share_a = share_b = away(early_a + early_b, n_gy, "away")
            gone_a = gone_b = swap(share_a, "gx", 1)
        else:
            share_a, share_b = away(early_a, n_gy, "away"), away(early_b, n_gy, "away")
            gone_a, gone_b = swap(share_a, "gx", 1), swap(share_b, "gx", 1)
        after = (share_a, share_b) if CFG["away_first"] else ()

    def homes(after):
        gate = CFG["gate"]
        if gate >= 1:
            after += (gather.near, gather.mid, gather.y0)
        if gate >= 3:
            after += (gather.far_end, gather.far_mid, gather.y1)
        if CFG["sc"]:
            send, group = home(early_a + early_b, n_gy, gone_a, "s", "home", after=after)
            return (send,), group, None
        send_a, group_a = home(early_a, n_gy, gone_a, "x", "home", after=after)
        after += (send_a,)
        if gate >= 2:
            after += (gather.far_end, gather.far_mid, gather.y1)
        if gate >= 3:
            after += (gather.last_end, gather.y2)
        first_row = 2 * group_a[0].shape[-2] if CFG["merged"] else 0
        send_b, group_b = home(early_b, n_gy, gone_b, CFG["b"], "home", first_row=first_row, after=after)
        return (send_a, send_b), group_a, group_b

    def second_steps(group_a, group_b, after):
        send_a, group_a = held_step(group_a, *ORDERS["x"][1], after)
        send_b, group_b = held_step(group_b, *ORDERS[CFG["b"]][1], after + (send_a,))
        return (send_a, send_b), group_a, group_b

    done_a = done_b = 1
    first = 0
    for i, size in enumerate(CFG["qp"]):
        after = query_piece(first, size, after)
        first += size
        if special and CFG["home"] == i:
            more, group_a, group_b = homes(after)
            after += more
    first = 0
    for i, size in enumerate(CFG["kp"]):
        part = key_piece(i, first, size, after)
        after = part
        first += size
        if special and CFG["ab2"] == i:
            more, group_a, group_b = second_steps(group_a, group_b, after)
            after += more
            done_a = done_b = 2
    dq = jnp.concatenate([p[0] for p in q_parts], axis=1)
    dk = jnp.concatenate([p[0] for p in k_parts], axis=1)
    dv = jnp.concatenate([p[1] for p in k_parts], axis=1)
    rim_grad, partial, joint_grad, first_sums = call(
        input_kernel,
        plain(dq, dk, dv, w_project, stream, arrived, row(first_gain), attn_grad),
        [mat(rim, width, BF16), mat(own, width, F32), mat(own + rim, 3 * width, BF16), mat(8, width, F32)],
        "input",
        cost=6.0,
        after=after,
    )
    returned = shifted(rim_grad, "gx", -1)
    project_pair = (first_low, joint_grad)
    after = ()
    if special:
        share_c = away([project_pair], n_gy, "away")
        gone_c = swap(share_c, "gx", 1)
        after = ()
        if CFG["ab2"] == "c":
            after, group_a, group_b = second_steps(group_a, group_b, (share_c,))
            done_a = done_b = 2
    embed_low, pixel_grad = call(
        pixel_kernel,
        plain(partial, returned, halo, w_patch),
        [mat(own, width, BF16), mat(own, depth, BF16)],
        "pixel",
        cost=3.0,
        after=after if special else (),
    )
    patch_pair = (pixels, embed_low)

    vectors = [
        first_sums[0],
        first_sums[1],
        first_sums[2:4].reshape(-1),
        merge_sum[0],
        second_gain_sum[0],
        second_bias_sum[0],
        up_sum[0],
        down_bias_grad,
    ]
    sizes = [v.shape[0] // n_gy for v in vectors]
    if special:
        core = bit_of("gx", 1)
        small = jnp.stack([jnp.pad(v.reshape(n_gy, z), ((0, 0), (0, LANES - z))) for v, z in zip(vectors, sizes)], axis=1)
        small = jnp.pad(small.astype(BF16).reshape(n_gy, 2, 4, LANES), ((0, 0), (0, 0), (0, MARKS - 4), (0, 0)))
        small_mine = lax.dynamic_index_in_dim(small, core, 1, keepdims=False)
        small_gone = swap(lax.dynamic_index_in_dim(small, 1 - core, 1, keepdims=False), "gx", 1)
        share_d = away([patch_pair], n_gy, "away")
        gone_d = swap(share_d, "gx", 1)
        send_c, group_c = home([project_pair], n_gy, gone_c, CFG["c"], "home", after=(share_d,) if CFG["chain"] in (True, "s") else ())
        send_d, group_d = home(
            [patch_pair], n_gy, gone_d, CFG["d"], "home", small=[small_mine, small_gone], after=(send_c,) if CFG["chain"] in (True, "d") else ()
        )
        if CFG["ab3"] and done_a == 2:
            send_a, group_a = held_step(group_a, *ORDERS["x"][2], (send_d,))
            send_b, group_b = held_step(group_b, *ORDERS[CFG["b"]][2], (send_d,))
            done_a = done_b = 3
        if CFG["join"]:

            def joined(groups, orders):
                groups = [next_step(group, *ORDERS[order][1])[1] for group, order in zip(groups, orders)]
                for axis, bit, dim in ORDERS["x"][2:]:
                    mine = bit_of(axis, bit)
                    pick = lambda x, i: lax.dynamic_index_in_dim(x, i, dim, keepdims=False)
                    put = lambda i: jnp.concatenate([pick(k, i) + pick(g, i) for k, g in groups], axis=-2)
                    groups = [(put(mine), swap(put(1 - mine), axis, bit))]
                return all_of(groups[0])

            sides = joined([group_a, group_b], ["x", CFG["b"]])
            (head_grad, down_grad, up_grad, output_grad), _ = cut(sides, early_a + early_b, n_gy)
            sides = joined([group_c, group_d], [CFG["c"], CFG["d"]])
            (project_grad, patch_grad), marks = cut(sides, [project_pair, patch_pair], n_gy)
            groups = None
        else:
            groups = []
            for group, hops in (
                *(((group_a, ()),) if CFG["sc"] else ((group_a, ORDERS["x"][done_a:]), (group_b, ORDERS[CFG["b"]][done_b:]))),
                (group_c, ORDERS[CFG["c"]][1:]),
                (group_d, ORDERS[CFG["d"]][1:]),
            ):
                for hop in hops:
                    _, group = next_step(group, *hop)
                groups.append(all_of(group))
        if groups is None:
            pass
        elif CFG["sc"]:
            groups.insert(0, None)
            (head_grad, down_grad, up_grad, output_grad), _ = cut(groups[1], early_a + early_b, n_gy)
        else:
            (head_grad, down_grad), _ = cut(groups[0], early_a, n_gy)
            (up_grad, output_grad), _ = cut(groups[1], early_b, n_gy)
        if groups is not None:
            (project_grad,), _ = cut(groups[2], [project_pair], n_gy)
            (patch_grad,), marks = cut(groups[3], [patch_pair], n_gy)
        small_outs = [marks[i // 4][i % 4, :size] for i, size in enumerate(sizes)]
    else:

        def total(x):
            part = lax.psum_scatter(x.astype(BF16), "gy", scatter_dimension=0, tiled=True)
            return lax.psum(part, "gx").astype(F32)

        pairs = [head_pair, down_pair, up_pair, output_pair, project_pair, patch_pair]
        head_grad, down_grad, up_grad, output_grad, project_grad, patch_grad = [total(dot_tn(a, b)) for a, b in pairs]
        tail = total(jnp.concatenate([v.reshape(n_gy, -1) for v in vectors], axis=1)).reshape(-1)
        starts = [sum(sizes[:i]) for i in range(len(sizes))]
        small_outs = [tail[s : s + z] for s, z in zip(starts, sizes)]
    return (
        predicted,
        pixel_grad,
        patch_grad,
        small_outs[0],
        small_outs[1],
        project_grad,
        small_outs[2],
        output_grad,
        small_outs[3],
        small_outs[4],
        small_outs[5],
        up_grad,
        small_outs[6],
        down_grad,
        small_outs[7],
        head_grad,
    )


def solution(mesh):
    tokens = P(("gx", "gy"))
    rows = P(("gx", "gy"), None)
    in_specs = (rows, tokens, P(None, ("gx", "gy")), tokens, tokens) + (P(),) * 14 + (rows,)
    matrix, vector = P("gy", None), P("gy")
    out_specs = (
        rows,
        rows,
        matrix,
        vector,
        vector,
        matrix,
        vector,
        matrix,
        vector,
        vector,
        vector,
        matrix,
        vector,
        matrix,
        vector,
        matrix,
    )
    return jax.shard_map(shards, mesh=mesh, in_specs=in_specs, out_specs=out_specs, check_vma=False)
```

```python
import functools

import jax
import jax.numpy as jnp
import numpy as np
from jax import lax
from jax.experimental import pallas as pl
from jax.experimental.pallas import tpu as pltpu
from jax.sharding import PartitionSpec as P

HEADS = 12
HEAD_DIM = 64
PAIR = 2 * HEAD_DIM
PAIRS = HEADS // 2
SCALE = HEAD_DIM**-0.5
LANES = 384
SHARED = 192
MARKS = 16
GRID_SIDE = 56
EPS = 1e-06
NEG = -1e30
F32 = jnp.float32
BF16 = jnp.bfloat16
VMEM_LIMIT = 56
CFG = dict(qp=(3, 3), kp=(3, 3), home=1, gate=1, b="yx", c="x", d="z", ab2=None, ab3=None, merged=False, direct=False, sc=False, limit=56, limits={}, chain="s", away_first=True, early=False, join=False)
PACE = 1.0


def dot(a, b):
    return jnp.dot(a, b, preferred_element_type=F32)


def dot_nt(a, b, precision=None):
    return lax.dot_general(a, b, (((1,), (1,)), ((), ())), preferred_element_type=F32, precision=precision)


def dot_tn(a, b):
    return lax.dot_general(a, b, (((0,), (0,)), ((), ())), preferred_element_type=F32)


def sds(shape, dtype):
    return jax.ShapeDtypeStruct(tuple(shape), dtype)


def shifted(x, axis, by):
    length = lax.axis_size(axis)
    pairs = [(i, i + by) for i in range(length) if 0 <= i + by < length]
    return lax.ppermute(x, axis, pairs)


def swap(x, axis, bit):
    length = lax.axis_size(axis)
    return lax.ppermute(x, axis, [(i, i ^ bit) for i in range(length)])


def swap_chip(x, dx, dz, dy):
    n_gx, n_gy = lax.axis_size("gx"), lax.axis_size("gy")
    flip = 2 * dx * n_gy + 2 * dz + dy
    return lax.ppermute(x, ("gx", "gy"), [(i, i ^ flip) for i in range(n_gx * n_gy)])


class ColumnGather:
    def __init__(self, unit):
        self.unit = unit
        self.direct = lax.axis_size("gy") == 8
        if not self.direct:
            self.groups = [[lax.all_gather(unit, "gy", axis=0, tiled=False)]]
            return
        self.y0 = self.across(unit)
        self.near = self.along(unit, [(0, 1), (1, 0), (2, 3), (3, 2)])
        self.mid = self.along(unit, [(1, 2), (2, 1)])

    def along(self, x, hops):
        return lax.ppermute(x, "gy", [(2 * a + y, 2 * b + y) for a, b in hops for y in (0, 1)])

    def across(self, x):
        return swap(x, "gy", 1)

    def second(self):
        self.y1 = self.across(self.near)
        self.far_end = self.along(self.mid, [(1, 0), (2, 3)])
        self.far_mid = self.along(self.near, [(1, 2), (2, 1)])

    def third(self, after):
        self.last_end = self.along(self.far_mid, [(1, 0), (2, 3)])
        self.far = choose(self.far_end, self.far_mid, after)
        self.y2 = self.across(self.far)

    def fourth(self, after):
        self.last = choose(self.last_end, self.mid, after)
        self.y3 = self.across(self.last)
        self.group()

    def group(self):
        groups = [[self.unit, self.near, self.y0], [self.y1, self.far], [self.last, self.y2, self.y3]]
        if CFG["early"]:
            groups = [[self.unit, self.near], [self.y0, self.y1, self.far], [self.last, self.y2, self.y3]]
        self.groups = [[part[None] for part in group] for group in groups]


class FreeGather(ColumnGather):
    def __init__(self, unit):
        super().__init__(unit)
        if not self.direct:
            return
        self.second()
        place = lax.axis_index("gy") // 2
        at_end = (place == 0) | (place == 3)
        self.far = jnp.where(at_end, self.far_end, self.far_mid)
        self.y2 = self.across(self.far)
        self.last_end = self.along(self.far_mid, [(1, 0), (2, 3)])
        self.last = jnp.where(at_end, self.last_end, self.mid)
        self.y3 = self.across(self.last)
        self.group()


class DirectGather:
    def __init__(self, unit):
        self.unit = unit
        if lax.axis_size("gy") != 8:
            self.groups = [[lax.all_gather(unit, "gy", axis=0, tiled=False)]]
            return
        self.near, self.y0 = swap_chip(unit, 0, 1, 0), swap_chip(unit, 0, 0, 1)
        self.mid = self.far_end = self.far_mid = self.last_end = self.near
        self.far, self.last = swap_chip(unit, 0, 2, 0), swap_chip(unit, 0, 3, 0)

        self.second()

    def second(self):
        y1, y2, y3 = (swap_chip(x, 0, 0, 1) for x in (self.near, self.far, self.last))
        self.y1, self.y2, self.y3 = y1, y2, y3
        groups = [[self.unit, self.near, self.y0], [y1, self.far], [self.last, y2, y3]]
        self.groups = [[part[None] for part in group] for group in groups]


def choose(at_end, inside, after):
    def kernel(a, b, out):
        place = lax.axis_index("gy") // 2
        out[...] = jnp.where((place == 0) | (place == 3), a[...], b[...])

    return call(kernel, plain(at_end, inside), [(sds(inside.shape, inside.dtype), VMEM)], "choose", cost=2.3, after=after)[0]


def bit_of(axis, bit):
    return (lax.axis_index(axis) // bit) % 2


def call(kernel, ins, outs, name, grid=None, scratch=(), cost=4.0, after=()):
    limit = CFG["limits"].get(name, CFG["limit"]) if lax.axis_size("gy") == 8 else VMEM_LIMIT
    specs = [spec for _, spec in ins] + [pl.BlockSpec(memory_space=pl.ANY)] * len(after)
    count = len(ins)

    def body(*refs):
        kernel(*refs[:count], *refs[count + len(after) :])

    return pl.pallas_call(
        body,
        grid=grid or (),
        in_specs=specs,
        out_specs=tuple(spec for _, spec in outs),
        out_shape=tuple(shape for shape, _ in outs),
        scratch_shapes=list(scratch),
        compiler_params=pltpu.CompilerParams(vmem_limit_bytes=limit * 2**20),
        cost_estimate=pl.CostEstimate(flops=int(cost * 1e8), bytes_accessed=int(cost * 3e5), transcendentals=0),
        name=name,
    )(*[array for array, _ in ins], *after)


VMEM = pl.BlockSpec(memory_space=pltpu.VMEM)


def plain(*arrays):
    return [(a, VMEM) for a in arrays]


def fixed(array):
    zeros = (0,) * len(array.shape)
    return (array, pl.BlockSpec(tuple(array.shape), lambda h: zeros, pipeline_mode=pl.Buffered(1)))


def lead(array, first=0):
    zeros = (0,) * (len(array.shape) - 1)
    return (array, pl.BlockSpec((1,) + tuple(array.shape[1:]), lambda h: (first + h,) + zeros))


def lanes(array, first=0, width=PAIR):
    return (array, pl.BlockSpec((array.shape[0], width), lambda h: (0, first + h)))


def half_mask(rows):
    return lax.broadcasted_iota(jnp.int32, (rows, PAIR), 1) < HEAD_DIM


def only_half(x, head):
    low_half = half_mask(x.shape[0])
    zero = jnp.zeros_like(x)
    return jnp.where(low_half, x, zero) if head == 0 else jnp.where(low_half, zero, x)


def merge_halves(first, second):
    rows = first.shape[0]
    return jnp.where(half_mask(rows), jnp.broadcast_to(first, (rows, PAIR)), jnp.broadcast_to(second, (rows, PAIR)))


def normalise(x):
    centered = x - jnp.mean(x, axis=1, keepdims=True)
    scale = lax.rsqrt(jnp.mean(centered * centered, axis=1, keepdims=True) + EPS)
    return centered * scale, scale


def norm_back(grad, unit_rows, scale, gain):
    g = grad * gain
    inner = jnp.mean(g * unit_rows, axis=1, keepdims=True)
    rows = scale * (g - jnp.mean(g, axis=1, keepdims=True) - unit_rows * inner)
    return rows, jnp.sum(grad * unit_rows, axis=0, keepdims=True), jnp.sum(grad, axis=0, keepdims=True)


def stack_heads(x):
    low_half = half_mask(x.shape[0])
    zero = jnp.zeros_like(x)
    return jnp.concatenate([jnp.where(low_half, x, zero), jnp.where(low_half, zero, x)], axis=0)


def unstack_heads(x):
    rows = x.shape[0] // 2
    return merge_halves(x[:rows], x[rows:])


def twice(x):
    return jnp.concatenate([x, x], axis=0)


def pair_lanes(ref, pair):
    return ref[:, pl.ds(pl.multiple_of(pair * PAIR, PAIR), PAIR)]


def group_blocks(block_refs):
    flat = [(ref, i) for ref in block_refs for i in range(ref.shape[0])]
    return [flat[i : i + 8] for i in range(0, len(flat), 8)]


def key_marks(ref, index, key_rows):
    marks = ref[index, key_rows : key_rows + MARKS, 0:256].astype(F32)
    return marks[0:1, 0:1], marks[0:1, 128:129]


def key_bias(group, key_rows):
    width = len(group) * key_rows
    lane = lax.broadcasted_iota(jnp.int32, (1, width), 1).astype(F32)
    bias = jnp.full((1, width), NEG, F32)
    for place, (ref, index) in enumerate(group):
        count, live = key_marks(ref, index, key_rows)
        local = lane - float(place * key_rows)
        good = (local >= 0.0) & (local < count)
        rim = (local >= float(SHARED)) & (local < float(key_rows)) & (live > 0.5)
        bias = jnp.where(good | rim, 0.0, bias)
    return bias


def key_bias_column(group, key_rows):
    parts = []
    for ref, index in group:
        count, live = key_marks(ref, index, key_rows)
        place = lax.broadcasted_iota(jnp.int32, (key_rows, 1), 0).astype(F32)
        good = (place < count) | ((place >= float(SHARED)) & (live > 0.5))
        parts.append(jnp.where(good, 0.0, NEG))
    return jnp.concatenate(parts, axis=0)


def position_table(width):
    unit_width = width // 16
    table = np.zeros((128, width), np.float32)
    bands = [(0, 8, 0, 4 * unit_width), (8, GRID_SIDE, 4 * unit_width, 6 * unit_width)]
    bands.append((64, GRID_SIDE, 10 * unit_width, 6 * unit_width))
    for row, count, lane, band in bands:
        half = band // 2
        power = np.arange(half, dtype=np.float32) / np.float32(half)
        omegas = np.float32(1.0) / np.power(np.float32(10000.0), power)
        angles = (np.arange(count, dtype=np.float32)[:, None] * omegas[None]).astype(np.float64)
        table[row : row + count, lane : lane + half] = np.sin(angles)
        table[row : row + count, lane + half : lane + band] = np.cos(angles)
    high = table.astype(jnp.bfloat16)
    low = (table - high.astype(np.float32)).astype(jnp.bfloat16)
    return jnp.asarray(high), jnp.asarray(low)


def embed_kernel(pix, weight, frame, cell, halo, high, low, gain, bias, stream_ref, rim_ref, low_ref):
    rows = pix.shape[0]
    code = lax.broadcasted_iota(jnp.int32, (128, rows), 0)
    first, second = cell[0:1, :], cell[1:2, :]
    hot = (code == frame[...]) | (code == first + 8) | (code == second + 64)
    hot = jnp.where(hot, 1.0, 0.0).astype(BF16)
    stream = dot(pix[...], weight[...]) + (dot_tn(hot, high[...]) + dot_tn(hot, low[...]))
    stream_ref[...] = stream
    place = lax.broadcasted_iota(jnp.int32, (rows, halo.shape[1]), 0)
    pick = jnp.where(place == halo[...], 1.0, 0.0).astype(BF16)
    rim_ref[...] = dot_tn(pick, stream.astype(BF16)).astype(BF16)
    unit_rows, _ = normalise(stream)
    low_ref[...] = (unit_rows * gain[...] + bias[...]).astype(BF16)


def unit_kernel(own, arrived, gain, bias, ids, live, unit_ref, joined_ref):
    rows, width = own.shape
    rim = arrived.shape[0]
    unit_rows, _ = normalise(arrived[...].astype(F32))
    rim_low = (unit_rows * gain[...] + bias[...]).astype(BF16)
    joined_ref[0:rows, :] = own[...]
    joined_ref[rows : rows + rim, :] = rim_low
    unit_ref[0:SHARED, :] = own[0:SHARED, :]
    unit_ref[SHARED : SHARED + rim, :] = rim_low
    count = jnp.sum(jnp.where(ids[...] == 0, 1.0, 0.0), axis=1, keepdims=True)
    lane = lax.broadcasted_iota(jnp.int32, (MARKS, width), 1)
    unit_ref[SHARED + rim :, :] = jnp.where(lane < 128, count, live[0:1, 0:1]).astype(BF16)


def attend_kernel(n_blocks, key_rows, first, last, *refs):
    refs = list(refs)

    def take(n):
        out = refs[:n]
        del refs[:n]
        return out

    block_refs = take(n_blocks)
    wk_ref, wv_ref, bias_ref = take(3)
    if first:
        own_ref, wq_ref, idr_ref = take(3)
    else:
        q_ref, acc_in, stat_in = take(3)
        if last:
            out_in, lse_in = take(2)
    idc_ref = take(1)[0]
    kv_ref = take(1)[0]
    if first:
        q_ref, kvown_ref = take(2)
        if not last:
            out_ref, lse_ref = take(2)
    if last:
        mixed_ref, full_lse_ref = take(2)
    else:
        acc_ref, stat_ref = take(2)
    pair = pl.program_id(0)
    own_rows = idc_ref.shape[0]
    groups = group_blocks(block_refs)
    biases = [key_bias_column(group, key_rows) for group in groups]
    here = pl.ds(pl.multiple_of(pair * PAIR, PAIR), PAIR)
    wkv = jnp.concatenate([wk_ref[...], wv_ref[...]], axis=1)
    shift = pair_lanes(bias_ref, PAIRS + pair)
    shift = jnp.concatenate([jnp.zeros_like(shift), shift], axis=1)
    base = 0
    for group in groups:
        for ref, index in group:
            kv_ref[0, base : base + key_rows, :] = (dot(ref[index, 0:key_rows, :], wkv) + shift).astype(BF16)
            base += key_rows
    if first:
        kvown_ref[0] = (dot(own_ref[...], wkv) + shift).astype(BF16)
        q = (dot(own_ref[0:own_rows, :], wq_ref[...]) + pair_lanes(bias_ref, pair)).astype(BF16) * BF16(SCALE)
        q_ref[0] = q
    else:
        q = q_ref[0]
    qs = stack_heads(q[0:SHARED])
    if first:
        peak = weight = total = None
    else:
        total = acc_in[0]
        peak, weight = stat_in[0, 0:1, :], stat_in[0, 8:9, :]
    base = 0
    for group, bias in zip(groups, biases):
        width = len(group) * key_rows
        span = slice(base, base + width)
        keys, values = kv_ref[0, span, 0:PAIR], kv_ref[0, span, PAIR:]
        base += width
        scores = dot_nt(keys, qs) + bias
        new = jnp.max(scores, axis=0, keepdims=True)
        if peak is not None:
            new = jnp.maximum(peak, new)
        probs = jnp.exp(scores - new)
        sums = jnp.sum(probs, axis=0, keepdims=True)
        part = dot_tn(values, probs.astype(BF16))
        if peak is None:
            weight, total = sums, part
        else:
            fade = jnp.exp(peak - new)
            weight = weight * fade + sums
            total = total * fade + part
        peak = new
    if first:
        idc = idc_ref[...]
        allowed = twice((idc == idr_ref[...]) & (idc != 0))
        scores = jnp.where(allowed, dot_nt(stack_heads(q), kvown_ref[0, 0:own_rows, 0:PAIR]), NEG)
        top = jnp.max(scores, axis=1, keepdims=True)
        probs = jnp.exp(scores - top)
        local_weight = jnp.sum(probs, axis=1, keepdims=True)
        local_out = unstack_heads(dot(probs.astype(BF16), kvown_ref[0, 0:own_rows, PAIR:]) / local_weight)
        local_lse = unstack_heads(top + jnp.log(local_weight))
        if not last:
            out_ref[:, here] = local_out
            lse_ref[:, here] = local_lse
    elif last:
        local_out, local_lse = out_in[:, here], lse_in[:, here]
    if last:
        shared_row = idc_ref[0:SHARED, :] == 0
        shared_out = unstack_heads((total / weight).T)
        shared_lse = unstack_heads(jnp.broadcast_to(peak + jnp.log(weight), (8, 2 * SHARED)).T[:, 0:1])
        mixed_ref[0:SHARED, here] = jnp.where(shared_row, shared_out, local_out[0:SHARED])
        mixed_ref[SHARED:, here] = local_out[SHARED:]
        full_lse_ref[0:SHARED, here] = jnp.where(shared_row, shared_lse, local_lse[0:SHARED])
        full_lse_ref[SHARED:, here] = local_lse[SHARED:]
    else:
        acc_ref[0] = total
        stat_ref[0, 0:8, :] = jnp.broadcast_to(peak, (8, 2 * SHARED))
        stat_ref[0, 8:16, :] = jnp.broadcast_to(weight, (8, 2 * SHARED))


class Attention:
    def __init__(self, first_low, weights, project_bias, idc, idr, key_rows):
        self.fixed = first_low, weights, project_bias, idc, idr
        self.key_rows = key_rows
        self.kvs = []

    def piece(self, blocks, last):
        first_low, weights, project_bias, idc, idr = self.fixed
        key_rows = self.key_rows
        own_rows, width = idc.shape[0], first_low.shape[1]
        wide = lambda rows: (sds((rows, width), F32), pl.BlockSpec((rows, width), lambda h: (0, 0)))
        deep = lambda rows, lane, dtype: (
            sds((PAIRS, rows, lane), dtype),
            pl.BlockSpec((1, rows, lane), lambda h: (h, 0, 0)),
        )
        first = not self.kvs
        keys = sum(b.shape[0] for b in blocks) * key_rows
        ins = [fixed(b) for b in blocks] + [lanes(weights, PAIRS), lanes(weights, 2 * PAIRS), fixed(project_bias)]
        if first:
            ins += [fixed(first_low), lanes(weights), fixed(idr)]
        else:
            ins += [lead(self.q)] + [lead(s) for s in self.state]
            if last:
                ins += [fixed(x) for x in self.local]
        ins += [fixed(idc)]
        outs = [deep(keys, 2 * PAIR, BF16)]
        if first:
            outs += [deep(own_rows, PAIR, BF16), deep(first_low.shape[0], 2 * PAIR, BF16)]
            if not last:
                outs += [wide(own_rows)] * 2
        outs += [wide(own_rows)] * 2 if last else [deep(PAIR, 2 * SHARED, F32), deep(16, 2 * SHARED, F32)]
        kernel = functools.partial(attend_kernel, len(blocks), key_rows, first, last)
        got = list(call(kernel, ins, outs, "attend", grid=(PAIRS,), cost=3.0 + keys / 90.0))
        self.kvs.append(got.pop(0))
        if first:
            self.q, self.kvown = got.pop(0), got.pop(0)
            if not last:
                self.local = [got.pop(0), got.pop(0)]
        self.state = got
        return (got[0],)


def erf(x):
    x = jnp.clip(x, -3.832506856900711, 3.832506856900711)
    s = x * x
    top = -2.72614225801306e-10
    for c in (2.77068142495902e-08, -2.10102402082508e-06, -5.69250639462346e-05, -7.34990630326855e-04, -2.95459980854025e-03, -1.60960333262415e-02):
        top = top * s + c
    low = -1.45660718464996e-05
    for c in (-2.13374055278905e-04, -1.68282697438203e-03, -7.37332916720468e-03, -1.42647390514189e-02):
        low = low * s + c
    return x * top / low


def middle_kernel(
    mixed, lse, stream, mlp_grad, act_grad, idc,
    w_output, merge_bias, gain, bias, w_up, up_bias, w_down, down_bias, w_head,
    predicted, act_ref, pre_ref, second_ref, mixed_low_ref, attn_low_ref, final_ref, attn_ref, grad_ref, unit_ref,
    stat_ref, up_sum, gain_sum, bias_sum, merge_sum,
):
    rows, width = mixed.shape
    hidden = w_up.shape[1]
    mixed_low = mixed[...].astype(BF16)
    mixed_low_ref[...] = mixed_low
    after = stream[...] + dot(mixed_low, w_output[...]) + merge_bias[...]
    unit_rows, scale = normalise(after)
    second = (unit_rows * gain[...] + bias[...]).astype(BF16)
    second_ref[...] = second
    out = after + down_bias[...]
    back = jnp.zeros((rows, width), F32)
    step = 768
    for start in range(0, hidden, step):
        part = slice(start, start + step)
        pre = dot(second, w_up[:, part]) + up_bias[:, part]
        cdf = 0.5 + 0.5 * erf(pre * 0.7071067811865476)
        act = (pre * cdf).astype(BF16)
        act_ref[:, part] = act
        slope = cdf + pre * (0.3989422804014327 * jnp.exp(-0.5 * pre * pre))
        grad = (act_grad[:, part] * slope).astype(BF16)
        pre_ref[:, part] = grad
        up_sum[:, part] = jnp.sum(grad.astype(F32), axis=0, keepdims=True)
        out += dot(act, w_down[part, :])
        back += dot_nt(grad, w_up[:, part])
    resid, gain_part, bias_part = norm_back(back, unit_rows, scale, gain[...])
    gain_sum[...] = gain_part
    bias_sum[...] = bias_part
    attn = mlp_grad[...] + resid
    attn_ref[...] = attn
    merge_sum[...] = jnp.sum(attn, axis=0, keepdims=True)
    attn_low = attn.astype(BF16)
    attn_low_ref[...] = attn_low
    grad = dot_nt(attn_low, w_output[...]).astype(BF16)
    grad_ref[...] = grad
    shared_row = idc[0:SHARED, :] == 0
    unit_ref[0:SHARED, :] = jnp.where(shared_row, grad[0:SHARED], jnp.zeros((SHARED, width), BF16))
    lane = lax.broadcasted_iota(jnp.int32, (MARKS, width), 1)
    head = lax.broadcasted_iota(jnp.int32, (MARKS, width), 0)
    ones = jnp.where(lane // HEAD_DIM == head, 1.0, 0.0)
    pick = jnp.where(lane == head * HEAD_DIM, 1.0, 0.0)

    def by_head(chooser, value):
        chooser, high = chooser.astype(BF16), value.astype(BF16)
        return dot_nt(chooser, high) + dot_nt(chooser, (value - high.astype(F32)).astype(BF16))

    delta = by_head(ones, grad.astype(F32) * mixed[...])
    turned = by_head(pick, lse[...])
    stat_ref[0] = turned
    stat_ref[1] = delta
    zeros = jnp.zeros((rows, 128), F32)
    ids = jnp.where(idc[...] == 0, 1.0, 0.0) + zeros
    row_ids = dot_nt(jnp.full((MARKS, 128), 1.0 / 128, F32), ids)
    shared_lane = row_ids[:, 0:SHARED] > 0.5
    sent = []
    for value, other in ((turned, -NEG), (delta, 0.0)):
        value = jnp.where(shared_lane, value[:, 0:SHARED], other)
        high = value.astype(BF16)
        sent += [high, (value - high.astype(F32)).astype(BF16)]
    unit_ref[SHARED:, :] = jnp.concatenate(sent, axis=1)
    final = out.astype(BF16)
    final_ref[...] = final
    predicted[...] = dot(final, w_head[...]).astype(BF16)


def query_kernel(n_blocks, n_kvs, key_rows, first, *refs):
    block_refs, kv_refs = refs[:n_blocks], refs[n_blocks : n_blocks + n_kvs]
    kvown_ref, q_ref, wq_ref, grad_ref, mixed_ref, lse_ref, bias_ref, idc_ref, idr_ref = refs[
        n_blocks + n_kvs : n_blocks + n_kvs + 9
    ]
    dq_ref, qall_ref = refs[-2:]
    pair = first + pl.program_id(0)
    own_rows = idc_ref.shape[0]
    flat = [(ref, i) for ref in block_refs for i in range(ref.shape[0])]
    base = 0
    wq, shift = wq_ref[...], pair_lanes(bias_ref, pair)
    for ref, index in flat:
        rows = (dot(ref[index, 0:SHARED, :], wq) + shift).astype(BF16)
        qall_ref[0, base : base + SHARED, :] = rows * BF16(SCALE)
        base += SHARED
    idc = idc_ref[...]
    allowed = twice((idc == idr_ref[...]) & (idc != 0))
    shared_row = idc == 0
    q = q_ref[0]
    grad = pair_lanes(grad_ref, pair)
    product = stack_heads(grad.astype(F32) * pair_lanes(mixed_ref, pair))
    delta = jnp.sum(product, axis=1, keepdims=True)
    lse = pair_lanes(lse_ref, pair)
    lse = jnp.concatenate([lse[:, 0:1], lse[:, HEAD_DIM : HEAD_DIM + 1]], axis=0)
    qm, gm = stack_heads(q), stack_heads(grad)
    part_rows = lambda x: jnp.concatenate([x[0:SHARED], x[own_rows : own_rows + SHARED]], axis=0)
    qs, gs, delta_s, lse_s = part_rows(qm), part_rows(gm), part_rows(delta), part_rows(lse)
    total, used = None, 0
    for kv_ref in kv_refs:
        count = kv_ref.shape[1] // key_rows
        for start in range(0, count, 8):
            size = min(8, count - start)
            bias = key_bias(flat[used : used + size], key_rows)
            used += size
            span = slice(start * key_rows, (start + size) * key_rows)
            keys = kv_ref[0, span, 0:PAIR]
            values = kv_ref[0, span, PAIR:]
            probs = jnp.exp(dot_nt(qs, keys) + bias - lse_s)
            ds = (probs * (dot_nt(gs, values) - delta_s)).astype(BF16)
            part = dot(ds, keys)
            total = part if total is None else total + part
    keys, values = kvown_ref[0, 0:own_rows, 0:PAIR], kvown_ref[0, 0:own_rows, PAIR:]
    probs = jnp.exp(jnp.where(allowed, dot_nt(qm, keys) - lse, NEG))
    ds = (probs * (dot_nt(gm, values) - delta)).astype(BF16)
    local = unstack_heads(dot(ds, keys)) * SCALE
    shared = jnp.where(shared_row[0:SHARED], unstack_heads(total) * SCALE, local[0:SHARED])
    here = pl.ds(pl.multiple_of(pl.program_id(0) * PAIR, PAIR), PAIR)
    dq_ref[0:SHARED, here] = shared.astype(BF16)
    dq_ref[SHARED:, here] = local[SHARED:].astype(BF16)


def query_back(groups, kvs, kvown, q, mixed_grad, mixed, lse, wq, project_bias, idc, idr, key_rows, first, pairs, after):
    own_rows = idc.shape[0]
    blocks = [b for group in groups for b in group]
    count = sum(b.shape[0] for b in blocks)
    ins = [fixed(b) for b in blocks] + [lead(kv, first) for kv in kvs] + [lead(x, first) for x in (kvown, q)] + [lanes(wq, first)]
    ins += [fixed(x) for x in (mixed_grad, mixed, lse, project_bias, idc, idr)]
    outs = [
        (sds((own_rows, pairs * PAIR), BF16), pl.BlockSpec((own_rows, pairs * PAIR), lambda h: (0, 0))),
        (sds((pairs, count * SHARED, PAIR), BF16), pl.BlockSpec((1, count * SHARED, PAIR), lambda h: (h, 0, 0))),
    ]
    kernel = functools.partial(query_kernel, len(blocks), len(kvs), key_rows, first)
    return call(kernel, ins, outs, "query_back", grid=(pairs,), cost=4.2 * pairs, after=after)


def key_kernel(n_blocks, first, *refs):
    grad_refs = refs[:n_blocks]
    kvown_ref, qall_ref, q_ref, grad_ref, own_stat_ref, idc_ref, idr_ref, live_ref = refs[n_blocks : n_blocks + 8]
    dk_ref, dv_ref, grads_ref, stats_ref = refs[n_blocks + 8 :]
    pair = first + pl.program_id(0)
    own_rows = idc_ref.shape[0]
    rim = kvown_ref.shape[1] - own_rows
    flat = [(ref, i) for ref in grad_refs for i in range(ref.shape[0])]

    @pl.when(pl.program_id(0) == 0)
    def _():
        base = 0
        for begin in range(0, len(flat), 2):
            sums = []
            for ref, i in flat[begin : begin + 2]:
                stat = ref[i, SHARED:, :].astype(F32)
                sums.append(
                    (
                        stat[:, 0:SHARED] + stat[:, SHARED : 2 * SHARED],
                        stat[:, 2 * SHARED : 3 * SHARED] + stat[:, 3 * SHARED :],
                    )
                )
            for kind in range(2):
                stats_ref[kind, :, base : base + 2 * SHARED] = jnp.concatenate([s[kind] for s in sums], axis=1)
            base += 2 * SHARED

    base = 0
    there = pl.ds(pl.multiple_of(pair * PAIR, PAIR), PAIR)
    for ref, i in flat:
        grads_ref[base : base + SHARED, :] = ref[i, 0:SHARED, there]
        base += SHARED
    idc = idc_ref[...]
    allowed = twice((idc == idr_ref[...]) & (idc != 0))
    shared_row = idc == 0
    live = live_ref[0:1, 0:1] > 0.5
    kv = kvown_ref[0]
    k_all, v_all = kv[:, 0:PAIR], kv[:, PAIR:]
    in_shared = lambda x: jnp.concatenate([x[0:SHARED], x[own_rows:]], axis=0)
    q, grad = q_ref[0], pair_lanes(grad_ref, pair)
    n_shared = SHARED + rim
    k_sh, v_sh = stack_heads(in_shared(k_all)), stack_heads(in_shared(v_all))

    def both_rows(ref, kind, rows, columns):
        picked = [ref[kind, pl.ds(2 * pair + head, 1), columns] for head in range(2)]
        return jnp.concatenate([jnp.broadcast_to(p, (rows, p.shape[1])) for p in picked], axis=0)

    dk = dv = None
    chunk = min(base, 1536)
    for start in range(0, base, chunk):
        span = slice(start, start + chunk)
        q_all, g_all = qall_ref[0, span, :], grads_ref[span, :]
        probs = jnp.exp(dot_nt(k_sh, q_all) - both_rows(stats_ref, 0, n_shared, span))
        part_v = dot(probs.astype(BF16), g_all)
        ds = (probs * (dot_nt(v_sh, g_all) - both_rows(stats_ref, 1, n_shared, span))).astype(BF16)
        part_k = dot(ds, q_all)
        dk = part_k if dk is None else dk + part_k
        dv = part_v if dv is None else dv + part_v
    every = slice(None)
    scores = dot_nt(stack_heads(k_all[0:own_rows]), q) - both_rows(own_stat_ref, 0, own_rows, every)
    probs = jnp.exp(jnp.where(allowed, scores, NEG))
    local_v = dot(probs.astype(BF16), grad)
    ds = dot_nt(stack_heads(v_all[0:own_rows]), grad) - both_rows(own_stat_ref, 1, own_rows, every)
    local_k = dot((probs * ds).astype(BF16), q)
    here = pl.ds(pl.multiple_of(pl.program_id(0) * PAIR, PAIR), PAIR)
    for out, shared, local in ((dk_ref, dk, local_k), (dv_ref, dv, local_v)):
        shared, local = unstack_heads(shared), unstack_heads(local)
        out[0:SHARED, here] = jnp.where(shared_row[0:SHARED], shared[0:SHARED], local[0:SHARED]).astype(BF16)
        out[SHARED:own_rows, here] = local[SHARED:].astype(BF16)
        out[own_rows:, here] = jnp.where(live, shared[SHARED:], 0.0).astype(BF16)


def key_back(groups, kvown, qall, q, mixed_grad, own_stats, idc, idr, live, first, pairs, after):
    joined_rows = kvown.shape[1]
    grads = [g for group in groups for g in group]
    ins = [fixed(g) for g in grads] + [lead(kvown, first), lead(qall), lead(q, first)]
    ins += [fixed(x) for x in (mixed_grad, own_stats, idc, idr, live)]
    out = (sds((joined_rows, pairs * PAIR), BF16), pl.BlockSpec((joined_rows, pairs * PAIR), lambda h: (0, 0)))
    scratch = [pltpu.VMEM((qall.shape[1], PAIR), BF16), pltpu.VMEM((2, MARKS, qall.shape[1]), F32)]
    kernel = functools.partial(key_kernel, len(grads), first)
    return call(kernel, ins, [out, out], "key_back", grid=(pairs,), scratch=scratch, cost=3.7 * pairs, after=after)


def input_kernel(dq, dk, dv, weight, stream, arrived, gain, attn_grad, rim_ref, rows_ref, joint_ref, vec_ref):
    own, width = dq.shape
    dq, dk, dv = dq[...], dk[...], dv[...]
    wq, wk, wv = weight[:, 0:width], weight[:, width : 2 * width], weight[:, 2 * width :]
    rim_grad = dot_nt(dk[own:], wk) + dot_nt(dv[own:], wv)
    rim_rows, rim_scale = normalise(arrived[...].astype(F32))
    rim_back, rim_gain, rim_bias = norm_back(rim_grad, rim_rows, rim_scale, gain[...])
    rim_ref[...] = rim_back.astype(BF16)
    own_grad = dot_nt(dq, wq) + dot_nt(dk[:own], wk) + dot_nt(dv[:own], wv)
    own_rows, own_scale = normalise(stream[...])
    own_back, own_gain, own_bias = norm_back(own_grad, own_rows, own_scale, gain[...])
    rows_ref[...] = own_back + attn_grad[...]
    joint_ref[0:own, 0:width] = dq
    joint_ref[own:, 0:width] = jnp.zeros((dk.shape[0] - own, width), BF16)
    joint_ref[:, width : 2 * width] = dk
    joint_ref[:, 2 * width :] = dv
    vec_ref[0:1, :] = own_gain + rim_gain
    vec_ref[1:2, :] = own_bias + rim_bias
    vec_ref[2:3, :] = jnp.sum(dq.astype(F32), axis=0, keepdims=True)
    vec_ref[3:4, :] = jnp.sum(dv.astype(F32), axis=0, keepdims=True)


def pixel_kernel(rows, returned, halo, weight, low_ref, grad_ref):
    place = lax.broadcasted_iota(jnp.int32, (rows.shape[0], halo.shape[1]), 0)
    spread = jnp.where(place == halo[...], 1.0, 0.0).astype(BF16)
    low = (rows[...] + dot(spread, returned[...])).astype(BF16)
    low_ref[...] = low
    grad_ref[...] = dot_nt(low, weight[...]).astype(BF16)


ORDERS = {
    "x": [("gx", 2, None), ("gy", 1, 2), ("gy", 2, 1), ("gy", 4, 0)],
    "y": [("gy", 1, None), ("gy", 2, 1), ("gy", 4, 0)],
    "z": [("gy", 2, None), ("gy", 4, 0), ("gy", 1, 0)],
    "s": [("gy", 1, None)],
    "yx": [("gy", 1, None), ("gx", 2, 2), ("gy", 2, 1), ("gy", 4, 0)],
}


def product_blocks(left, right, core_half, n):
    half = right.shape[1] // 2
    x = left[...]
    for j in range(half // LANES):
        columns = pl.ds(pl.multiple_of(core_half * half + j * LANES, 128), LANES)
        out = dot_tn(x, right[:, columns])
        yield out.reshape(n, out.shape[0] // n, LANES)


def away_kernel(n, n_pairs, *refs):
    pairs, outs = refs[: 2 * n_pairs], refs[2 * n_pairs :]
    other = 1 - lax.axis_index("gx") % 2
    (out,) = outs
    row = 0
    for p in range(n_pairs):
        for block in product_blocks(pairs[2 * p], pairs[2 * p + 1], other, n):
            out[:, row : row + block.shape[1], :] = block.astype(BF16)
            row += block.shape[1]


def home_kernel(n, n_pairs, order, n_small, row, *refs):
    pairs = refs[: 2 * n_pairs]
    arrived = refs[2 * n_pairs]
    small = refs[2 * n_pairs + 1 : 2 * n_pairs + 1 + n_small]
    send, keep = refs[2 * n_pairs + 1 + n_small :][-2:] if order != "s" else (None, refs[-1])
    core = lax.axis_index("gx") % 2
    axis, bit = ORDERS[order][0][:2]
    low = lax.axis_index(axis) // bit % 2 == 0
    half_row = 0

    def put(first, second, start, rows):
        if order == "s":
            for half, value in ((0, first), (1, second)):
                keep[:, half, start : start + rows, :] = value
            return
        if order == "x":
            span = slice(start, start + rows)
            send[:, span, :] = jnp.where(low, second, first)
            keep[:, span, :] = jnp.where(low, first, second)
            return
        for half, value in ((0, first), (1, second)):
            span = slice(start, start + rows)
            value = value.reshape(n // 2 // bit, 2, bit, rows, LANES)
            for out, one, other in ((send, value[:, 1], value[:, 0]), (keep, value[:, 0], value[:, 1])):
                out[:, half, span, :] = jnp.where(low, one, other).reshape(n // 2, rows, LANES)

    for p in range(n_pairs):
        for block in product_blocks(pairs[2 * p], pairs[2 * p + 1], core, n):
            r = block.shape[1]
            block = (block + arrived[:, row : row + r, :].astype(F32)).astype(BF16)
            put(block[:, : r // 2], block[:, r // 2 :], half_row, r // 2)
            row += r
            half_row += r // 2
    if n_small:
        value = small[0][...] + small[1][...]
        put(value, jnp.zeros(value.shape, BF16), half_row, value.shape[1])


def away(pairs, n, name, after=()):
    arrays = [x for pair in pairs for x in pair]
    rows = sum(b.shape[1] // 2 // LANES * a.shape[1] // n for a, b in pairs)
    outs = [(sds((n, rows, LANES), BF16), VMEM)]
    return call(functools.partial(away_kernel, n, len(pairs)), plain(*arrays), outs, name, cost=rows / 135.0, after=after)[0]


def home(pairs, n, arrived, order, name, small=(), first_row=0, after=()):
    arrays = [x for pair in pairs for x in pair] + [arrived] + list(small)
    rows = sum(b.shape[1] // 2 // LANES * a.shape[1] // n // 2 for a, b in pairs)
    rows += small[0].shape[1] if small else 0
    shape = (n, rows, LANES) if order == "x" else (n // 2, 2, rows, LANES)
    kernel = functools.partial(home_kernel, n, len(pairs), order, len(small), first_row)
    if order == "s":
        outs = [(sds((n, 2, rows, LANES), BF16), VMEM)]
        whole = call(kernel, plain(*arrays), outs, name, after=after)[0]
        return whole, lax.psum_scatter(whole, "gy", scatter_dimension=0, tiled=False)
    outs = [(sds(shape, BF16), VMEM)] * 2
    send, keep = call(kernel, plain(*arrays), outs, name, after=after)
    got = swap(send, *ORDERS[order][0][:2])
    shape = ((2, 2, 2) if order == "x" else (2, 2)) + keep.shape[1:]
    return send, (keep.reshape(shape), got.reshape(shape))


def next_step(group, axis, bit, dim):
    keep, got = group
    mine = bit_of(axis, bit)
    pick = lambda x, i: lax.dynamic_index_in_dim(x, i, dim, keepdims=False)
    send = pick(keep, 1 - mine) + pick(got, 1 - mine)
    return send, (pick(keep, mine) + pick(got, mine), swap(send, axis, bit))


def held_step(group, axis, bit, dim, after):
    keep, got = group
    shape = keep.shape[:dim] + keep.shape[dim + 1 :]

    def kernel(keep, got, send, left):
        mine = lax.axis_index(axis) // bit % 2
        for out, side in ((send, 1 - mine), (left, mine)):
            index = (slice(None),) * dim + (side,)
            out[...] = keep[index] + got[index]

    send, left = call(kernel, plain(keep, got), [(sds(shape, BF16), VMEM)] * 2, "step", after=after)
    return send, (left, swap(send, axis, bit))


def all_of(group):
    part = group[0] + group[1] if isinstance(group, tuple) else group
    x_low, core_low = bit_of("gx", 2) == 0, bit_of("gx", 1) == 0
    over = swap(part, "gx", 2)
    if part.ndim == 3:
        both = part + over
    else:
        both = jnp.stack([jnp.where(x_low, part, over), jnp.where(x_low, over, part)])
    across = swap(both, "gx", 1)
    return [jnp.where(core_low, both, across), jnp.where(core_low, across, both)]


def cut(sides, pairs, n):
    outs, start = [], 0
    for a, b in pairs:
        r, blocks = a.shape[1] // n, b.shape[1] // 2 // LANES
        halves = []
        for side in sides:
            piece = side[:, start : start + blocks * r // 2].reshape(2, blocks, r // 2, LANES)
            halves.append(piece.transpose(0, 2, 1, 3).reshape(r, blocks * LANES))
        start += blocks * r // 2
        outs.append(jnp.concatenate(halves, axis=1).astype(F32))
    return outs, [side[0, start:].astype(F32) for side in sides]


def shards(
    pixels,
    frame_index,
    patch_cell,
    tile_id,
    halo_index,
    w_patch,
    first_gain,
    first_bias,
    w_project,
    project_bias,
    w_output,
    merge_bias,
    second_gain,
    second_bias,
    w_up,
    up_bias,
    w_down,
    down_bias,
    w_head,
    cotangent,
):
    n_gx, n_gy = lax.axis_size("gx"), lax.axis_size("gy")
    own, rim = pixels.shape[0], halo_index.shape[0]
    width, hidden, depth = w_output.shape[0], w_up.shape[1], pixels.shape[1]
    key_rows = SHARED + rim
    idc, idr = tile_id.reshape(own, 1), tile_id.reshape(1, own)
    live = jnp.broadcast_to(jnp.where(lax.axis_index("gx") > 0, 1.0, 0.0).astype(F32), (8, 128))
    halo = halo_index.reshape(1, rim)
    row = lambda v: v.reshape(1, -1)
    mat = lambda rows, columns, dtype: (sds((rows, columns), dtype), VMEM)

    high, low = position_table(width)
    stream, outgoing, own_low = call(
        embed_kernel,
        plain(
            pixels, w_patch, row(frame_index), patch_cell, halo, high, low, row(first_gain), row(first_bias)
        ),
        [mat(own, width, F32), mat(rim, width, BF16), mat(own, width, BF16)],
        "embed",
    )
    arrived = shifted(outgoing, "gx", 1)
    unit, first_low = call(
        unit_kernel,
        plain(own_low, arrived, row(first_gain), row(first_bias), idr, live),
        [mat(key_rows + MARKS, width, BF16), mat(own + rim, width, BF16)],
        "unit",
        cost=2.4,
    )
    column = ColumnGather(unit)
    shift = row(project_bias)
    attention = Attention(first_low, w_project, shift, idc, idr, key_rows)
    if column.direct:
        column.second()
        if CFG["early"]:
            after = attention.piece([unit[None], column.near[None]], False)
            column.third(after)
            column.fourth((column.far,))
            attention.piece(column.groups[1], False)
            attention.piece(column.groups[2], True)
        else:
            after = attention.piece([unit[None], column.near[None], column.y0[None]], False)
            column.third(after)
            after = attention.piece([column.y1[None], column.far[None]], False)
            column.fourth(after)
            attention.piece([column.last[None], column.y2[None], column.y3[None]], True)
    else:
        attention.piece(column.groups[0], True)
    groups, kvs, kvown, q = column.groups, attention.kvs, attention.kvown, attention.q
    mixed, lse = attention.state

    mlp_grad = dot_nt(cotangent, w_head)
    down_bias_grad = jnp.sum(mlp_grad, axis=0)
    mlp_low = mlp_grad.astype(BF16)
    act_grad = dot_nt(mlp_low, w_down)
    (
        predicted, act_low, pre_grad, second_low, mixed_low, attn_low, final_low, attn_grad, mixed_grad, grad_unit,
        own_stats, up_sum, second_gain_sum, second_bias_sum, merge_sum,
    ) = call(
        middle_kernel,
        plain(
            mixed, lse, stream, mlp_grad, act_grad, idc, w_output, row(merge_bias), row(second_gain),
            row(second_bias), w_up, row(up_bias), w_down, row(down_bias), w_head,
        ),
        [mat(own, depth, BF16), mat(own, hidden, BF16), mat(own, hidden, BF16)]
        + [mat(own, width, BF16)] * 4
        + [mat(own, width, F32), mat(own, width, BF16), mat(SHARED + MARKS, width, BF16)]
        + [(sds((2, MARKS, own), F32), VMEM), mat(1, hidden, F32)]
        + [mat(1, width, F32)] * 3,
        "middle",
        cost=18.0,
    )
    special = n_gx == 4 and n_gy == 8
    head_pair, down_pair = (final_low, cotangent), (act_low, mlp_low)
    up_pair, output_pair = (second_low, pre_grad), (mixed_low, attn_low)
    gather = (DirectGather if CFG["direct"] else FreeGather)(grad_unit)
    early_a, early_b = [head_pair, down_pair], [up_pair, output_pair]
    q_parts, k_parts = [], []

    def query_piece(first, pairs, after):
        part = query_back(
            groups, kvs, kvown, q, mixed_grad, mixed, lse, w_project, shift, idc, idr, key_rows, first, pairs, after
        )
        q_parts.append(part)
        return (part[0],)

    def key_piece(place, first, pairs, after):
        qall = jnp.concatenate([p[1] for p in q_parts], axis=0) if CFG["qp"] != CFG["kp"] else q_parts[place][1]
        part = key_back(gather.groups, kvown, qall, q, mixed_grad, own_stats, idc, idr, live, first, pairs, after)
        k_parts.append(part)
        return (part[0],)

    after = ()
    if special:
        if CFG["merged"]:
            share_a = share_b = away(early_a + early_b, n_gy, "away")
            gone_a = gone_b = swap(share_a, "gx", 1)
        else:
            share_a, share_b = away(early_a, n_gy, "away"), away(early_b, n_gy, "away")
            gone_a, gone_b = swap(share_a, "gx", 1), swap(share_b, "gx", 1)
        after = (share_a, share_b) if CFG["away_first"] else ()

    def homes(after):
        gate = CFG["gate"]
        if gate >= 1:
            after += (gather.near, gather.mid, gather.y0)
        if gate >= 3:
            after += (gather.far_end, gather.far_mid, gather.y1)
        if CFG["sc"]:
            send, group = home(early_a + early_b, n_gy, gone_a, "s", "home", after=after)
            return (send,), group, None
        send_a, group_a = home(early_a, n_gy, gone_a, "x", "home", after=after)
        after += (send_a,)
        if gate >= 2:
            after += (gather.far_end, gather.far_mid, gather.y1)
        if gate >= 3:
            after += (gather.last_end, gather.y2)
        first_row = 2 * group_a[0].shape[-2] if CFG["merged"] else 0
        send_b, group_b = home(early_b, n_gy, gone_b, CFG["b"], "home", first_row=first_row, after=after)
        return (send_a, send_b), group_a, group_b

    def second_steps(group_a, group_b, after):
        send_a, group_a = held_step(group_a, *ORDERS["x"][1], after)
        send_b, group_b = held_step(group_b, *ORDERS[CFG["b"]][1], after + (send_a,))
        return (send_a, send_b), group_a, group_b

    done_a = done_b = 1
    first = 0
    for i, size in enumerate(CFG["qp"]):
        after = query_piece(first, size, after)
        first += size
        if special and CFG["home"] == i:
            more, group_a, group_b = homes(after)
            after += more
    first = 0
    for i, size in enumerate(CFG["kp"]):
        part = key_piece(i, first, size, after)
        after = part
        first += size
        if special and CFG["ab2"] == i:
            more, group_a, group_b = second_steps(group_a, group_b, after)
            after += more
            done_a = done_b = 2
    dq = jnp.concatenate([p[0] for p in q_parts], axis=1)
    dk = jnp.concatenate([p[0] for p in k_parts], axis=1)
    dv = jnp.concatenate([p[1] for p in k_parts], axis=1)
    rim_grad, partial, joint_grad, first_sums = call(
        input_kernel,
        plain(dq, dk, dv, w_project, stream, arrived, row(first_gain), attn_grad),
        [mat(rim, width, BF16), mat(own, width, F32), mat(own + rim, 3 * width, BF16), mat(8, width, F32)],
        "input",
        cost=6.0,
        after=after,
    )
    returned = shifted(rim_grad, "gx", -1)
    project_pair = (first_low, joint_grad)
    after = ()
    if special:
        share_c = away([project_pair], n_gy, "away")
        gone_c = swap(share_c, "gx", 1)
        after = ()
        if CFG["ab2"] == "c":
            after, group_a, group_b = second_steps(group_a, group_b, (share_c,))
            done_a = done_b = 2
    embed_low, pixel_grad = call(
        pixel_kernel,
        plain(partial, returned, halo, w_patch),
        [mat(own, width, BF16), mat(own, depth, BF16)],
        "pixel",
        cost=3.0,
        after=after if special else (),
    )
    patch_pair = (pixels, embed_low)

    vectors = [
        first_sums[0],
        first_sums[1],
        first_sums[2:4].reshape(-1),
        merge_sum[0],
        second_gain_sum[0],
        second_bias_sum[0],
        up_sum[0],
        down_bias_grad,
    ]
    sizes = [v.shape[0] // n_gy for v in vectors]
    if special:
        core = bit_of("gx", 1)
        small = jnp.stack([jnp.pad(v.reshape(n_gy, z), ((0, 0), (0, LANES - z))) for v, z in zip(vectors, sizes)], axis=1)
        small = jnp.pad(small.astype(BF16).reshape(n_gy, 2, 4, LANES), ((0, 0), (0, 0), (0, MARKS - 4), (0, 0)))
        small_mine = lax.dynamic_index_in_dim(small, core, 1, keepdims=False)
        small_gone = swap(lax.dynamic_index_in_dim(small, 1 - core, 1, keepdims=False), "gx", 1)
        share_d = away([patch_pair], n_gy, "away")
        gone_d = swap(share_d, "gx", 1)
        send_c, group_c = home([project_pair], n_gy, gone_c, CFG["c"], "home", after=(share_d,) if CFG["chain"] in (True, "s") else ())
        send_d, group_d = home(
            [patch_pair], n_gy, gone_d, CFG["d"], "home", small=[small_mine, small_gone], after=(send_c,) if CFG["chain"] in (True, "d") else ()
        )
        if CFG["ab3"] and done_a == 2:
            send_a, group_a = held_step(group_a, *ORDERS["x"][2], (send_d,))
            send_b, group_b = held_step(group_b, *ORDERS[CFG["b"]][2], (send_d,))
            done_a = done_b = 3
        if CFG["join"]:

            def joined(groups, orders):
                groups = [next_step(group, *ORDERS[order][1])[1] for group, order in zip(groups, orders)]
                for axis, bit, dim in ORDERS["x"][2:]:
                    mine = bit_of(axis, bit)
                    pick = lambda x, i: lax.dynamic_index_in_dim(x, i, dim, keepdims=False)
                    put = lambda i: jnp.concatenate([pick(k, i) + pick(g, i) for k, g in groups], axis=-2)
                    groups = [(put(mine), swap(put(1 - mine), axis, bit))]
                return all_of(groups[0])

            sides = joined([group_a, group_b], ["x", CFG["b"]])
            (head_grad, down_grad, up_grad, output_grad), _ = cut(sides, early_a + early_b, n_gy)
            sides = joined([group_c, group_d], [CFG["c"], CFG["d"]])
            (project_grad, patch_grad), marks = cut(sides, [project_pair, patch_pair], n_gy)
            groups = None
        else:
            groups = []
            for group, hops in (
                *(((group_a, ()),) if CFG["sc"] else ((group_a, ORDERS["x"][done_a:]), (group_b, ORDERS[CFG["b"]][done_b:]))),
                (group_c, ORDERS[CFG["c"]][1:]),
                (group_d, ORDERS[CFG["d"]][1:]),
            ):
                for hop in hops:
                    _, group = next_step(group, *hop)
                groups.append(all_of(group))
        if groups is None:
            pass
        elif CFG["sc"]:
            groups.insert(0, None)
            (head_grad, down_grad, up_grad, output_grad), _ = cut(groups[1], early_a + early_b, n_gy)
        else:
            (head_grad, down_grad), _ = cut(groups[0], early_a, n_gy)
            (up_grad, output_grad), _ = cut(groups[1], early_b, n_gy)
        if groups is not None:
            (project_grad,), _ = cut(groups[2], [project_pair], n_gy)
            (patch_grad,), marks = cut(groups[3], [patch_pair], n_gy)
        small_outs = [marks[i // 4][i % 4, :size] for i, size in enumerate(sizes)]
    else:

        def total(x):
            part = lax.psum_scatter(x.astype(BF16), "gy", scatter_dimension=0, tiled=True)
            return lax.psum(part, "gx").astype(F32)

        pairs = [head_pair, down_pair, up_pair, output_pair, project_pair, patch_pair]
        head_grad, down_grad, up_grad, output_grad, project_grad, patch_grad = [total(dot_tn(a, b)) for a, b in pairs]
        tail = total(jnp.concatenate([v.reshape(n_gy, -1) for v in vectors], axis=1)).reshape(-1)
        starts = [sum(sizes[:i]) for i in range(len(sizes))]
        small_outs = [tail[s : s + z] for s, z in zip(starts, sizes)]
    return (
        predicted,
        pixel_grad,
        patch_grad,
        small_outs[0],
        small_outs[1],
        project_grad,
        small_outs[2],
        output_grad,
        small_outs[3],
        small_outs[4],
        small_outs[5],
        up_grad,
        small_outs[6],
        down_grad,
        small_outs[7],
        head_grad,
    )


def solution(mesh):
    tokens = P(("gx", "gy"))
    rows = P(("gx", "gy"), None)
    in_specs = (rows, tokens, P(None, ("gx", "gy")), tokens, tokens) + (P(),) * 14 + (rows,)
    matrix, vector = P("gy", None), P("gy")
    out_specs = (
        rows,
        rows,
        matrix,
        vector,
        vector,
        matrix,
        vector,
        matrix,
        vector,
        vector,
        vector,
        matrix,
        vector,
        matrix,
        vector,
        matrix,
    )
    return jax.shard_map(shards, mesh=mesh, in_specs=in_specs, out_specs=out_specs, check_vma=False)
```
